32 devices in a mesh: row: 8 (over z, core), col: 4 (over y, x).
Axes of the slice: x: 2, y: 2, z: 4, core: 2. Of those that a mesh axis runs over, the one named last changes fastest.
Arguments:
- features: bfloat16 [4096, 768], P(('col', 'row')), may hold values from -6 to 6
- w_neigh: bfloat16 [768, 1024], replicated, may hold values from -0.875 to 0.875
- w_self: bfloat16 [768, 1024], replicated, may hold values from -0.21875 to 0.21875
- bias: float32 [1024], replicated, may hold values from -3 to 3
- cotangent: bfloat16 [4096, 1024], P(('row', 'col')), may hold values from -6 to 6
- block_rows: int32 [8, 4, 24], P('row', 'col'), may hold values from 0 to 3
- block_cols: int32 [8, 4, 24], P('row', 'col'), may hold values from 0 to 7
- block_vals: bfloat16 [8, 4, 24, 128, 128], P('row', 'col'), may hold values from 0 to 1, as said below
- block_count: int32 [8, 4], P('row', 'col'), may hold values from 6 to 24, as said below
Outputs:
- output: bfloat16 [4096, 1024], P(('row', 'col'))
- grad_input: bfloat16 [4096, 768], P(('col', 'row'))
- grad_self: float32 [768, 1024], replicated
- grad_neigh: float32 [768, 1024], replicated
- grad_bias: float32 [1024], replicated
The draws below stay inside these ranges and needn't reach their ends.
Inputs may be any that keep to these rules, and one draw needn't show every extreme that they name: `block_vals`: block values are non-negative edge weights. `block_count`: some tile in every draw has all 24 slots live.
All inputs are finite; a program needn't handle non-finite values.
Results may differ from the reference program's by a relative error of at most 0.0053.
Values may be sent and summed in bfloat16 or wider, within the bound.
No kernel may reach another device: no remote copies, remote signals or barrier semaphores. Data moves between devices by JAX's collectives and lax.ppermute only.
A program may use at most 128 MiB of HBM per device.

```python
import math
import jax
import jax.numpy as jnp
from jax import lax

D = 768
HID = 1024
NODE_DEV = 128
BLK = 128
NODES = 4096
TB_R = 4
TB_C = 8
NBLK = 24
N_ROW = 8
N_COL = 4


def draw_block_vals(key, part):
    key = jax.random.fold_in(key, 7)
    first_key, second_key = jax.random.split(key)
    shape = (N_ROW, N_COL, NBLK, BLK, BLK)
    keep_mask = jax.random.randint(first_key, shape, 0, 8) == 0
    magnitude = jnp.exp(jax.random.uniform(second_key, shape, jnp.float32, math.log(0.25), 0.0))
    return jnp.where(keep_mask, magnitude, 0.0).astype(jnp.bfloat16)


def draw_block_count(key, part):
    key = jax.random.fold_in(key, 11)
    first_key, second_key = jax.random.split(key)
    counts = jax.random.randint(first_key, (N_ROW * N_COL,), NBLK // 4, NBLK + 1)
    busiest = jax.random.randint(second_key, (), 0, N_ROW * N_COL)
    flattened = jnp.where(jnp.arange(N_ROW * N_COL) == busiest, NBLK, counts)
    return flattened.reshape(N_ROW, N_COL).astype(jnp.int32)


def with_ends(entries, key, low, top_value):
    dims = entries.shape
    place = [jax.random.randint(jax.random.fold_in(key, axis), (), 0, dims[axis]) for axis in range(len(dims))]
    entries = entries.at[tuple(place)].set(low)
    longest = dims.index(max(dims))
    place[longest] = (place[longest] + 1) % dims[longest]
    return entries.at[tuple(place)].set(top_value)


def levels(own_key, shape, cuts, smallest, high):
    level = 1.0
    for dim, blocks in cuts:
        steps = jax.random.uniform(jax.random.fold_in(jax.random.fold_in(own_key, 6), dim), (blocks,), jnp.float32, smallest / len(cuts), high / len(cuts))
        level = level * jnp.repeat(jnp.exp(steps), shape[dim] // blocks).reshape((-1,) + (1,) * (len(shape) - 1 - dim))
    return level


def noise(stream_key, dims, scale, reach, cuts=(), held_as=jnp.bfloat16):
    loudness = levels(stream_key, dims, cuts, -0.22, 0.18) if cuts else 1.0
    array = jax.random.normal(stream_key, dims, jnp.float32) * scale * loudness
    return jnp.minimum(jnp.maximum(array, -reach), reach).astype(held_as)


def setup_inputs(seed: int = 0) -> dict:
    splits = jax.random.split(jax.random.key(seed), 10)
    features = noise(splits[0], (NODES, D), 1.0, 6.0, ((0, 32),))
    w_neigh = noise(splits[1], (D, HID), (D // 16) ** -0.5, 0.875)
    w_self = noise(splits[2], (D, HID), D ** -0.5, 0.21875)
    bias = noise(splits[3], (HID,), 0.5, 3.0, (), jnp.float32)
    cotangent = noise(splits[4], (NODES, HID), 1.0, 6.0, ((0, 32),))
    block_rows = with_ends(jax.random.randint(splits[5], (N_ROW, N_COL, NBLK), 0, TB_R), jax.random.fold_in(splits[5], 1), 0, TB_R - 1).astype(jnp.int32)
    block_cols = with_ends(jax.random.randint(splits[6], (N_ROW, N_COL, NBLK), 0, TB_C), jax.random.fold_in(splits[6], 1), 0, TB_C - 1).astype(jnp.int32)
    block_vals = draw_block_vals(jax.random.fold_in(splits[9], 71), 0)
    block_count = draw_block_count(jax.random.fold_in(splits[9], 71), 0)
    return dict(features=features, w_neigh=w_neigh, w_self=w_self, bias=bias, cotangent=cotangent, block_rows=block_rows, block_cols=block_cols, block_vals=block_vals, block_count=block_count)


def block_term(block_vals, take_ids, put_ids, live_count, source, seg_count, flipped, start_slot, group_size):
    chosen = lax.dynamic_slice_in_dim(block_vals, start_slot, group_size, 0)
    taken = lax.dynamic_slice_in_dim(take_ids, start_slot, group_size, 0)
    placed = lax.dynamic_slice_in_dim(put_ids, start_slot, group_size, 0)
    slot_ids = start_slot + jnp.arange(group_size, dtype=jnp.int32)
    live_mask = (slot_ids < live_count).astype(jnp.float32)
    weights = chosen.astype(jnp.float32) * live_mask[:, None, None]
    gathered = source[taken].astype(jnp.float32)
    pattern = 'gji,gjw->giw' if flipped else 'gij,gjw->giw'
    products = jnp.einsum(pattern, weights, gathered)
    return jax.ops.segment_sum(products, placed, num_segments=seg_count)

def sparse_product(block_vals, take_ids, put_ids, live_count, source, seg_count, flipped):
    slot_total = block_vals.shape[0]
    group_size = min(8, slot_total)
    width = source.shape[2]

    def advance(turn, accum):
        start_slot = (turn * group_size).astype(jnp.int32)
        return accum + block_term(block_vals, take_ids, put_ids, live_count, source, seg_count, flipped, start_slot, group_size)
    initial = jnp.zeros((seg_count, source.shape[1], width), jnp.float32)
    return lax.fori_loop(0, slot_total // group_size, advance, initial)

def reference(features, w_neigh, w_self, bias, cotangent, block_rows, block_cols, block_vals, block_count):
    rows_tile = NODE_DEV * N_COL
    cols_tile = NODE_DEV * N_ROW
    both_w = jnp.concatenate([w_neigh, w_self], axis=1)
    projected = jnp.dot(features, both_w, preferred_element_type=jnp.float32).astype(jnp.bfloat16)
    neigh = projected[:, :HID]
    own = projected[:, HID:]

    def forward_row(row_index):
        accum = jnp.zeros((TB_R, BLK, HID), jnp.float32)
        masses = jnp.zeros((TB_R, BLK), jnp.float32)
        for col_index in range(N_COL):
            values = block_vals[row_index, col_index]
            row_ids = block_rows[row_index, col_index]
            col_ids = block_cols[row_index, col_index]
            live_count = block_count[row_index, col_index]
            source = neigh[col_index * cols_tile:(col_index + 1) * cols_tile].reshape(TB_C, BLK, HID)
            accum = accum + sparse_product(values, col_ids, row_ids, live_count, source, TB_R, False)
            live_mask = (jnp.arange(NBLK, dtype=jnp.int32) < live_count).astype(jnp.float32)
            row_mass = lax.optimization_barrier(jnp.sum(values.astype(jnp.float32), axis=2)) * live_mask[:, None]
            masses = masses + jax.ops.segment_sum(row_mass, row_ids, num_segments=TB_R)
        return (accum.reshape(rows_tile, HID), masses.reshape(rows_tile))
    aggregate, degree = lax.map(forward_row, jnp.arange(N_ROW, dtype=jnp.int32))
    aggregate = aggregate.reshape(NODES, HID)
    degree = degree.reshape(NODES)
    inverse = 1.0 / (degree + 1.0)
    preact = own.astype(jnp.float32) + aggregate * inverse[:, None] + bias
    output = jax.nn.elu(preact).astype(jnp.bfloat16)
    slopes = jnp.where(preact > 0, 1.0, jnp.exp(jnp.minimum(preact, 0.0)))
    grad_pre = cotangent.astype(jnp.float32) * slopes
    grad_round = grad_pre.astype(jnp.bfloat16)
    scaled = (grad_pre * inverse[:, None]).astype(jnp.bfloat16)

    def backward_col(col_index):
        accum = jnp.zeros((TB_C, BLK, HID), jnp.float32)
        for row_index in range(N_ROW):
            values = block_vals[row_index, col_index]
            row_ids = block_rows[row_index, col_index]
            col_ids = block_cols[row_index, col_index]
            live_count = block_count[row_index, col_index]
            source = scaled[row_index * rows_tile:(row_index + 1) * rows_tile].reshape(TB_R, BLK, HID)
            accum = accum + sparse_product(values, row_ids, col_ids, live_count, source, TB_C, True)
        return accum.reshape(cols_tile, HID)
    back = lax.map(backward_col, jnp.arange(N_COL, dtype=jnp.int32)).reshape(NODES, HID).astype(jnp.bfloat16)
    factor = 1.0 / math.sqrt(NODES)
    grad_self = jnp.dot(features.T, grad_round, preferred_element_type=jnp.float32) * factor
    grad_neigh = jnp.dot(features.T, back, preferred_element_type=jnp.float32) * (32.0 * factor)
    grad_bias = lax.optimization_barrier(jnp.sum(grad_pre, axis=0)) * factor
    grad_input = jnp.dot(grad_round, w_self.T, preferred_element_type=jnp.float32) + jnp.dot(back, w_neigh.T, preferred_element_type=jnp.float32)
    return (output, grad_input.astype(jnp.bfloat16), grad_self, grad_neigh, grad_bias)
```

```python
import math

import jax
import jax.numpy as jnp
from jax import lax
from jax.experimental import pallas as pl
from jax.experimental.pallas import tpu as pltpu
from jax.sharding import PartitionSpec as P

F32 = jnp.float32
BF16 = jnp.bfloat16
LANES = 128
EXTRA = 16
VMEM = pl.BlockSpec(memory_space=pltpu.VMEM)
SMEM = pl.BlockSpec(memory_space=pltpu.SMEM)
PARAMS = pltpu.CompilerParams(vmem_limit_bytes=48 * 1024 * 1024)


def call(body, outs, args, scratch=(), smem=0, flops=0):
    moved = sum(math.prod(o.shape) * o.dtype.itemsize for o in outs)
    moved += sum(a.size * a.dtype.itemsize for a in args)
    return pl.pallas_call(
        body,
        out_shape=outs,
        in_specs=[SMEM] * smem + [VMEM] * (len(args) - smem),
        out_specs=[VMEM] * len(outs),
        scratch_shapes=list(scratch),
        compiler_params=PARAMS,
        cost_estimate=pl.CostEstimate(flops=flops, bytes_accessed=moved, transcendentals=0),
    )(*args)


def shape(dims, dtype):
    return jax.ShapeDtypeStruct(tuple(dims), dtype)


def mm(a, b, ca=1, cb=0):
    return lax.dot_general(a, b, (((ca,), (cb,)), ((), ())), preferred_element_type=F32)


def densify(rows, cols, count, values, nd, rs, cs):
    rt, ct, half = nd * cs, nd * rs, rs // 2

    def body(rows_ref, cols_ref, count_ref, values_ref, tile_ref, mass_ref, acc):
        i, j = lax.axis_index("row"), lax.axis_index("col")
        z, c = i // 2, lax.rem(i, 2)
        acc[...] = jnp.zeros_like(acc)

        def add(s, carry):
            row, col = rows_ref[s], cols_ref[s]
            row = lax.rem(row + cs - j, cs)
            turn = lax.rem(z + half - col // 2, half)
            col = jnp.where(lax.rem(col, 2) == c, turn, turn + half)
            r = pl.multiple_of(row * nd, nd)
            c0 = pl.multiple_of(col * nd, nd)
            acc[pl.ds(r, nd), pl.ds(c0, nd)] += values_ref[s].astype(F32)
            return carry

        lax.fori_loop(0, count_ref[0], add, 0)
        tile_ref[...] = acc[...].astype(BF16)
        ones = jnp.ones((8, ct), BF16)
        for k in range(cs):
            place = pl.multiple_of(lax.rem(j + k, cs) * nd, nd)
            mass_ref[:, pl.ds(place, nd)] = mm(ones, tile_ref[k * nd : (k + 1) * nd, :], 1, 1)

    return call(
        body,
        [shape((rt, ct), BF16), shape((8, rt), F32)],
        [rows, cols, count, values],
        [pltpu.VMEM((rt, ct), F32)],
        smem=3,
        flops=2 * 8 * rt * ct,
    )


def forward_parts(tile, blocks, nd, cs):
    width = blocks[0].shape[1]

    def body(*refs):
        tile_ref, feat_refs = refs[0], refs[1 : 1 + len(blocks)]
        outs = refs[1 + len(blocks) :]
        feats = jnp.concatenate([r[...] for r in feat_refs], axis=0)
        for k in range(cs):
            part = mm(tile_ref[k * nd : (k + 1) * nd, :], feats)
            outs[k][...] = part.astype(outs[k].dtype)

    return call(
        body,
        [shape((nd, width), BF16 if k else F32) for k in range(cs)],
        [tile, *blocks],
        flops=2 * tile.size * width,
    )


def activation(own, mean, w_neigh, bias, cotangent):
    nd, hid = own.shape

    def body(own_ref, mean_ref, w_ref, bias_ref, cot_ref, out_ref, grad_ref, sum_ref):
        pre = own_ref[...].astype(F32) + mm(mean_ref[...], w_ref[...]) + bias_ref[...]
        slope = jnp.where(pre > 0, 1.0, jnp.exp(jnp.minimum(pre, 0.0)))
        out_ref[...] = jnp.where(pre > 0, pre, slope - 1.0).astype(BF16)
        grad = cot_ref[...].astype(F32) * slope
        grad_ref[...] = grad.astype(BF16)
        sum_ref[...] = jnp.broadcast_to(jnp.sum(grad, axis=0, keepdims=True), (8, hid))

    return call(
        body,
        [shape((nd, hid), BF16), shape((nd, hid), BF16), shape((8, hid), F32)],
        [own, mean, w_neigh, bias, cotangent],
        flops=2 * mean.size * hid,
    )


def split_pair(total):
    high = total.astype(BF16).astype(F32)
    return jnp.concatenate([high, total - high], axis=0)


def weight_parts(xs, gs, sums, rs, xr, nc):
    cs = len(xs)
    nd, xw = xs[0].shape
    hid = gs[0].shape[1]
    half = rs // 2

    def body(*refs):
        x_refs, g_refs = refs[:cs], refs[cs : 2 * cs]
        sum_ref, keep_ref, send_ref, acc = refs[2 * cs :]
        x_all = jnp.concatenate([r[...] for r in x_refs], axis=0)
        g_all = jnp.concatenate([r[...] for r in g_refs], axis=0)
        acc[...] = mm(x_all, g_all, 0, 0)
        i = lax.axis_index("row")
        z, c = i // 2, lax.rem(i, 2)
        for k in range(half):
            for core, ref in ((c, keep_ref), (1 - c, send_ref)):
                q = 2 * lax.rem(z + k, half) + core
                row = pl.multiple_of((q // nc) * xr, xr)
                col = pl.multiple_of(lax.rem(q, nc) * LANES, LANES)
                ref[k, :xr, :] = acc[pl.ds(row, xr), pl.ds(col, LANES)].astype(ref.dtype)
                ref[k, xr:, :] = split_pair(sum_ref[:, pl.ds(col, LANES)]).astype(ref.dtype)

    dims = (half, xr + EXTRA, LANES)
    return call(
        body,
        [shape(dims, F32), shape(dims, BF16)],
        [*xs, *gs, sums],
        [pltpu.VMEM((xw, hid), F32)],
        flops=2 * cs * nd * xw * hid,
    )


def back_parts(tile, gs, inverse, w_neigh, nd, rs):
    cs = len(gs)
    rt = tile.shape[0]
    depth, hid = w_neigh.shape
    half = rs // 2

    def body(*refs):
        tile_ref, w_ref, inv_ref = refs[:3]
        g_refs = refs[3 : 3 + cs]
        keep_ref, send_ref, scaled = refs[3 + cs :]
        j = lax.axis_index("col")
        for k in range(cs):
            start = pl.multiple_of(lax.rem(j + cs - k, cs) * nd, nd)
            inv = inv_ref[pl.ds(start, nd), :]
            inv = jnp.concatenate([inv] * (depth // LANES), axis=1)
            product = mm(g_refs[k][...], w_ref[...], 1, 1) * inv
            place = (cs - k) % cs * nd
            scaled[place : place + nd, :] = product.astype(BF16)
        for ref, base in ((send_ref, half), (keep_ref, 0)):
            for k in range(half):
                place = (base + (half - k) % half) * nd
                cut = tile_ref[:, place : place + nd]
                ref[k] = mm(cut, scaled[...], 0, 0).astype(ref.dtype)

    dims = (half, nd, depth)
    return call(
        body,
        [shape(dims, F32), shape(dims, BF16)],
        [tile, w_neigh, inverse, *gs],
        [pltpu.VMEM((rt, depth), BF16)],
        flops=2 * rt * depth * (hid + nd * rs),
    )


def pair_sum(keep, came, paired):
    half, rows, width = keep.shape
    main = rows - EXTRA if paired else rows

    def body(keep_ref, came_ref, *outs):
        for k in range(half):
            total = keep_ref[k] + came_ref[k].astype(F32)
            dtype = outs[k].dtype
            outs[k][:main, :] = total[:main].astype(dtype)
            if paired:
                merged = total[main : main + 8] + total[main + 8 :]
                outs[k][main:, :] = split_pair(merged).astype(dtype)

    return call(
        body,
        [shape((rows, width), BF16 if k else F32) for k in range(half)],
        [keep, came],
    )


def last_sum(parts, paired, dtype=BF16):
    rows, width = parts[0].shape
    main = rows - EXTRA if paired else rows

    def body(*refs):
        out_ref = refs[-1]
        total = refs[0][...].astype(F32)
        for ref in refs[1:-1]:
            total = total + ref[...].astype(F32)
        out_ref[:main, :] = total[:main].astype(dtype)
        if paired:
            merged = total[main : main + 8] + total[main + 8 :]
            out_ref[main:, :] = split_pair(merged).astype(dtype)

    return call(body, [shape((rows, width), dtype)], parts)[0]


def assemble(mine, theirs, depth, hid, xr, nc, factors):
    cs, half = len(mine), mine[0].shape[0]
    xw = 2 * depth // cs
    side = cs // 2

    def body(*refs):
        groups = (refs[:cs], refs[cs : 2 * cs])
        self_ref, neigh_ref, bias_ref = refs[2 * cs :]
        i, j = lax.axis_index("row"), lax.axis_index("col")
        z, c = i // 2, lax.rem(i, 2)
        for group, core in zip(groups, (c, 1 - c)):
            for t in range(half):
                q = 2 * lax.rem(z + half - t, half) + core
                col = pl.multiple_of(lax.rem(q, nc) * LANES, LANES)
                turn = q // nc
                for k in range(cs):
                    owner = lax.rem(j + cs - k, cs)
                    row = pl.multiple_of(lax.rem(owner, side) * xw + turn * xr, xr)
                    chunk = group[k][t, :xr, :].astype(F32)

                    @pl.when(owner < side)
                    def _():
                        self_ref[pl.ds(row, xr), pl.ds(col, LANES)] = chunk * factors[0]

                    @pl.when(owner >= side)
                    def _():
                        neigh_ref[pl.ds(row, xr), pl.ds(col, LANES)] = chunk * factors[1]

                @pl.when(turn == 0)
                def _():
                    total = sum(group[k][t, xr:, :].astype(F32) for k in range(cs))
                    bias_ref[:, pl.ds(col, LANES)] = (total[:8] + total[8:]) * factors[0]

    weight = shape((depth, hid), F32)
    return call(body, [weight, weight, shape((8, hid), F32)], [*mine, *theirs])


def local(
    features, w_neigh, w_self, bias, cotangent, block_rows, block_cols, block_vals, block_count
):
    rs = lax.axis_size("row")
    cs = lax.axis_size("col")
    j = lax.axis_index("col")
    nd, depth = features.shape
    hid = w_self.shape[1]
    rt = nd * cs
    half = rs // 2
    xw = 2 * depth // cs
    nc = min(rs, hid // LANES)
    nr = rs // nc
    xr = xw // nr

    def along_col(x, k):
        return lax.ppermute(x, "col", [(s, (s + k) % cs) for s in range(cs)])

    def along_chips(x, k):
        return lax.ppermute(
            x, "row", [(s, 2 * ((s // 2 + k) % half) + s % 2) for s in range(rs)]
        )

    def other_core(x):
        return lax.ppermute(x, "row", [(s, s ^ 1) for s in range(rs)])

    swap = [((b % rs) * cs + b // rs, b) for b in range(rs * cs)]
    blocks = [features] + [along_chips(features, k) for k in range(1, half)]
    blocks = blocks + [other_core(x) for x in blocks]
    own_feat = lax.ppermute(features, ("row", "col"), swap)
    tile, mass = densify(
        block_rows.reshape(-1),
        block_cols.reshape(-1),
        block_count.reshape(-1),
        block_vals[0, 0],
        nd,
        rs,
        cs,
    )
    degree = mass
    for k in range(1, cs):
        degree = degree + along_col(mass, k)
    inverse = 1.0 / (degree[0] + 1.0)
    inverse = jnp.broadcast_to(inverse[:, None], (rt, LANES))
    own = jnp.dot(own_feat, w_self, preferred_element_type=F32).astype(BF16)

    parts = forward_parts(tile, blocks, nd, cs)
    aggregate = parts[0]
    for k in range(1, cs):
        aggregate = aggregate + along_col(parts[k], k).astype(F32)
    own_inverse = lax.dynamic_slice_in_dim(inverse, j * nd, nd, 0)
    mean = (aggregate * own_inverse[:, :1]).astype(BF16)
    output, grad, sums = activation(own, mean, w_neigh, bias[None, :], cotangent)
    both = jnp.concatenate([own_feat, mean], axis=1)

    def cut(k):
        return lax.dynamic_slice_in_dim(both, lax.rem(j + k, cs) * xw, xw, 1)

    xs = [cut(0)] + [along_col(cut(k), k) for k in range(1, cs)]
    gs = [grad] + [along_col(grad, k) for k in range(1, cs)]

    keep, send = weight_parts(xs, gs, sums, rs, xr, nc)
    chunks = pair_sum(keep, other_core(send), True)
    chunk = last_sum([chunks[0]] + [along_chips(chunks[k], k) for k in range(1, half)], True)
    line = jnp.stack([chunk] + [along_chips(chunk, k) for k in range(1, half)])
    mine = [line] + [along_col(line, k) for k in range(1, cs)]
    theirs = [other_core(x) for x in mine]

    keep, send = back_parts(tile, gs, inverse, w_neigh, nd, rs)
    blocks = pair_sum(keep, other_core(send), False)
    self_part = jnp.einsum("nh,dh->nd", grad, w_self, preferred_element_type=F32).astype(BF16)
    self_part = lax.ppermute(self_part, ("row", "col"), [(b, a) for a, b in swap])
    grad_input = last_sum(
        [blocks[0], self_part] + [along_chips(blocks[k], k) for k in range(1, half)], False
    )

    factor = 1.0 / math.sqrt(nd * rs * cs)
    total_self, total_neigh, total_bias = assemble(
        mine, theirs, depth, hid, xr, nc, (factor, 32.0 * factor)
    )
    return output, grad_input, total_self, total_neigh, total_bias[0]


def solution(mesh):
    in_specs = (
        P(("col", "row"), None),
        P(),
        P(),
        P(),
        P(("row", "col"), None),
        P("row", "col", None),
        P("row", "col", None),
        P("row", "col", None, None, None),
        P("row", "col"),
    )
    out_specs = (P(("row", "col"), None), P(("col", "row"), None), P(), P(), P())
    return jax.shard_map(local, mesh=mesh, in_specs=in_specs, out_specs=out_specs, check_vma=False)
```

```python
import math

import jax
import jax.numpy as jnp
from jax import lax
from jax.experimental import pallas as pl
from jax.experimental.pallas import tpu as pltpu
from jax.sharding import PartitionSpec as P

F32 = jnp.float32
BF16 = jnp.bfloat16
LANES = 128
EXTRA = 16
VMEM = pl.BlockSpec(memory_space=pltpu.VMEM)
SMEM = pl.BlockSpec(memory_space=pltpu.SMEM)
PARAMS = pltpu.CompilerParams(vmem_limit_bytes=48 * 1024 * 1024)


def call(body, outs, args, scratch=(), smem=0, flops=0, after=()):
    count = len(args)
    moved = sum(math.prod(o.shape) * o.dtype.itemsize for o in outs)
    moved += sum(a.size * a.dtype.itemsize for a in args)

    def run(*refs):
        body(*refs[:count], *refs[count + len(after) :])

    return pl.pallas_call(
        run,
        out_shape=outs,
        in_specs=[SMEM] * smem
        + [VMEM] * (count - smem)
        + [pl.BlockSpec(memory_space=pl.ANY)] * len(after),
        out_specs=[VMEM] * len(outs),
        scratch_shapes=list(scratch),
        compiler_params=PARAMS,
        cost_estimate=pl.CostEstimate(flops=flops, bytes_accessed=moved, transcendentals=0),
    )(*args, *after)


def follow(x, after):
    def body(x_ref, out_ref):
        out_ref[...] = x_ref[...]

    return call(body, [shape(x.shape, x.dtype)], [x], after=after)[0]


def shape(dims, dtype):
    return jax.ShapeDtypeStruct(tuple(dims), dtype)


def mm(a, b, ca=1, cb=0):
    return lax.dot_general(a, b, (((ca,), (cb,)), ((), ())), preferred_element_type=F32)


def stack(parts, after):
    def body(*refs):
        for k, ref in enumerate(refs[:-1]):
            refs[-1][k] = ref[...]

    out = shape((len(parts), *parts[0].shape), parts[0].dtype)
    return call(body, [out], parts, after=after)[0]


def densify(rows, cols, count, values, nd, rs, cs):
    rt, ct, half = nd * cs, nd * rs, rs // 2

    def body(rows_ref, cols_ref, count_ref, values_ref, tile_ref, turned_ref, mass_ref, acc):
        i, j = lax.axis_index("row"), lax.axis_index("col")
        z, c = i // 2, lax.rem(i, 2)
        acc[...] = jnp.zeros_like(acc)

        def add(s, carry):
            row, col = rows_ref[s], cols_ref[s]
            row = lax.rem(row + cs - j, cs)
            turn = lax.rem(z + half - col // 2, half)
            col = jnp.where(lax.rem(col, 2) == c, turn, turn + half)
            r = pl.multiple_of(row * nd, nd)
            c0 = pl.multiple_of(col * nd, nd)
            acc[pl.ds(r, nd), pl.ds(c0, nd)] += values_ref[s].astype(F32)
            return carry

        lax.fori_loop(0, count_ref[0], add, 0)
        tile_ref[...] = acc[...].astype(BF16)
        for k in range(rs):
            cut = acc[:, k * nd : (k + 1) * nd]
            turned_ref[k * nd : (k + 1) * nd, :] = cut.T.astype(BF16)
        ones = jnp.ones((8, ct), BF16)
        for k in range(cs):
            place = pl.multiple_of(lax.rem(j + k, cs) * nd, nd)
            mass_ref[:, pl.ds(place, nd)] = mm(ones, tile_ref[k * nd : (k + 1) * nd, :], 1, 1)

    return call(
        body,
        [shape((rt, ct), BF16), shape((ct, rt), BF16), shape((8, rt), F32)],
        [rows, cols, count, values],
        [pltpu.VMEM((rt, ct), F32)],
        smem=3,
        flops=2 * 8 * rt * ct,
    )


def forward_parts(tile, blocks, nd, cs):
    width = blocks[0].shape[1]

    def body(*refs):
        tile_ref, feat_refs = refs[0], refs[1 : 1 + len(blocks)]
        outs = refs[1 + len(blocks) :]
        feats = jnp.concatenate([r[...] for r in feat_refs], axis=0)
        parts = mm(tile_ref[...], feats)
        for k in range(cs):
            outs[k][...] = parts[k * nd : (k + 1) * nd].astype(outs[k].dtype)

    return call(
        body,
        [shape((nd, width), BF16 if k else F32) for k in range(cs)],
        [tile, *blocks],
        flops=2 * tile.size * width,
    )


def activation(parts, inverse, own, own_feat, w_neigh, bias, cotangent):
    cs = len(parts)
    nd, hid = own.shape
    depth = own_feat.shape[1]
    xw = 2 * depth // cs

    def body(*refs):
        part_refs = refs[:cs]
        inv_ref, own_ref, feat_ref, w_ref, bias_ref, cot_ref = refs[cs : cs + 6]
        out_ref, sum_ref, *packs = refs[cs + 6 : -1]
        both = refs[-1]
        j = lax.axis_index("col")
        inv = inv_ref[pl.ds(pl.multiple_of(j * nd, nd), nd), :]
        total = sum(r[...].astype(F32) for r in part_refs)
        mean = (total * jnp.concatenate([inv] * (depth // LANES), axis=1)).astype(BF16)
        both[:, :depth] = feat_ref[...]
        both[:, depth:] = mean
        pre = own_ref[...].astype(F32) + mm(mean, w_ref[...]) + bias_ref[...]
        slope = jnp.where(pre > 0, 1.0, jnp.exp(jnp.minimum(pre, 0.0)))
        out_ref[...] = jnp.where(pre > 0, pre, slope - 1.0).astype(BF16)
        grad = cot_ref[...].astype(F32) * slope
        sum_ref[...] = jnp.broadcast_to(jnp.sum(grad, axis=0, keepdims=True), (8, hid))
        grad = grad.astype(BF16)
        for k in range(cs):
            packs[k][:, :hid] = grad
            target = lax.rem(j + k, cs)
            if xw % LANES == 0:
                start = pl.multiple_of(target * xw, LANES)
                packs[k][:, hid:] = both[:, pl.ds(start, xw)]
            else:
                for d in range(cs):

                    @pl.when(target == d)
                    def _():
                        packs[k][:, hid:] = both[:, d * xw : (d + 1) * xw]

    return call(
        body,
        [shape((nd, hid), BF16), shape((8, hid), F32)] + [shape((nd, hid + xw), BF16)] * cs,
        [*parts, inverse, own, own_feat, w_neigh, bias, cotangent],
        [pltpu.VMEM((nd, 2 * depth), BF16)],
        flops=2 * own_feat.size * hid,
    )


def split_pair(total):
    high = total.astype(BF16).astype(F32)
    return jnp.concatenate([high, total - high], axis=0)


def weight_parts(packs, sums, rs, xr, nc):
    cs = len(packs)
    hid = sums.shape[1]
    nd, xw = packs[0].shape[0], packs[0].shape[1] - hid
    half = rs // 2

    def body(*refs):
        pack_refs = refs[:cs]
        sum_ref, keep_ref, send_ref, acc = refs[cs:]
        x_all = jnp.concatenate([r[:, hid:] for r in pack_refs], axis=0)
        g_all = jnp.concatenate([r[:, :hid] for r in pack_refs], axis=0)
        acc[...] = mm(x_all, g_all, 0, 0)
        i = lax.axis_index("row")
        z, c = i // 2, lax.rem(i, 2)
        for k in range(half):
            for core, ref in ((c, keep_ref), (1 - c, send_ref)):
                q = 2 * lax.rem(z + k, half) + core
                row = pl.multiple_of((q // nc) * xr, xr)
                col = pl.multiple_of(lax.rem(q, nc) * LANES, LANES)
                ref[k, :xr, :] = acc[pl.ds(row, xr), pl.ds(col, LANES)].astype(ref.dtype)
                ref[k, xr:, :] = split_pair(sum_ref[:, pl.ds(col, LANES)]).astype(ref.dtype)

    dims = (half, xr + EXTRA, LANES)
    return call(
        body,
        [shape(dims, F32), shape(dims, BF16)],
        [*packs, sums],
        [pltpu.VMEM((xw, hid), F32)],
        flops=2 * cs * nd * xw * hid,
    )


def scaled_parts(packs, inverse, w_neigh, w_self, after):
    cs = len(packs)
    nd = packs[0].shape[0]
    depth, hid = w_neigh.shape

    def body(*refs):
        w_ref, ws_ref, inv_ref = refs[:3]
        pack_refs = refs[3 : 3 + cs]
        scaled_ref, self_ref = refs[3 + cs :]
        i, j = lax.axis_index("row"), lax.axis_index("col")
        grads = jnp.concatenate([pack_refs[(cs - r) % cs][:, :hid] for r in range(cs)], axis=0)
        product = mm(grads, w_ref[...], 1, 1)
        for r in range(cs):
            start = pl.multiple_of(lax.rem(j + r, cs) * nd, nd)
            inv = inv_ref[pl.ds(start, nd), :]
            inv = jnp.concatenate([inv] * (depth // LANES), axis=1)
            rows = slice(r * nd, (r + 1) * nd)
            scaled_ref[rows, :] = (product[rows] * inv).astype(BF16)

        @pl.when(i * cs // lax.axis_size("row") == j)
        def _():
            self_ref[...] = mm(grads, ws_ref[...], 1, 1)

        @pl.when(i * cs // lax.axis_size("row") != j)
        def _():
            self_ref[...] = jnp.zeros_like(self_ref)

    dims = (cs * nd, depth)
    return call(
        body,
        [shape(dims, BF16), shape(dims, F32)],
        [w_neigh, w_self, inverse, *packs],
        flops=2 * cs * nd * hid * depth,
        after=after,
    )


def back_parts(turned, scaled, self_part, nd, cs, rs, after):
    depth = scaled.shape[1]
    half = rs // 2

    def body(tile_ref, scaled_ref, self_ref, keep_ref, send_ref, acc):
        i, j = lax.axis_index("row"), lax.axis_index("col")
        z, c = i // 2, lax.rem(i, 2)
        acc[...] = mm(tile_ref[...], scaled_ref[...])

        @pl.when(i * cs // rs == j)
        def _():
            for r in range(cs):
                q = i * cs - j * rs + lax.rem(j + r, cs)
                turn = lax.rem(z + half - q // 2, half)
                place = jnp.where(lax.rem(q, 2) == c, turn, turn + half) * nd
                acc[pl.ds(pl.multiple_of(place, nd), nd), :] += self_ref[r * nd : (r + 1) * nd]

        for ref, base in ((send_ref, half), (keep_ref, 0)):
            for k in range(half):
                place = (base + (half - k) % half) * nd
                ref[k] = acc[place : place + nd, :].astype(ref.dtype)

    dims = (half, nd, depth)
    return call(
        body,
        [shape(dims, F32), shape(dims, BF16)],
        [turned, scaled, self_part],
        [pltpu.VMEM((rs * nd, depth), F32)],
        flops=2 * turned.size * depth,
        after=after,
    )


def pair_sum(keep, came, paired, after=()):
    half, rows, width = keep.shape
    main = rows - EXTRA if paired else rows

    def body(keep_ref, came_ref, *outs):
        for k in range(half):
            total = keep_ref[k] + came_ref[k].astype(F32)
            dtype = outs[k].dtype
            outs[k][:main, :] = total[:main].astype(dtype)
            if paired:
                merged = total[main : main + 8] + total[main + 8 :]
                outs[k][main:, :] = split_pair(merged).astype(dtype)

    return call(
        body,
        [shape((rows, width), BF16 if k else F32) for k in range(half)],
        [keep, came],
        after=after,
    )


def last_sum(parts, paired, dtype=BF16):
    rows, width = parts[0].shape
    main = rows - EXTRA if paired else rows

    def body(*refs):
        out_ref = refs[-1]
        total = refs[0][...].astype(F32)
        for ref in refs[1:-1]:
            total = total + ref[...].astype(F32)
        out_ref[:main, :] = total[:main].astype(dtype)
        if paired:
            merged = total[main : main + 8] + total[main + 8 :]
            out_ref[main:, :] = split_pair(merged).astype(dtype)

    return call(body, [shape((rows, width), dtype)], parts)[0]


def assemble(pieces, depth, hid, xr, nc, half, cs, factors, after):
    xw = 2 * depth // cs
    side = cs // 2

    def body(*refs):
        piece_refs = refs[: len(pieces)]
        self_ref, neigh_ref, bias_ref = refs[len(pieces) :]
        i, j = lax.axis_index("row"), lax.axis_index("col")
        z, c = i // 2, lax.rem(i, 2)
        bias_ref[...] = jnp.zeros_like(bias_ref)
        for ref, (array, first, owner_of, mine) in zip(piece_refs, pieces):
            owner = owner_of(j)
            for t in range(array.shape[0]):
                q = 2 * lax.rem(z + half - first - t, half) + (c if mine else 1 - c)
                col = pl.multiple_of(lax.rem(q, nc) * LANES, LANES)
                turn = q // nc
                row = pl.multiple_of(lax.rem(owner, side) * xw + turn * xr, xr)
                chunk = ref[t, :xr, :].astype(F32)

                @pl.when(owner < side)
                def _():
                    self_ref[pl.ds(row, xr), pl.ds(col, LANES)] = chunk * factors[0]

                @pl.when(owner >= side)
                def _():
                    neigh_ref[pl.ds(row, xr), pl.ds(col, LANES)] = chunk * factors[1]

                @pl.when(turn == 0)
                def _():
                    total = ref[t, xr:, :].astype(F32)
                    total = (total[:1] + total[8:9]) * factors[0]
                    bias_ref[:, pl.ds(col, LANES)] += total

    weight = shape((depth, hid), F32)
    outs = [weight, weight, shape((1, hid), F32)]
    return call(body, outs, [p[0] for p in pieces], after=after)


def local(
    features, w_neigh, w_self, bias, cotangent, block_rows, block_cols, block_vals, block_count
):
    rs = lax.axis_size("row")
    cs = lax.axis_size("col")
    nd, depth = features.shape
    hid = w_self.shape[1]
    rt = nd * cs
    half = rs // 2
    xw = 2 * depth // cs
    nc = min(rs, hid // LANES)
    nr = rs // nc
    xr = xw // nr

    def along_col(x, k):
        return lax.ppermute(x, "col", [(s, (s + k) % cs) for s in range(cs)])

    def along_chips(x, k):
        return lax.ppermute(
            x, "row", [(s, 2 * ((s // 2 + k) % half) + s % 2) for s in range(rs)]
        )

    def other_core(x):
        return lax.ppermute(x, "row", [(s, s ^ 1) for s in range(rs)])

    def from_shift(k):
        return lambda own: lax.rem(own + cs - k, cs)

    def from_flip(bits):
        return lambda own: own ^ bits

    def flip_col(x, bits):
        return lax.ppermute(x, "col", [(s, s ^ bits) for s in range(cs)])

    blocks = [features] + [along_chips(features, k) for k in range(1, half)]
    blocks = blocks + [other_core(x) for x in blocks]
    own_feat = lax.ppermute(
        follow(features, blocks[1:half]),
        ("row", "col"),
        [((b % rs) * cs + b // rs, b) for b in range(rs * cs)],
    )
    tile, turned, mass = densify(
        block_rows.reshape(-1),
        block_cols.reshape(-1),
        block_count.reshape(-1),
        block_vals[0, 0],
        nd,
        rs,
        cs,
    )
    degree = mass
    for k in range(1, cs):
        degree = degree + along_col(mass, k)
    inverse = 1.0 / (degree[0] + 1.0)
    inverse = jnp.broadcast_to(inverse[:, None], (rt, LANES))
    own = jnp.dot(own_feat, w_self, preferred_element_type=F32).astype(BF16)

    parts = forward_parts(tile, blocks, nd, cs)
    parts = [parts[0]] + [along_col(parts[k], k) for k in range(1, cs)]
    output, sums, *packs = activation(
        parts, inverse, own, own_feat, w_neigh, bias[None, :], cotangent
    )
    packs = [packs[0]] + [along_col(packs[k], k) for k in range(1, cs)]

    keep, send = weight_parts(packs, sums, rs, xr, nc)
    came = other_core(send)
    scaled, self_part = scaled_parts(packs, inverse, w_neigh, w_self, [keep])
    chunks = pair_sum(keep, came, True)
    chunk = last_sum([chunks[0]] + [along_chips(chunks[k], k) for k in range(1, half)], True)
    line = [chunk] + [along_chips(chunk, k) for k in range(1, half)]

    keep, send = back_parts(turned, scaled, self_part, nd, cs, rs, [chunks[1]])
    blocks = pair_sum(keep, other_core(send), False, line[1:])
    grad_input = last_sum(
        [blocks[0]] + [along_chips(blocks[k], k) for k in range(1, half)], False
    )

    line = stack(line, [blocks[1]])
    if cs == 4 and half % 2 == 0:
        first, second = flip_col(line, 1), flip_col(line, 2)
        mine = [
            (line, 0, from_flip(0)),
            (first, 0, from_flip(1)),
            (second, 0, from_flip(2)),
            (flip_col(first[: half // 2], 2), 0, from_flip(3)),
            (flip_col(second[half // 2 :], 1), half // 2, from_flip(3)),
        ]
    else:
        mine = [(line, 0, from_shift(0))]
        mine += [(along_col(line, k), 0, from_shift(k)) for k in range(1, cs)]
    pieces = [(*piece, True) for piece in mine]
    pieces += [(other_core(array), first, owner, False) for array, first, owner in mine]
    factor = 1.0 / math.sqrt(nd * rs * cs)
    total_self, total_neigh, total_bias = assemble(
        pieces, depth, hid, xr, nc, half, cs, (factor, 32.0 * factor), [grad_input]
    )
    return output, grad_input, total_self, total_neigh, total_bias.reshape(-1)


def solution(mesh):
    in_specs = (
        P(("col", "row"), None),
        P(),
        P(),
        P(),
        P(("row", "col"), None),
        P("row", "col", None),
        P("row", "col", None),
        P("row", "col", None, None, None),
        P("row", "col"),
    )
    out_specs = (P(("row", "col"), None), P(("col", "row"), None), P(), P(), P())
    return jax.shard_map(local, mesh=mesh, in_specs=in_specs, out_specs=out_specs, check_vma=False)
```

```python
import math

import jax
import jax.numpy as jnp
from jax import lax
from jax.experimental import pallas as pl
from jax.experimental.pallas import tpu as pltpu
from jax.sharding import PartitionSpec as P

F32 = jnp.float32
BF16 = jnp.bfloat16
LANES = 128
EXTRA = 16
VMEM = pl.BlockSpec(memory_space=pltpu.VMEM)
SMEM = pl.BlockSpec(memory_space=pltpu.SMEM)
PARAMS = pltpu.CompilerParams(vmem_limit_bytes=48 * 1024 * 1024)


def call(body, outs, args, scratch=(), smem=0, flops=0, after=()):
    count = len(args)
    moved = sum(math.prod(o.shape) * o.dtype.itemsize for o in outs)
    moved += sum(a.size * a.dtype.itemsize for a in args)

    def run(*refs):
        body(*refs[:count], *refs[count + len(after) :])

    return pl.pallas_call(
        run,
        out_shape=outs,
        in_specs=[SMEM] * smem
        + [VMEM] * (count - smem)
        + [pl.BlockSpec(memory_space=pl.ANY)] * len(after),
        out_specs=[VMEM] * len(outs),
        scratch_shapes=list(scratch),
        compiler_params=PARAMS,
        cost_estimate=pl.CostEstimate(flops=flops, bytes_accessed=moved, transcendentals=0),
    )(*args, *after)


def shape(dims, dtype):
    return jax.ShapeDtypeStruct(tuple(dims), dtype)


def mm(a, b, ca=1, cb=0):
    return lax.dot_general(a, b, (((ca,), (cb,)), ((), ())), preferred_element_type=F32)


def follow(x, after):
    def body(x_ref, out_ref):
        out_ref[...] = x_ref[...]

    return call(body, [shape(x.shape, x.dtype)], [x], after=after)[0]


def turn(weights, after):
    def body(*refs):
        for ref, out_ref in zip(refs, refs[len(weights) :]):
            out_ref[...] = ref[...].T

    return call(body, [shape(w.shape[::-1], w.dtype) for w in weights], weights, after=after)


def stack(parts, after):
    def body(*refs):
        for k, ref in enumerate(refs[:-1]):
            refs[-1][k] = ref[...]

    out = shape((len(parts), *parts[0].shape), parts[0].dtype)
    return call(body, [out], parts, after=after)[0]


def densify(rows, cols, count, values, nd, rs, cs, after):
    rt, ct, half = nd * cs, nd * rs, rs // 2

    def body(rows_ref, cols_ref, count_ref, values_ref, tile_ref, turned_ref, mass_ref, acc):
        i, j = lax.axis_index("row"), lax.axis_index("col")
        z, c = i // 2, lax.rem(i, 2)
        acc[...] = jnp.zeros_like(acc)

        def add(s, carry):
            col = cols_ref[s]
            row = rows_ref[s] ^ j
            col = (z ^ (col // 2)) + half * (lax.rem(col, 2) ^ c)
            r = pl.multiple_of(row * nd, nd)
            c0 = pl.multiple_of(col * nd, nd)
            acc[pl.ds(r, nd), pl.ds(c0, nd)] += values_ref[s].astype(F32)
            return carry

        lax.fori_loop(0, count_ref[0], add, 0)
        tile_ref[...] = acc[...].astype(BF16)
        ones = jnp.ones((8, ct), BF16)
        for k in range(cs):
            place = pl.multiple_of((j ^ k) * nd, nd)
            mass_ref[:, pl.ds(place, nd)] = mm(ones, tile_ref[k * nd : (k + 1) * nd, :], 1, 1)
        for k in range(rs):
            cut = acc[:, k * nd : (k + 1) * nd]
            turned_ref[k * nd : (k + 1) * nd, :] = cut.T.astype(BF16)

    return call(
        body,
        [shape((rt, ct), BF16), shape((ct, rt), BF16), shape((8, rt), F32)],
        [rows, cols, count, values],
        [pltpu.VMEM((rt, ct), F32)],
        smem=3,
        flops=2 * 8 * rt * ct,
        after=after,
    )


def forward_parts(tile, blocks, nd, cs, after):
    width = blocks[0].shape[1]

    def body(*refs):
        tile_ref, feat_refs = refs[0], refs[1 : 1 + len(blocks)]
        outs = refs[1 + len(blocks) :]
        feats = jnp.concatenate([r[...] for r in feat_refs], axis=0)
        parts = mm(tile_ref[...], feats)
        for k in range(cs):
            outs[k][...] = parts[k * nd : (k + 1) * nd].astype(outs[k].dtype)

    return call(
        body,
        [shape((nd, width), BF16 if k else F32) for k in range(cs)],
        [tile, *blocks],
        flops=2 * tile.size * width,
        after=after,
    )


def activation(parts, inverse, own, own_feat, w_neigh, bias, cotangent, after):
    cs = len(parts)
    nd, hid = own.shape
    depth = own_feat.shape[1]
    xw = 2 * depth // cs

    def body(*refs):
        part_refs = refs[:cs]
        inv_ref, own_ref, feat_ref, w_ref, bias_ref, cot_ref = refs[cs : cs + 6]
        out_ref, sum_ref, *packs = refs[cs + 6 : -1]
        both = refs[-1]
        j = lax.axis_index("col")
        inv = inv_ref[pl.ds(pl.multiple_of(j * nd, nd), nd), :]
        total = sum(r[...].astype(F32) for r in part_refs)
        mean = (total * jnp.concatenate([inv] * (depth // LANES), axis=1)).astype(BF16)
        both[:, :depth] = feat_ref[...]
        both[:, depth:] = mean
        pre = own_ref[...].astype(F32) + mm(mean, w_ref[...]) + bias_ref[...]
        slope = jnp.where(pre > 0, 1.0, jnp.exp(jnp.minimum(pre, 0.0)))
        out_ref[...] = jnp.where(pre > 0, pre, slope - 1.0).astype(BF16)
        grad = cot_ref[...].astype(F32) * slope
        sum_ref[...] = jnp.broadcast_to(jnp.sum(grad, axis=0, keepdims=True), (8, hid))
        grad = grad.astype(BF16)
        for k in range(cs):
            packs[k][:, :hid] = grad
            target = j ^ k
            if xw % LANES == 0:
                start = pl.multiple_of(target * xw, LANES)
                packs[k][:, hid:] = both[:, pl.ds(start, xw)]
            else:
                for d in range(cs):

                    @pl.when(target == d)
                    def _():
                        packs[k][:, hid:] = both[:, d * xw : (d + 1) * xw]

    return call(
        body,
        [shape((nd, hid), BF16), shape((8, hid), F32)] + [shape((nd, hid + xw), BF16)] * cs,
        [*parts, inverse, own, own_feat, w_neigh, bias, cotangent],
        [pltpu.VMEM((nd, 2 * depth), BF16)],
        flops=2 * own_feat.size * hid,
        after=after,
    )


def split_pair(total):
    high = total.astype(BF16).astype(F32)
    return jnp.concatenate([high, total - high], axis=0)


def weight_parts(packs, sums, rs, xr, nc):
    cs = len(packs)
    hid = sums.shape[1]
    nd, xw = packs[0].shape[0], packs[0].shape[1] - hid
    half = rs // 2

    def body(*refs):
        pack_refs = refs[:cs]
        sum_ref, keep_ref, send_ref, acc = refs[cs:]
        x_all = jnp.concatenate([r[:, hid:] for r in pack_refs], axis=0)
        g_all = jnp.concatenate([r[:, :hid] for r in pack_refs], axis=0)
        acc[...] = mm(x_all, g_all, 0, 0)
        i = lax.axis_index("row")
        z, c = i // 2, lax.rem(i, 2)
        for k in range(half):
            for core, ref in ((c, keep_ref), (1 - c, send_ref)):
                q = 2 * (z ^ k) + core
                row = pl.multiple_of((q // nc) * xr, xr)
                col = pl.multiple_of(lax.rem(q, nc) * LANES, LANES)
                ref[k, :xr, :] = acc[pl.ds(row, xr), pl.ds(col, LANES)].astype(ref.dtype)
                ref[k, xr:, :] = split_pair(sum_ref[:, pl.ds(col, LANES)]).astype(ref.dtype)

    dims = (half, xr + EXTRA, LANES)
    return call(
        body,
        [shape(dims, F32), shape(dims, BF16)],
        [*packs, sums],
        [pltpu.VMEM((xw, hid), F32)],
        flops=2 * cs * nd * xw * hid,
    )


def scaled_parts(packs, inverse, turned_neigh, turned_self, rs, after):
    cs = len(packs)
    nd = packs[0].shape[0]
    hid, depth = turned_neigh.shape

    def body(neigh_ref, own_ref, inv_ref, *refs):
        pack_refs, scaled_ref, self_ref = refs[:cs], refs[cs], refs[cs + 1]
        i, j = lax.axis_index("row"), lax.axis_index("col")
        grads = jnp.concatenate([r[:, :hid] for r in pack_refs], axis=0)
        product = mm(grads, neigh_ref[...])
        for r in range(cs):
            inv = inv_ref[pl.ds(pl.multiple_of((j ^ r) * nd, nd), nd), :]
            inv = jnp.concatenate([inv] * (depth // LANES), axis=1)
            rows = slice(r * nd, (r + 1) * nd)
            scaled_ref[rows, :] = (product[rows] * inv).astype(BF16)

        @pl.when(i * cs // rs == j)
        def _():
            self_ref[...] = mm(grads, own_ref[...])

    return call(
        body,
        [shape((cs * nd, depth), BF16), shape((cs * nd, depth), F32)],
        [turned_neigh, turned_self, inverse, *packs],
        flops=4 * cs * nd * hid * depth,
        after=after,
    )


def halving_order(count):
    order = [0]
    step = count // 2
    while step:
        order = order + [d + step for d in order]
        step //= 2
    return order


def back_parts(turned, scaled, self_part, nd, cs, rs, after):
    depth = scaled.shape[1]
    half = rs // 2

    def body(tile_ref, scaled_ref, self_ref, keep_ref, send_ref, acc):
        i, j = lax.axis_index("row"), lax.axis_index("col")
        z, c = i // 2, lax.rem(i, 2)
        acc[...] = mm(tile_ref[...], scaled_ref[...])

        @pl.when(i * cs // rs == j)
        def _():
            for r in range(cs):
                q = i * cs - j * rs + (j ^ r)
                place = ((z ^ (q // 2)) + half * (lax.rem(q, 2) ^ c)) * nd
                acc[pl.ds(pl.multiple_of(place, nd), nd), :] += self_ref[r * nd : (r + 1) * nd]

        for ref, base in ((send_ref, half), (keep_ref, 0)):
            for k, distance in enumerate(halving_order(half)):
                place = (base + distance) * nd
                ref[k] = acc[place : place + nd, :].astype(ref.dtype)

    dims = (half, nd, depth)
    return call(
        body,
        [shape(dims, F32), shape(dims, BF16)],
        [turned, scaled, self_part],
        [pltpu.VMEM((rs * nd, depth), F32)],
        flops=2 * turned.size * depth,
        after=after,
    )


def fold(keep, came, after=()):
    count, rows, width = keep.shape
    half = count // 2

    def body(keep_ref, came_ref, *outs):
        total = keep_ref[...] + came_ref[...].astype(F32)
        if count == 1:
            outs[0][...] = total[0].astype(BF16)
        else:
            outs[0][...] = total[:half]
            outs[1][...] = total[half:].astype(BF16)

    if count == 1:
        return call(body, [shape((rows, width), BF16)], [keep, came], after=after)[0]
    dims = (half, rows, width)
    return call(body, [shape(dims, F32), shape(dims, BF16)], [keep, came], after=after)


def pair_sum(keep, came):
    half, rows, width = keep.shape
    main = rows - EXTRA

    def body(keep_ref, came_ref, *outs):
        for k in range(half):
            total = keep_ref[k] + came_ref[k].astype(F32)
            dtype = outs[k].dtype
            outs[k][:main, :] = total[:main].astype(dtype)
            merged = total[main : main + 8] + total[main + 8 :]
            outs[k][main:, :] = split_pair(merged).astype(dtype)

    return call(
        body,
        [shape((rows, width), BF16 if k else F32) for k in range(half)],
        [keep, came],
    )


def last_sum(parts):
    rows, width = parts[0].shape
    main = rows - EXTRA

    def body(*refs):
        out_ref = refs[-1]
        total = refs[0][...]
        for ref in refs[1:-1]:
            total = total + ref[...].astype(F32)
        out_ref[:main, :] = total[:main].astype(BF16)
        merged = total[main : main + 8] + total[main + 8 :]
        out_ref[main:, :] = split_pair(merged).astype(BF16)

    return call(body, [shape((rows, width), BF16)], parts)[0]


def assemble(pieces, mine, begun, depth, hid, xr, nc, cs, factors, after):
    xw = 2 * depth // cs
    side = cs // 2
    copies = sum(len(distances) for _, distances, _ in pieces)
    arrays = [array for array, _, _ in pieces]
    inputs = arrays + list(begun)
    weight = shape((depth, hid), F32)

    def body(*refs):
        piece_refs = refs[: len(pieces)]
        self_ref, neigh_ref, bias_ref, staged, sems = refs[-5:]
        i, j = lax.axis_index("row"), lax.axis_index("col")
        z, c = i // 2, lax.rem(i, 2)
        if begun:
            bias_ref[...] = refs[len(inputs) - 1][...]
        else:
            bias_ref[...] = jnp.zeros_like(bias_ref)
        waits = []
        at = 0
        for ref, (_, distances, column) in zip(piece_refs, pieces):
            owner = j ^ column
            first = owner < side
            for t, distance in enumerate(distances):
                q = 2 * (z ^ distance) + (c if mine else 1 - c)
                col = pl.multiple_of(lax.rem(q, nc) * LANES, LANES)
                turn = q // nc
                row = pl.multiple_of(lax.rem(owner, side) * xw + turn * xr, xr)
                scale = jnp.where(first, factors[0], factors[1])
                staged[at] = ref[t, :xr, :].astype(F32) * scale
                for target, here in ((self_ref, first), (neigh_ref, jnp.logical_not(first))):
                    copy = pltpu.make_async_copy(
                        staged.at[at],
                        target.at[pl.ds(row, xr), pl.ds(col, LANES)],
                        sems.at[at],
                    )
                    pl.when(here)(copy.start)
                    waits.append((here, copy))

                @pl.when(turn == 0)
                def _():
                    total = ref[t, xr:, :].astype(F32)
                    total = (total[:1] + total[8:9]) * factors[0]
                    bias_ref[:, pl.ds(col, LANES)] += total

                at += 1
        for here, copy in waits:
            pl.when(here)(copy.wait)

    def run(*refs):
        body(*refs[: len(inputs)], *refs[len(inputs) + len(after) :])

    somewhere = pl.BlockSpec(memory_space=pl.ANY)
    moved = 2 * copies * xr * LANES * 6
    return pl.pallas_call(
        run,
        out_shape=[weight, weight, shape((1, hid), F32)],
        in_specs=[VMEM] * len(arrays)
        + ([somewhere, somewhere, VMEM] if begun else [])
        + [somewhere] * len(after),
        out_specs=[somewhere, somewhere, VMEM],
        scratch_shapes=[
            pltpu.VMEM((copies, xr, LANES), F32),
            pltpu.SemaphoreType.DMA((copies,)),
        ],
        input_output_aliases={len(arrays): 0, len(arrays) + 1: 1} if begun else {},
        compiler_params=PARAMS,
        cost_estimate=pl.CostEstimate(flops=0, bytes_accessed=moved, transcendentals=0),
    )(*inputs, *after)


def local(
    features, w_neigh, w_self, bias, cotangent, block_rows, block_cols, block_vals, block_count
):
    rs = lax.axis_size("row")
    cs = lax.axis_size("col")
    nd, depth = features.shape
    hid = w_self.shape[1]
    rt = nd * cs
    half = rs // 2
    xw = 2 * depth // cs
    nc = min(rs, hid // LANES)
    nr = rs // nc
    xr = xw // nr

    def along_col(x, k):
        return lax.ppermute(x, "col", [(s, s ^ k) for s in range(cs)])

    def along_chips(x, k):
        return lax.ppermute(x, "row", [(s, s ^ (2 * k)) for s in range(rs)])

    def other_core(x):
        return lax.ppermute(x, "row", [(s, s ^ 1) for s in range(rs)])

    def gather_chips(x, after=()):
        found = {0: x}
        step = half // 2
        while step:
            if step == 1 and after:
                last = {d: follow(y, after) if d else y for d, y in found.items()}
            else:
                last = found
            found.update({d + step: along_chips(last[d], step) for d in list(found)})
            step //= 2
        return [found[d] for d in range(half)]

    swap = [((b % rs) * cs + b // rs, b) for b in range(rs * cs)]
    across = other_core(features)
    own_feat = lax.ppermute(features, ("row", "col"), swap)
    tile, turned, mass = densify(
        block_rows.reshape(-1),
        block_cols.reshape(-1),
        block_count.reshape(-1),
        block_vals[0, 0],
        nd,
        rs,
        cs,
        [across],
    )
    blocks = gather_chips(features, [mass])
    blocks = blocks + [across] + [other_core(x) for x in blocks[1:]]
    degree = mass
    for k in range(1, cs):
        degree = degree + along_col(mass, k)
    inverse = 1.0 / (degree[0] + 1.0)
    inverse = jnp.broadcast_to(inverse[:, None], (rt, LANES))
    own = jnp.dot(own_feat, w_self, preferred_element_type=F32).astype(BF16)

    parts = forward_parts(tile, blocks, nd, cs, [own_feat])
    turned_neigh, turned_self = turn([w_neigh, w_self], [parts[0]])
    parts = [parts[0]] + [along_col(parts[k], k) for k in range(1, cs)]
    output, sums, *packs = activation(
        parts, inverse, own, own_feat, w_neigh, bias[None, :], cotangent, [turned_neigh]
    )
    packs = [packs[0]] + [along_col(packs[k], k) for k in range(1, cs)]

    keep, send = weight_parts(packs, sums, rs, xr, nc)
    came = other_core(send)
    scaled, self_part = scaled_parts(packs, inverse, turned_neigh, turned_self, rs, [keep])
    chunks = pair_sum(keep, came)
    back_after = [chunks[1]]
    chunks = [chunks[0]] + [along_chips(chunks[k], k) for k in range(1, half)]
    line = gather_chips(last_sum(chunks))

    keep, send = back_parts(turned, scaled, self_part, nd, cs, rs, back_after)
    keep, send = fold(keep, other_core(send), line[1:])
    line = stack(line, [send])
    step = 1
    while step < half:
        folded = fold(keep, along_chips(send, step))
        keep, send = folded if 2 * step < half else (folded, None)
        step *= 2
    grad_input = keep

    distances = list(range(half))
    mine = [(line, distances, 0)]
    if cs == 4 and half % 2 == 0:
        mid = half // 2
        first, second = along_col(line, 1), along_col(line, 2)
        mine += [
            (first, distances, 1),
            (second, distances, 2),
            (along_col(first[:mid], 2), distances[:mid], 3),
            (along_col(second[mid:], 1), distances[mid:], 3),
        ]
    else:
        mine += [(along_col(line, k), distances, k) for k in range(1, cs)]
    theirs = [(other_core(array), where, column) for array, where, column in mine]
    factor = 1.0 / math.sqrt(nd * rs * cs)
    sizes = (depth, hid, xr, nc, cs, (factor, 32.0 * factor))
    begun = assemble(mine, True, (), *sizes, ())
    total_self, total_neigh, total_bias = assemble(theirs, False, begun, *sizes, [grad_input])
    return output, grad_input, total_self, total_neigh, total_bias.reshape(-1)


def solution(mesh):
    in_specs = (
        P(("col", "row"), None),
        P(),
        P(),
        P(),
        P(("row", "col"), None),
        P("row", "col", None),
        P("row", "col", None),
        P("row", "col", None, None, None),
        P("row", "col"),
    )
    out_specs = (P(("row", "col"), None), P(("col", "row"), None), P(), P(), P())
    return jax.shard_map(local, mesh=mesh, in_specs=in_specs, out_specs=out_specs, check_vma=False)
```

```python
import math

import jax
import jax.numpy as jnp
from jax import lax
from jax.experimental import pallas as pl
from jax.experimental.pallas import tpu as pltpu
from jax.sharding import PartitionSpec as P

F32 = jnp.float32
BF16 = jnp.bfloat16
LANES = 128
EXTRA = 16
VMEM = pl.BlockSpec(memory_space=pltpu.VMEM)
SMEM = pl.BlockSpec(memory_space=pltpu.SMEM)
PARAMS = pltpu.CompilerParams(vmem_limit_bytes=48 * 1024 * 1024)


def call(body, outs, args, scratch=(), smem=0, flops=0, after=()):
    count = len(args)
    moved = sum(math.prod(o.shape) * o.dtype.itemsize for o in outs)
    moved += sum(a.size * a.dtype.itemsize for a in args)

    def run(*refs):
        body(*refs[:count], *refs[count + len(after) :])

    return pl.pallas_call(
        run,
        out_shape=outs,
        in_specs=[SMEM] * smem
        + [VMEM] * (count - smem)
        + [pl.BlockSpec(memory_space=pl.ANY)] * len(after),
        out_specs=[VMEM] * len(outs),
        scratch_shapes=list(scratch),
        compiler_params=PARAMS,
        cost_estimate=pl.CostEstimate(flops=flops, bytes_accessed=moved, transcendentals=0),
    )(*args, *after)


def shape(dims, dtype):
    return jax.ShapeDtypeStruct(tuple(dims), dtype)


def mm(a, b, ca=1, cb=0):
    return lax.dot_general(a, b, (((ca,), (cb,)), ((), ())), preferred_element_type=F32)


def follow(x, after):
    def body(x_ref, out_ref):
        out_ref[...] = x_ref[...]

    return call(body, [shape(x.shape, x.dtype)], [x], after=after)[0]


def turn(weights, after):
    def body(*refs):
        for ref, out_ref in zip(refs, refs[len(weights) :]):
            out_ref[...] = ref[...].T

    return call(body, [shape(w.shape[::-1], w.dtype) for w in weights], weights, after=after)


def stack(parts, after):
    def body(*refs):
        for k, ref in enumerate(refs[:-1]):
            refs[-1][k] = ref[...]

    out = shape((len(parts), *parts[0].shape), parts[0].dtype)
    return call(body, [out], parts, after=after)[0]


def densify(rows, cols, count, values, nd, rs, cs, after):
    rt, ct, half = nd * cs, nd * rs, rs // 2

    def body(rows_ref, cols_ref, count_ref, values_ref, tile_ref, turned_ref, acc):
        i, j = lax.axis_index("row"), lax.axis_index("col")
        z, c = i // 2, lax.rem(i, 2)
        acc[...] = jnp.zeros_like(acc)

        def add(s, carry):
            col = cols_ref[s]
            row = rows_ref[s] ^ j
            col = (z ^ (col // 2)) + half * (lax.rem(col, 2) ^ c)
            r = pl.multiple_of(row * nd, nd)
            c0 = pl.multiple_of(col * nd, nd)
            acc[pl.ds(r, nd), pl.ds(c0, nd)] += values_ref[s].astype(F32)
            return carry

        lax.fori_loop(0, count_ref[0], add, 0)
        tile_ref[...] = acc[...].astype(BF16)
        for k in range(rs):
            cut = acc[:, k * nd : (k + 1) * nd]
            turned_ref[k * nd : (k + 1) * nd, :] = cut.T.astype(BF16)

    return call(
        body,
        [shape((rt, ct), BF16), shape((ct, rt), BF16)],
        [rows, cols, count, values],
        [pltpu.VMEM((rt, ct), F32)],
        smem=3,
        flops=rt * ct,
        after=after,
    )


def tile_columns(tile_ref, places, nd):
    return jnp.concatenate([tile_ref[:, p * nd : (p + 1) * nd] for p in places], axis=1)


def forward_first(tile, places, blocks, nd, cs, after):
    rt, ct = tile.shape
    width = blocks[0].shape[1]

    def body(*refs):
        tile_ref, feat_refs = refs[0], refs[1 : 1 + len(blocks)]
        sum_ref, mass_ref = refs[1 + len(blocks) :]
        j = lax.axis_index("col")
        feats = jnp.concatenate([r[...] for r in feat_refs], axis=0)
        sum_ref[...] = mm(tile_columns(tile_ref, places, nd), feats)
        ones = jnp.ones((8, ct), BF16)
        for k in range(cs):
            place = pl.multiple_of((j ^ k) * nd, nd)
            mass_ref[:, pl.ds(place, nd)] = mm(ones, tile_ref[k * nd : (k + 1) * nd, :], 1, 1)

    return call(
        body,
        [shape((rt, width), F32), shape((8, rt), F32)],
        [tile, *blocks],
        flops=2 * rt * len(places) * nd * width,
        after=after,
    )


def forward_parts(begun, tile, places, blocks, nd, cs, after):
    width = blocks[0].shape[1]

    def body(*refs):
        sum_ref, tile_ref, feat_refs = refs[0], refs[1], refs[2 : 2 + len(blocks)]
        outs = refs[2 + len(blocks) :]
        feats = jnp.concatenate([r[...] for r in feat_refs], axis=0)
        parts = sum_ref[...] + mm(tile_columns(tile_ref, places, nd), feats)
        for k in range(cs):
            outs[k][...] = parts[k * nd : (k + 1) * nd].astype(outs[k].dtype)

    return call(
        body,
        [shape((nd, width), BF16 if k else F32) for k in range(cs)],
        [begun, tile, *blocks],
        flops=2 * tile.shape[0] * len(places) * nd * width,
        after=after,
    )


def activation(parts, inverse, own, own_feat, w_neigh, bias, cotangent, after):
    cs = len(parts)
    nd, hid = own.shape
    depth = own_feat.shape[1]
    xw = 2 * depth // cs

    def body(*refs):
        part_refs = refs[:cs]
        inv_ref, own_ref, feat_ref, w_ref, bias_ref, cot_ref = refs[cs : cs + 6]
        out_ref, sum_ref, *packs = refs[cs + 6 : -1]
        both = refs[-1]
        j = lax.axis_index("col")
        inv = inv_ref[pl.ds(pl.multiple_of(j * nd, nd), nd), :]
        total = sum(r[...].astype(F32) for r in part_refs)
        mean = (total * jnp.concatenate([inv] * (depth // LANES), axis=1)).astype(BF16)
        both[:, :depth] = feat_ref[...]
        both[:, depth:] = mean
        pre = own_ref[...].astype(F32) + mm(mean, w_ref[...]) + bias_ref[...]
        slope = jnp.where(pre > 0, 1.0, jnp.exp(jnp.minimum(pre, 0.0)))
        out_ref[...] = jnp.where(pre > 0, pre, slope - 1.0).astype(BF16)
        grad = cot_ref[...].astype(F32) * slope
        sum_ref[...] = jnp.broadcast_to(jnp.sum(grad, axis=0, keepdims=True), (8, hid))
        grad = grad.astype(BF16)
        for k in range(cs):
            packs[k][:, :hid] = grad
            target = j ^ k
            if xw % LANES == 0:
                start = pl.multiple_of(target * xw, LANES)
                packs[k][:, hid:] = both[:, pl.ds(start, xw)]
            else:
                for d in range(cs):

                    @pl.when(target == d)
                    def _():
                        packs[k][:, hid:] = both[:, d * xw : (d + 1) * xw]

    return call(
        body,
        [shape((nd, hid), BF16), shape((8, hid), F32)] + [shape((nd, hid + xw), BF16)] * cs,
        [*parts, inverse, own, own_feat, w_neigh, bias, cotangent],
        [pltpu.VMEM((nd, 2 * depth), BF16)],
        flops=2 * own_feat.size * hid,
        after=after,
    )


def split_pair(total):
    high = total.astype(BF16).astype(F32)
    return jnp.concatenate([high, total - high], axis=0)


def weight_parts(packs, sums, rs, xr, nc, after):
    cs = len(packs)
    hid = sums.shape[1]
    nd, xw = packs[0].shape[0], packs[0].shape[1] - hid
    half = rs // 2

    def body(*refs):
        pack_refs = refs[:cs]
        sum_ref, keep_ref, send_ref, acc = refs[cs:]
        x_all = jnp.concatenate([r[:, hid:] for r in pack_refs], axis=0)
        g_all = jnp.concatenate([r[:, :hid] for r in pack_refs], axis=0)
        acc[...] = mm(x_all, g_all, 0, 0)
        i = lax.axis_index("row")
        z, c = i // 2, lax.rem(i, 2)
        for k in range(half):
            for core, ref in ((c, keep_ref), (1 - c, send_ref)):
                q = 2 * (z ^ k) + core
                row = pl.multiple_of((q // nc) * xr, xr)
                col = pl.multiple_of(lax.rem(q, nc) * LANES, LANES)
                ref[k, :xr, :] = acc[pl.ds(row, xr), pl.ds(col, LANES)].astype(ref.dtype)
                ref[k, xr:, :] = split_pair(sum_ref[:, pl.ds(col, LANES)]).astype(ref.dtype)

    dims = (half, xr + EXTRA, LANES)
    return call(
        body,
        [shape(dims, F32), shape(dims, BF16)],
        [*packs, sums],
        [pltpu.VMEM((xw, hid), F32)],
        flops=2 * cs * nd * xw * hid,
        after=after,
    )


def scaled_parts(packs, first, inverse, turned_neigh, turned_self, cs, rs, after=()):
    count = len(packs)
    nd = packs[0].shape[0]
    hid, depth = turned_neigh.shape

    def body(neigh_ref, own_ref, inv_ref, *refs):
        pack_refs, scaled_ref, self_ref = refs[:count], refs[count], refs[count + 1]
        i, j = lax.axis_index("row"), lax.axis_index("col")
        grads = jnp.concatenate([r[:, :hid] for r in pack_refs], axis=0)
        product = mm(grads, neigh_ref[...])
        for r in range(count):
            start = pl.multiple_of((j ^ (first + r)) * nd, nd)
            inv = inv_ref[pl.ds(start, nd), :]
            inv = jnp.concatenate([inv] * (depth // LANES), axis=1)
            rows = slice(r * nd, (r + 1) * nd)
            scaled_ref[rows, :] = (product[rows] * inv).astype(BF16)

        @pl.when(i * cs // rs == j)
        def _():
            self_ref[...] = mm(grads, own_ref[...])

    return call(
        body,
        [shape((count * nd, depth), BF16), shape((count * nd, depth), F32)],
        [turned_neigh, turned_self, inverse, *packs],
        flops=4 * count * nd * hid * depth,
        after=after,
    )


def halving_order(count):
    order = [0]
    step = count // 2
    while step:
        order = order + [d + step for d in order]
        step //= 2
    return order


def back_parts(turned, scaled, self_parts, nd, cs, rs, after):
    depth = scaled[0].shape[1]
    half = rs // 2
    count = len(scaled)
    each = cs // count

    def body(tile_ref, *refs):
        scaled_refs, self_refs = refs[:count], refs[count : 2 * count]
        keep_ref, send_ref, acc = refs[2 * count :]
        i, j = lax.axis_index("row"), lax.axis_index("col")
        z, c = i // 2, lax.rem(i, 2)
        acc[...] = mm(tile_ref[...], jnp.concatenate([r[...] for r in scaled_refs], axis=0))

        @pl.when(i * cs // rs == j)
        def _():
            for r in range(cs):
                q = i * cs - j * rs + (j ^ r)
                place = ((z ^ (q // 2)) + half * (lax.rem(q, 2) ^ c)) * nd
                rows = slice(r % each * nd, (r % each + 1) * nd)
                acc[pl.ds(pl.multiple_of(place, nd), nd), :] += self_refs[r // each][rows]

        for ref, base in ((send_ref, half), (keep_ref, 0)):
            for k, distance in enumerate(halving_order(half)):
                place = (base + distance) * nd
                ref[k] = acc[place : place + nd, :].astype(ref.dtype)

    dims = (half, nd, depth)
    return call(
        body,
        [shape(dims, F32), shape(dims, BF16)],
        [turned, *scaled, *self_parts],
        [pltpu.VMEM((rs * nd, depth), F32)],
        flops=2 * turned.size * depth,
        after=after,
    )


def fold(keep, came, after=()):
    count, rows, width = keep.shape
    half = count // 2

    def body(keep_ref, came_ref, *outs):
        total = keep_ref[...] + came_ref[...].astype(F32)
        if count == 1:
            outs[0][...] = total[0].astype(BF16)
        else:
            outs[0][...] = total[:half]
            outs[1][...] = total[half:].astype(BF16)

    if count == 1:
        return call(body, [shape((rows, width), BF16)], [keep, came], after=after)[0]
    dims = (half, rows, width)
    return call(body, [shape(dims, F32), shape(dims, BF16)], [keep, came], after=after)


def pair_sum(keep, came):
    half, rows, width = keep.shape
    main = rows - EXTRA

    def body(keep_ref, came_ref, *outs):
        for k in range(half):
            total = keep_ref[k] + came_ref[k].astype(F32)
            dtype = outs[k].dtype
            outs[k][:main, :] = total[:main].astype(dtype)
            merged = total[main : main + 8] + total[main + 8 :]
            outs[k][main:, :] = split_pair(merged).astype(dtype)

    return call(
        body,
        [shape((rows, width), BF16 if k else F32) for k in range(half)],
        [keep, came],
    )


def last_sum(parts):
    rows, width = parts[0].shape
    main = rows - EXTRA

    def body(*refs):
        out_ref = refs[-1]
        total = refs[0][...]
        for ref in refs[1:-1]:
            total = total + ref[...].astype(F32)
        out_ref[:main, :] = total[:main].astype(BF16)
        merged = total[main : main + 8] + total[main + 8 :]
        out_ref[main:, :] = split_pair(merged).astype(BF16)

    return call(body, [shape((rows, width), BF16)], parts)[0]


def assemble(pieces, mine, begun, depth, hid, xr, nc, cs, factors, after):
    xw = 2 * depth // cs
    side = cs // 2
    copies = sum(len(distances) for _, distances, _ in pieces)
    arrays = [array for array, _, _ in pieces]
    inputs = arrays + list(begun)
    weight = shape((depth, hid), F32)

    def body(*refs):
        piece_refs = refs[: len(pieces)]
        self_ref, neigh_ref, bias_ref, staged, sems = refs[-5:]
        i, j = lax.axis_index("row"), lax.axis_index("col")
        z, c = i // 2, lax.rem(i, 2)
        if begun:
            bias_ref[...] = refs[len(inputs) - 1][...]
        else:
            bias_ref[...] = jnp.zeros_like(bias_ref)
        waits = []
        at = 0
        for ref, (_, distances, column) in zip(piece_refs, pieces):
            owner = j ^ column
            first = owner < side
            for t, distance in enumerate(distances):
                q = 2 * (z ^ distance) + (c if mine else 1 - c)
                col = pl.multiple_of(lax.rem(q, nc) * LANES, LANES)
                turn = q // nc
                row = pl.multiple_of(lax.rem(owner, side) * xw + turn * xr, xr)
                scale = jnp.where(first, factors[0], factors[1])
                staged[at] = ref[t, :xr, :].astype(F32) * scale
                for target, here in ((self_ref, first), (neigh_ref, jnp.logical_not(first))):
                    copy = pltpu.make_async_copy(
                        staged.at[at],
                        target.at[pl.ds(row, xr), pl.ds(col, LANES)],
                        sems.at[at],
                    )
                    pl.when(here)(copy.start)
                    waits.append((here, copy))

                @pl.when(turn == 0)
                def _():
                    total = ref[t, xr:, :].astype(F32)
                    total = (total[:1] + total[8:9]) * factors[0]
                    bias_ref[:, pl.ds(col, LANES)] += total

                at += 1
        for here, copy in waits:
            pl.when(here)(copy.wait)

    def run(*refs):
        body(*refs[: len(inputs)], *refs[len(inputs) + len(after) :])

    somewhere = pl.BlockSpec(memory_space=pl.ANY)
    moved = 2 * copies * xr * LANES * 6
    return pl.pallas_call(
        run,
        out_shape=[weight, weight, shape((1, hid), F32)],
        in_specs=[VMEM] * len(arrays)
        + ([somewhere, somewhere, VMEM] if begun else [])
        + [somewhere] * len(after),
        out_specs=[somewhere, somewhere, VMEM],
        scratch_shapes=[
            pltpu.VMEM((copies, xr, LANES), F32),
            pltpu.SemaphoreType.DMA((copies,)),
        ],
        input_output_aliases={len(arrays): 0, len(arrays) + 1: 1} if begun else {},
        compiler_params=PARAMS,
        cost_estimate=pl.CostEstimate(flops=0, bytes_accessed=moved, transcendentals=0),
    )(*inputs, *after)


def local(
    features, w_neigh, w_self, bias, cotangent, block_rows, block_cols, block_vals, block_count
):
    rs = lax.axis_size("row")
    cs = lax.axis_size("col")
    nd, depth = features.shape
    hid = w_self.shape[1]
    rt = nd * cs
    half = rs // 2
    xw = 2 * depth // cs
    nc = min(rs, hid // LANES)
    nr = rs // nc
    xr = xw // nr

    def along_col(x, k):
        return lax.ppermute(x, "col", [(s, s ^ k) for s in range(cs)])

    def along_chips(x, k):
        return lax.ppermute(x, "row", [(s, s ^ (2 * k)) for s in range(rs)])

    def other_core(x):
        return lax.ppermute(x, "row", [(s, s ^ 1) for s in range(rs)])

    def gather_chips(x):
        found = {0: x}
        step = half // 2
        while step:
            found.update({d + step: along_chips(found[d], step) for d in list(found)})
            step //= 2
        return [found[d] for d in range(half)]

    if rs == 2 * cs:

        def send_own(block, t):
            pairs = []
            for z in range(half):
                for core in range(2):
                    q = 2 * (z ^ t) + core
                    source = (2 * z + core) * cs + z
                    pairs.append((source, (2 * z + q // cs) * cs + q % cs))
            return lax.ppermute(block, ("row", "col"), pairs)

    else:
        swap = [((b % rs) * cs + b // rs, b) for b in range(rs * cs)]

        def send_own(block, t):
            return lax.ppermute(block, ("row", "col"), swap if t == 0 else [])

    near = along_chips(features, 1)
    mine_first = {0: features, 1: near}
    step = half // 2
    while step > 1:
        evens = [d for d in mine_first if d % 2 == 0]
        mine_first.update({d + step: along_chips(mine_first[d], step) for d in evens})
        step //= 2
    theirs_first = {0: other_core(features), 1: other_core(near)}
    own_feats = {0: send_own(features, 0)}
    tile, turned = densify(
        block_rows.reshape(-1),
        block_cols.reshape(-1),
        block_count.reshape(-1),
        block_vals[0, 0],
        nd,
        rs,
        cs,
        [near, theirs_first[0], own_feats[0]],
    )
    mine_first.update(
        {d: follow(x, [tile, theirs_first[1]]) for d, x in mine_first.items() if d > 1}
    )
    mine_last = {d + 1: along_chips(x, 1) for d, x in mine_first.items() if d > 1}
    theirs_first.update({d: other_core(x) for d, x in mine_first.items() if d > 1})
    theirs_last = {d: other_core(x) for d, x in mine_last.items()}
    own_feats.update({d: send_own(x, d) for d, x in mine_first.items() if d})
    own_feats.update({d: send_own(x, d) for d, x in mine_last.items()})

    def placed(mine, theirs):
        places = list(mine) + [half + d for d in theirs]
        return places, [*mine.values(), *theirs.values()]

    begun, mass = forward_first(
        tile, *placed(mine_first, theirs_first), nd, cs, [own_feats[1]]
    )
    evens = [x for d, x in own_feats.items() if d and d % 2 == 0]
    parts = forward_parts(begun, tile, *placed(mine_last, theirs_last), nd, cs, evens)
    own_feat = sum(list(own_feats.values())[1:], own_feats[0])
    degree = mass
    step = 1
    while step < cs:
        degree = degree + along_col(degree, step)
        step *= 2
    inverse = 1.0 / (degree[0] + 1.0)
    inverse = jnp.broadcast_to(inverse[:, None], (rt, LANES))
    own = jnp.dot(own_feat, w_self, preferred_element_type=F32).astype(BF16)

    turned_neigh, turned_self = turn([w_neigh, w_self], [parts[0]])
    parts = [parts[0]] + [along_col(parts[k], k) for k in range(1, cs)]
    output, sums, *packs = activation(
        parts, inverse, own, own_feat, w_neigh, bias[None, :], cotangent, [turned_neigh]
    )
    packs = [packs[0]] + [along_col(packs[k], k) for k in range(1, cs)]

    mid = cs // 2
    scaled_args = (inverse, turned_neigh, turned_self, cs, rs)
    early = scaled_parts(packs[:mid], 0, *scaled_args)
    keep, send = weight_parts(packs, sums, rs, xr, nc, early[:1])
    came = other_core(send)
    late = scaled_parts(packs[mid:], mid, *scaled_args, [keep])
    scaled, self_parts = zip(early, late)
    chunks = pair_sum(keep, came)
    back_after = [chunks[1]]
    chunks = [chunks[0]] + [along_chips(chunks[k], k) for k in range(1, half)]
    line = gather_chips(last_sum(chunks))

    keep, send = back_parts(turned, scaled, self_parts, nd, cs, rs, back_after)
    keep, send = fold(keep, other_core(send), line[1:])
    line = stack(line, [send])
    step = 1
    while step < half:
        folded = fold(keep, along_chips(send, step))
        keep, send = folded if 2 * step < half else (folded, None)
        step *= 2
    grad_input = keep

    distances = list(range(half))
    mine = [(line, distances, 0)]
    if cs == 4 and half % 2 == 0:
        mid = half // 2
        first, second = along_col(line, 1), along_col(line, 2)
        mine += [
            (first, distances, 1),
            (second, distances, 2),
            (along_col(first[:mid], 2), distances[:mid], 3),
            (along_col(second[mid:], 1), distances[mid:], 3),
        ]
    else:
        mine += [(along_col(line, k), distances, k) for k in range(1, cs)]
    theirs = [(other_core(array), where, column) for array, where, column in mine]
    factor = 1.0 / math.sqrt(nd * rs * cs)
    sizes = (depth, hid, xr, nc, cs, (factor, 32.0 * factor))
    begun = assemble(mine, True, (), *sizes, ())
    total_self, total_neigh, total_bias = assemble(theirs, False, begun, *sizes, [grad_input])
    return output, grad_input, total_self, total_neigh, total_bias.reshape(-1)


def solution(mesh):
    in_specs = (
        P(("col", "row"), None),
        P(),
        P(),
        P(),
        P(("row", "col"), None),
        P("row", "col", None),
        P("row", "col", None),
        P("row", "col", None, None, None),
        P("row", "col"),
    )
    out_specs = (P(("row", "col"), None), P(("col", "row"), None), P(), P(), P())
    return jax.shard_map(local, mesh=mesh, in_specs=in_specs, out_specs=out_specs, check_vma=False)
```

```python
import math

import jax
import jax.numpy as jnp
from jax import lax
from jax.experimental import pallas as pl
from jax.experimental.pallas import tpu as pltpu
from jax.sharding import PartitionSpec as P

F32 = jnp.float32
BF16 = jnp.bfloat16
LANES = 128
EXTRA = 16
VMEM = pl.BlockSpec(memory_space=pltpu.VMEM)
SMEM = pl.BlockSpec(memory_space=pltpu.SMEM)
PARAMS = pltpu.CompilerParams(vmem_limit_bytes=48 * 1024 * 1024)


def call(body, outs, args, scratch=(), smem=0, flops=0, after=()):
    count = len(args)
    moved = sum(math.prod(o.shape) * o.dtype.itemsize for o in outs)
    moved += sum(a.size * a.dtype.itemsize for a in args)

    def run(*refs):
        body(*refs[:count], *refs[count + len(after) :])

    return pl.pallas_call(
        run,
        out_shape=outs,
        in_specs=[SMEM] * smem
        + [VMEM] * (count - smem)
        + [pl.BlockSpec(memory_space=pl.ANY)] * len(after),
        out_specs=[VMEM] * len(outs),
        scratch_shapes=list(scratch),
        compiler_params=PARAMS,
        cost_estimate=pl.CostEstimate(flops=flops, bytes_accessed=moved, transcendentals=0),
    )(*args, *after)


def shape(dims, dtype):
    return jax.ShapeDtypeStruct(tuple(dims), dtype)


def mm(a, b, ca=1, cb=0):
    return lax.dot_general(a, b, (((ca,), (cb,)), ((), ())), preferred_element_type=F32)


def follow(x, after):
    def body(x_ref, out_ref):
        out_ref[...] = x_ref[...]

    return call(body, [shape(x.shape, x.dtype)], [x], after=after)[0]


def turn(weights, after):
    def body(*refs):
        for ref, out_ref in zip(refs, refs[len(weights) :]):
            out_ref[...] = ref[...].T

    return call(body, [shape(w.shape[::-1], w.dtype) for w in weights], weights, after=after)


def stack(parts, joined=False, after=()):
    count = parts[0].shape[0] if joined else 1

    def body(*refs):
        for k, ref in enumerate(refs[:-1]):
            if joined:
                refs[-1][k * count : (k + 1) * count] = ref[...]
            else:
                refs[-1][k] = ref[...]

    dims = parts[0].shape[1:] if joined else parts[0].shape
    out = shape((len(parts) * count, *dims), parts[0].dtype)
    return call(body, [out], parts, after=after)[0]


def densify(rows, cols, count, values, nd, rs, cs, after):
    rt, ct, half = nd * cs, nd * rs, rs // 2

    def body(rows_ref, cols_ref, count_ref, values_ref, tile_ref, turned_ref, acc):
        i, j = lax.axis_index("row"), lax.axis_index("col")
        z, c = i // 2, lax.rem(i, 2)
        acc[...] = jnp.zeros_like(acc)

        def add(s, carry):
            col = cols_ref[s]
            row = rows_ref[s] ^ j
            col = (z ^ (col // 2)) + half * (lax.rem(col, 2) ^ c)
            r = pl.multiple_of(row * nd, nd)
            c0 = pl.multiple_of(col * nd, nd)
            acc[pl.ds(r, nd), pl.ds(c0, nd)] += values_ref[s].astype(F32)
            return carry

        lax.fori_loop(0, count_ref[0], add, 0)
        tile_ref[...] = acc[...].astype(BF16)
        for k in range(rs):
            cut = acc[:, k * nd : (k + 1) * nd]
            turned_ref[k * nd : (k + 1) * nd, :] = cut.T.astype(BF16)

    return call(
        body,
        [shape((rt, ct), BF16), shape((ct, rt), BF16)],
        [rows, cols, count, values],
        [pltpu.VMEM((rt, ct), F32)],
        smem=3,
        flops=rt * ct,
        after=after,
    )


def tile_columns(tile_ref, places, nd):
    return jnp.concatenate([tile_ref[:, p * nd : (p + 1) * nd] for p in places], axis=1)


def row_sums(tile, nd, cs, after):
    rt, ct = tile.shape

    def body(tile_ref, mass_ref):
        j = lax.axis_index("col")
        ones = jnp.ones((8, ct), BF16)
        for k in range(cs):
            place = pl.multiple_of((j ^ k) * nd, nd)
            mass_ref[:, pl.ds(place, nd)] = mm(ones, tile_ref[k * nd : (k + 1) * nd, :], 1, 1)

    return call(body, [shape((8, rt), F32)], [tile], flops=16 * tile.size, after=after)[0]


def forward_first(tile, places, blocks, nd, after):
    rt = tile.shape[0]
    width = blocks[0].shape[1]

    def body(*refs):
        tile_ref, feat_refs = refs[0], refs[1 : 1 + len(blocks)]
        sum_ref = refs[1 + len(blocks)]
        feats = jnp.concatenate([r[...] for r in feat_refs], axis=0)
        sum_ref[...] = mm(tile_columns(tile_ref, places, nd), feats)

    return call(
        body,
        [shape((rt, width), F32)],
        [tile, *blocks],
        flops=2 * rt * len(places) * nd * width,
        after=after,
    )[0]


def forward_parts(begun, tile, places, blocks, nd, cs, after=()):
    width = blocks[0].shape[1]

    def body(*refs):
        sum_ref, tile_ref, feat_refs = refs[0], refs[1], refs[2 : 2 + len(blocks)]
        outs = refs[2 + len(blocks) :]
        feats = jnp.concatenate([r[...] for r in feat_refs], axis=0)
        parts = sum_ref[...] + mm(tile_columns(tile_ref, places, nd), feats)
        for k in range(cs):
            outs[k][...] = parts[k * nd : (k + 1) * nd].astype(outs[k].dtype)

    return call(
        body,
        [shape((nd, width), BF16 if k else F32) for k in range(cs)],
        [begun, tile, *blocks],
        flops=2 * tile.shape[0] * len(places) * nd * width,
        after=after,
    )


def activation(parts, inverse, own, own_feat, w_neigh, bias, cotangent):
    cs = len(parts)
    nd, hid = own.shape
    depth = own_feat.shape[1]
    xw = 2 * depth // cs

    def body(*refs):
        part_refs = refs[:cs]
        inv_ref, own_ref, feat_ref, w_ref, bias_ref, cot_ref = refs[cs : cs + 6]
        out_ref, sum_ref, *packs = refs[cs + 6 : -1]
        both = refs[-1]
        j = lax.axis_index("col")
        inv = inv_ref[pl.ds(pl.multiple_of(j * nd, nd), nd), :]
        total = sum(r[...].astype(F32) for r in part_refs)
        mean = (total * jnp.concatenate([inv] * (depth // LANES), axis=1)).astype(BF16)
        both[:, :depth] = feat_ref[...]
        both[:, depth:] = mean
        pre = own_ref[...].astype(F32) + mm(mean, w_ref[...]) + bias_ref[...]
        slope = jnp.where(pre > 0, 1.0, jnp.exp(jnp.minimum(pre, 0.0)))
        out_ref[...] = jnp.where(pre > 0, pre, slope - 1.0).astype(BF16)
        grad = cot_ref[...].astype(F32) * slope
        sum_ref[...] = jnp.broadcast_to(jnp.sum(grad, axis=0, keepdims=True), (8, hid))
        grad = grad.astype(BF16)
        for k in range(cs):
            packs[k][:, :hid] = grad
            target = j ^ k
            if xw % LANES == 0:
                start = pl.multiple_of(target * xw, LANES)
                packs[k][:, hid:] = both[:, pl.ds(start, xw)]
            else:
                for d in range(cs):

                    @pl.when(target == d)
                    def _():
                        packs[k][:, hid:] = both[:, d * xw : (d + 1) * xw]

    return call(
        body,
        [shape((nd, hid), BF16), shape((8, hid), F32)] + [shape((nd, hid + xw), BF16)] * cs,
        [*parts, inverse, own, own_feat, w_neigh, bias, cotangent],
        [pltpu.VMEM((nd, 2 * depth), BF16)],
        flops=2 * own_feat.size * hid,
    )


def split_pair(total):
    high = total.astype(BF16).astype(F32)
    return jnp.concatenate([high, total - high], axis=0)


def weight_parts(packs, sums, rs, xr, nc, after):
    cs = len(packs)
    hid = sums.shape[1]
    nd, xw = packs[0].shape[0], packs[0].shape[1] - hid
    half = rs // 2

    def body(*refs):
        pack_refs = refs[:cs]
        sum_ref, keep_ref, send_ref, acc = refs[cs:]
        x_all = jnp.concatenate([r[:, hid:] for r in pack_refs], axis=0)
        g_all = jnp.concatenate([r[:, :hid] for r in pack_refs], axis=0)
        acc[...] = mm(x_all, g_all, 0, 0)
        i = lax.axis_index("row")
        z, c = i // 2, lax.rem(i, 2)
        for k in range(half):
            for core, ref in ((c, keep_ref), (1 - c, send_ref)):
                q = 2 * (z ^ k) + core
                row = pl.multiple_of((q // nc) * xr, xr)
                col = pl.multiple_of(lax.rem(q, nc) * LANES, LANES)
                ref[k, :xr, :] = acc[pl.ds(row, xr), pl.ds(col, LANES)].astype(ref.dtype)
                ref[k, xr:, :] = split_pair(sum_ref[:, pl.ds(col, LANES)]).astype(ref.dtype)

    dims = (half, xr + EXTRA, LANES)
    return call(
        body,
        [shape(dims, F32), shape(dims, BF16)],
        [*packs, sums],
        [pltpu.VMEM((xw, hid), F32)],
        flops=2 * cs * nd * xw * hid,
        after=after,
    )


def scaled_parts(packs, first, inverse, turned_neigh, turned_self, cs, rs, after=()):
    count = len(packs)
    nd = packs[0].shape[0]
    hid, depth = turned_neigh.shape

    def body(neigh_ref, own_ref, inv_ref, *refs):
        pack_refs, scaled_ref, self_ref = refs[:count], refs[count], refs[count + 1]
        i, j = lax.axis_index("row"), lax.axis_index("col")
        grads = jnp.concatenate([r[:, :hid] for r in pack_refs], axis=0)
        product = mm(grads, neigh_ref[...])
        for r in range(count):
            start = pl.multiple_of((j ^ (first + r)) * nd, nd)
            inv = inv_ref[pl.ds(start, nd), :]
            inv = jnp.concatenate([inv] * (depth // LANES), axis=1)
            rows = slice(r * nd, (r + 1) * nd)
            scaled_ref[rows, :] = (product[rows] * inv).astype(BF16)

        @pl.when(i * cs // rs == j)
        def _():
            self_ref[...] = mm(grads, own_ref[...])

    return call(
        body,
        [shape((count * nd, depth), BF16), shape((count * nd, depth), F32)],
        [turned_neigh, turned_self, inverse, *packs],
        flops=4 * count * nd * hid * depth,
        after=after,
    )


def halving_order(count):
    order = [0]
    step = count // 2
    while step:
        order = order + [d + step for d in order]
        step //= 2
    return order


def back_parts(turned, scaled, self_parts, nd, cs, rs, after):
    depth = scaled[0].shape[1]
    half = rs // 2
    count = len(scaled)
    each = cs // count

    def body(tile_ref, *refs):
        scaled_refs, self_refs = refs[:count], refs[count : 2 * count]
        keep_ref, send_ref, acc = refs[2 * count :]
        i, j = lax.axis_index("row"), lax.axis_index("col")
        z, c = i // 2, lax.rem(i, 2)
        acc[...] = mm(tile_ref[...], jnp.concatenate([r[...] for r in scaled_refs], axis=0))

        @pl.when(i * cs // rs == j)
        def _():
            for r in range(cs):
                q = i * cs - j * rs + (j ^ r)
                place = ((z ^ (q // 2)) + half * (lax.rem(q, 2) ^ c)) * nd
                rows = slice(r % each * nd, (r % each + 1) * nd)
                acc[pl.ds(pl.multiple_of(place, nd), nd), :] += self_refs[r // each][rows]

        for ref, base in ((send_ref, half), (keep_ref, 0)):
            for k, distance in enumerate(halving_order(half)):
                place = (base + distance) * nd
                ref[k] = acc[place : place + nd, :].astype(ref.dtype)

    dims = (half, nd, depth)
    return call(
        body,
        [shape(dims, F32), shape(dims, BF16)],
        [turned, *scaled, *self_parts],
        [pltpu.VMEM((rs * nd, depth), F32)],
        flops=2 * turned.size * depth,
        after=after,
    )


def fold(keep, came, after=()):
    count, rows, width = keep.shape
    half = count // 2

    def body(keep_ref, came_ref, *outs):
        total = keep_ref[...] + came_ref[...].astype(F32)
        if count == 1:
            outs[0][...] = total[0].astype(BF16)
        else:
            outs[0][...] = total[:half]
            outs[1][...] = total[half:].astype(BF16)

    if count == 1:
        return call(body, [shape((rows, width), BF16)], [keep, came], after=after)[0]
    dims = (half, rows, width)
    return call(body, [shape(dims, F32), shape(dims, BF16)], [keep, came], after=after)


def pair_sum(keep, came):
    half, rows, width = keep.shape
    main = rows - EXTRA

    def body(keep_ref, came_ref, *outs):
        for k in range(half):
            total = keep_ref[k] + came_ref[k].astype(F32)
            dtype = outs[k].dtype
            outs[k][:main, :] = total[:main].astype(dtype)
            merged = total[main : main + 8] + total[main + 8 :]
            outs[k][main:, :] = split_pair(merged).astype(dtype)

    return call(
        body,
        [shape((rows, width), BF16 if k else F32) for k in range(half)],
        [keep, came],
    )


def last_sum(parts):
    rows, width = parts[0].shape
    main = rows - EXTRA

    def body(*refs):
        out_ref = refs[-1]
        total = refs[0][...]
        for ref in refs[1:-1]:
            total = total + ref[...].astype(F32)
        out_ref[:main, :] = total[:main].astype(BF16)
        merged = total[main : main + 8] + total[main + 8 :]
        out_ref[main:, :] = split_pair(merged).astype(BF16)

    return call(body, [shape((rows, width), BF16)], parts)[0]


def assemble(pieces, begun, depth, hid, xr, nc, cs, factors, after):
    xw = 2 * depth // cs
    side = cs // 2
    copies = sum(len(where) for _, where, _ in pieces)
    arrays = [array for array, _, _ in pieces]
    inputs = arrays + list(begun)
    weight = shape((depth, hid), F32)

    def body(*refs):
        piece_refs = refs[: len(pieces)]
        self_ref, neigh_ref, bias_ref, staged, sems = refs[-5:]
        i, j = lax.axis_index("row"), lax.axis_index("col")
        z, c = i // 2, lax.rem(i, 2)
        if begun:
            bias_ref[...] = refs[len(inputs) - 1][...]
        else:
            bias_ref[...] = jnp.zeros_like(bias_ref)
        waits = []
        at = 0
        for ref, (_, where, mine) in zip(piece_refs, pieces):
            for t, (distance, column) in enumerate(where):
                owner = j ^ column
                first = owner < side
                q = 2 * (z ^ distance) + (c if mine else 1 - c)
                col = pl.multiple_of(lax.rem(q, nc) * LANES, LANES)
                turn = q // nc
                row = pl.multiple_of(lax.rem(owner, side) * xw + turn * xr, xr)
                scale = jnp.where(first, factors[0], factors[1])
                staged[at] = ref[t, :xr, :].astype(F32) * scale
                for target, here in ((self_ref, first), (neigh_ref, jnp.logical_not(first))):
                    copy = pltpu.make_async_copy(
                        staged.at[at],
                        target.at[pl.ds(row, xr), pl.ds(col, LANES)],
                        sems.at[at],
                    )
                    pl.when(here)(copy.start)
                    waits.append((here, copy))

                @pl.when(turn == 0)
                def _():
                    total = ref[t, xr:, :].astype(F32)
                    total = (total[:1] + total[8:9]) * factors[0]
                    bias_ref[:, pl.ds(col, LANES)] += total

                at += 1
        for here, copy in waits:
            pl.when(here)(copy.wait)

    def run(*refs):
        body(*refs[: len(inputs)], *refs[len(inputs) + len(after) :])

    somewhere = pl.BlockSpec(memory_space=pl.ANY)
    moved = 2 * copies * xr * LANES * 6
    return pl.pallas_call(
        run,
        out_shape=[weight, weight, shape((1, hid), F32)],
        in_specs=[VMEM] * len(arrays)
        + ([somewhere, somewhere, VMEM] if begun else [])
        + [somewhere] * len(after),
        out_specs=[somewhere, somewhere, VMEM],
        scratch_shapes=[
            pltpu.VMEM((copies, xr, LANES), F32),
            pltpu.SemaphoreType.DMA((copies,)),
        ],
        input_output_aliases={len(arrays): 0, len(arrays) + 1: 1} if begun else {},
        compiler_params=PARAMS,
        cost_estimate=pl.CostEstimate(flops=0, bytes_accessed=moved, transcendentals=0),
    )(*inputs, *after)


def local(
    features, w_neigh, w_self, bias, cotangent, block_rows, block_cols, block_vals, block_count
):
    rs = lax.axis_size("row")
    cs = lax.axis_size("col")
    nd, depth = features.shape
    hid = w_self.shape[1]
    rt = nd * cs
    half = rs // 2
    xw = 2 * depth // cs
    nc = min(rs, hid // LANES)
    nr = rs // nc
    xr = xw // nr

    def along_col(x, k):
        return lax.ppermute(x, "col", [(s, s ^ k) for s in range(cs)])

    def along_chips(x, k):
        return lax.ppermute(x, "row", [(s, s ^ (2 * k)) for s in range(rs)])

    def other_core(x):
        return lax.ppermute(x, "row", [(s, s ^ 1) for s in range(rs)])

    def gather_chips(x):
        found = {0: x}
        step = half // 2
        while step:
            found.update({d + step: along_chips(found[d], step) for d in list(found)})
            step //= 2
        return [found[d] for d in range(half)]

    if rs == 2 * cs:

        def send_own(block, t):
            pairs = []
            for z in range(half):
                for core in range(2):
                    q = 2 * (z ^ t) + core
                    source = (2 * z + core) * cs + z
                    pairs.append((source, (2 * z + q // cs) * cs + q % cs))
            return lax.ppermute(block, ("row", "col"), pairs)

    else:
        swap = [((b % rs) * cs + b // rs, b) for b in range(rs * cs)]

        def send_own(block, t):
            return lax.ppermute(block, ("row", "col"), swap if t == 0 else [])

    near = along_chips(features, 1)
    mine_first = {0: features, 1: near}
    step = half // 2
    while step > 1:
        evens = [d for d in mine_first if d % 2 == 0]
        mine_first.update({d + step: along_chips(mine_first[d], step) for d in evens})
        step //= 2
    theirs_first = {0: other_core(features), 1: other_core(near)}
    own_feats = {0: send_own(features, 0)}
    turned_neigh, turned_self = turn([w_neigh, w_self], [theirs_first[0]])
    tile, turned = densify(
        block_rows.reshape(-1),
        block_cols.reshape(-1),
        block_count.reshape(-1),
        block_vals[0, 0],
        nd,
        rs,
        cs,
        [near, turned_neigh, own_feats[0]],
    )
    mine_first.update(
        {d: follow(x, [tile, theirs_first[1]]) for d, x in mine_first.items() if d > 1}
    )
    mine_last = {d + 1: along_chips(x, 1) for d, x in mine_first.items() if d > 1}
    theirs_first.update({d: other_core(x) for d, x in mine_first.items() if d > 1})
    theirs_last = {d: other_core(x) for d, x in mine_last.items()}
    own_feats.update({d: send_own(x, d) for d, x in mine_first.items() if d})

    def placed(mine, theirs):
        places = list(mine) + [half + d for d in theirs]
        return places, [*mine.values(), *theirs.values()]

    begun = forward_first(
        tile, *placed(mine_first, theirs_first), nd, [own_feats[0], own_feats[1]]
    )
    evens = [x for d, x in own_feats.items() if d and d % 2 == 0]
    parts = forward_parts(begun, tile, *placed(mine_last, theirs_last), nd, cs, evens)
    own_feats.update({d: send_own(follow(x, parts[:1]), d) for d, x in mine_last.items()})
    own_feat = sum(list(own_feats.values())[1:], own_feats[0])
    mass = row_sums(tile, nd, cs, parts[1:2])
    degree = mass
    for k in range(1, cs):
        degree = degree + along_col(mass, k)
    inverse = 1.0 / (degree[:1] + 1.0)
    inverse = jnp.broadcast_to(inverse[0][:, None], (rt, LANES))
    own = jnp.dot(own_feat, w_self, preferred_element_type=F32).astype(BF16)

    parts = [parts[0]] + [along_col(parts[k], k) for k in range(1, cs)]
    output, sums, *packs = activation(
        parts, inverse, own, own_feat, w_neigh, bias[None, :], cotangent
    )
    packs = [packs[0]] + [along_col(packs[k], k) for k in range(1, cs)]

    mid = cs // 2
    scaled_args = (inverse, turned_neigh, turned_self, cs, rs)
    early = scaled_parts(packs[:mid], 0, *scaled_args)
    keep, send = weight_parts(packs, sums, rs, xr, nc, early[:1])
    came = other_core(send)
    late = scaled_parts(packs[mid:], mid, *scaled_args, [keep])
    scaled, self_parts = zip(early, late)
    chunks = pair_sum(keep, came)
    back_after = [chunks[1]]
    chunks = [chunks[0]] + [along_chips(chunks[k], k) for k in range(1, half)]
    chunk = last_sum(chunks)
    line = gather_chips(chunk)

    keep, send = back_parts(turned, scaled, self_parts, nd, cs, rs, back_after)
    keep, send = fold(keep, other_core(send), [chunk])
    keep, send = fold(keep, along_chips(send, 1))
    line = stack(line, after=[send])
    step = 2
    while step < half:
        folded = fold(keep, along_chips(send, step))
        keep, send = folded if 2 * step < half else (folded, None)
        step *= 2
    grad_input = keep

    def at(where, k):
        return [(d, k) for d in where]

    distances = list(range(half))
    factor = 1.0 / math.sqrt(nd * rs * cs)
    sizes = (depth, hid, xr, nc, cs, (factor, 32.0 * factor))

    def both_cores(array, where):
        return [(array, where, True), (other_core(array), where, False)]

    if cs == 4:
        first, second = along_col(line, 1), along_col(line, 2)
        near = [line, first, second]
    else:
        near = [line] + [along_col(line, k) for k in range(1, cs - 1)]
    near = stack(near, joined=True, after=[grad_input])
    near_where = sum((at(distances, k) for k in range(cs - 1)), [])
    begun = assemble(both_cores(near, near_where), (), *sizes, ())
    if cs == 4:
        mid = half // 2
        rest = [along_col(first[:mid], 2), along_col(second[mid:], 1)]
    else:
        rest = [along_col(line, cs - 1)]
    rest = stack(rest, joined=True, after=begun[2:])
    pieces = both_cores(rest, at(distances, cs - 1))
    total_self, total_neigh, total_bias = assemble(pieces, begun, *sizes, ())
    return output, grad_input, total_self, total_neigh, total_bias.reshape(-1)


def solution(mesh):
    in_specs = (
        P(("col", "row"), None),
        P(),
        P(),
        P(),
        P(("row", "col"), None),
        P("row", "col", None),
        P("row", "col", None),
        P("row", "col", None, None, None),
        P("row", "col"),
    )
    out_specs = (P(("row", "col"), None), P(("col", "row"), None), P(), P(), P())
    return jax.shard_map(local, mesh=mesh, in_specs=in_specs, out_specs=out_specs, check_vma=False)
```

```python
import math

import jax
import jax.numpy as jnp
from jax import lax
from jax.experimental import pallas as pl
from jax.experimental.pallas import tpu as pltpu
from jax.sharding import PartitionSpec as P

F32 = jnp.float32
BF16 = jnp.bfloat16
LANES = 128
EXTRA = 16
VMEM = pl.BlockSpec(memory_space=pltpu.VMEM)
SMEM = pl.BlockSpec(memory_space=pltpu.SMEM)
PARAMS = pltpu.CompilerParams(vmem_limit_bytes=48 * 1024 * 1024)


def call(body, outs, args, scratch=(), smem=0, flops=0, after=()):
    count = len(args)
    moved = sum(math.prod(o.shape) * o.dtype.itemsize for o in outs)
    moved += sum(a.size * a.dtype.itemsize for a in args)

    def run(*refs):
        body(*refs[:count], *refs[count + len(after) :])

    return pl.pallas_call(
        run,
        out_shape=outs,
        in_specs=[SMEM] * smem
        + [VMEM] * (count - smem)
        + [pl.BlockSpec(memory_space=pl.ANY)] * len(after),
        out_specs=[VMEM] * len(outs),
        scratch_shapes=list(scratch),
        compiler_params=PARAMS,
        cost_estimate=pl.CostEstimate(flops=flops, bytes_accessed=moved, transcendentals=0),
    )(*args, *after)


def shape(dims, dtype):
    return jax.ShapeDtypeStruct(tuple(dims), dtype)


def mm(a, b, ca=1, cb=0):
    return lax.dot_general(a, b, (((ca,), (cb,)), ((), ())), preferred_element_type=F32)


def follow(x, after):
    def body(x_ref, out_ref):
        out_ref[...] = x_ref[...]

    return call(body, [shape(x.shape, x.dtype)], [x], after=after)[0]


def turn(weights, after):
    def body(*refs):
        for ref, out_ref in zip(refs, refs[len(weights) :]):
            out_ref[...] = ref[...].T

    return call(body, [shape(w.shape[::-1], w.dtype) for w in weights], weights, after=after)


def stack(parts, joined=False, after=()):
    count = parts[0].shape[0] if joined else 1

    def body(*refs):
        for k, ref in enumerate(refs[:-1]):
            if joined:
                refs[-1][k * count : (k + 1) * count] = ref[...]
            else:
                refs[-1][k] = ref[...]

    dims = parts[0].shape[1:] if joined else parts[0].shape
    out = shape((len(parts) * count, *dims), parts[0].dtype)
    return call(body, [out], parts, after=after)[0]


def densify(rows, cols, count, values, nd, rs, cs, after):
    rt, ct, half = nd * cs, nd * rs, rs // 2

    def body(rows_ref, cols_ref, count_ref, values_ref, tile_ref, turned_ref, acc):
        i, j = lax.axis_index("row"), lax.axis_index("col")
        z, c = i // 2, lax.rem(i, 2)
        acc[...] = jnp.zeros_like(acc)

        def add(s, carry):
            col = cols_ref[s]
            row = rows_ref[s] ^ j
            col = (z ^ (col // 2)) + half * (lax.rem(col, 2) ^ c)
            r = pl.multiple_of(row * nd, nd)
            c0 = pl.multiple_of(col * nd, nd)
            acc[pl.ds(r, nd), pl.ds(c0, nd)] += values_ref[s].astype(F32)
            return carry

        lax.fori_loop(0, count_ref[0], add, 0)
        tile_ref[...] = acc[...].astype(BF16)
        for k in range(rs):
            cut = acc[:, k * nd : (k + 1) * nd]
            turned_ref[k * nd : (k + 1) * nd, :] = cut.T.astype(BF16)

    return call(
        body,
        [shape((rt, ct), BF16), shape((ct, rt), BF16)],
        [rows, cols, count, values],
        [pltpu.VMEM((rt, ct), F32)],
        smem=3,
        flops=rt * ct,
        after=after,
    )


def tile_columns(tile_ref, places, nd):
    return jnp.concatenate([tile_ref[:, p * nd : (p + 1) * nd] for p in places], axis=1)


def row_sums(tile, nd, cs, after):
    rt, ct = tile.shape

    def body(tile_ref, mass_ref):
        j = lax.axis_index("col")
        ones = jnp.ones((8, ct), BF16)
        for k in range(cs):
            place = pl.multiple_of((j ^ k) * nd, nd)
            mass_ref[:, pl.ds(place, nd)] = mm(ones, tile_ref[k * nd : (k + 1) * nd, :], 1, 1)

    return call(body, [shape((8, rt), F32)], [tile], flops=16 * tile.size, after=after)[0]


def forward_first(tile, places, blocks, nd, after):
    rt = tile.shape[0]
    width = blocks[0].shape[1]

    def body(*refs):
        tile_ref, feat_refs = refs[0], refs[1 : 1 + len(blocks)]
        sum_ref = refs[1 + len(blocks)]
        feats = jnp.concatenate([r[...] for r in feat_refs], axis=0)
        sum_ref[...] = mm(tile_columns(tile_ref, places, nd), feats)

    return call(
        body,
        [shape((rt, width), F32)],
        [tile, *blocks],
        flops=2 * rt * len(places) * nd * width,
        after=after,
    )[0]


def forward_parts(begun, tile, places, blocks, nd, cs, after=()):
    width = blocks[0].shape[1]

    def body(*refs):
        sum_ref, tile_ref, feat_refs = refs[0], refs[1], refs[2 : 2 + len(blocks)]
        outs = refs[2 + len(blocks) :]
        feats = jnp.concatenate([r[...] for r in feat_refs], axis=0)
        parts = sum_ref[...] + mm(tile_columns(tile_ref, places, nd), feats)
        for k in range(cs):
            outs[k][...] = parts[k * nd : (k + 1) * nd].astype(outs[k].dtype)

    return call(
        body,
        [shape((nd, width), BF16 if k else F32) for k in range(cs)],
        [begun, tile, *blocks],
        flops=2 * tile.shape[0] * len(places) * nd * width,
        after=after,
    )


def activation(parts, own_feats, inverse, w_neigh, w_self, bias, cotangent):
    cs, count = len(parts), len(own_feats)
    nd, hid = cotangent.shape
    depth = own_feats[0].shape[1]
    xw = 2 * depth // cs

    def body(*refs):
        part_refs, feat_refs = refs[:cs], refs[cs : cs + count]
        inv_ref, wn_ref, ws_ref, bias_ref, cot_ref = refs[cs + count : cs + count + 5]
        out_ref, sum_ref, *packs = refs[cs + count + 5 : -1]
        both = refs[-1]
        j = lax.axis_index("col")
        inv = inv_ref[pl.ds(pl.multiple_of(j * nd, nd), nd), :]
        feats = sum(r[...].astype(F32) for r in feat_refs).astype(BF16)
        own = mm(feats, ws_ref[...]).astype(BF16).astype(F32)
        total = sum(r[...].astype(F32) for r in part_refs)
        mean = (total * jnp.concatenate([inv] * (depth // LANES), axis=1)).astype(BF16)
        both[:, :depth] = feats
        both[:, depth:] = mean
        pre = own + mm(mean, wn_ref[...]) + bias_ref[...]
        slope = jnp.where(pre > 0, 1.0, jnp.exp(jnp.minimum(pre, 0.0)))
        out_ref[...] = jnp.where(pre > 0, pre, slope - 1.0).astype(BF16)
        grad = cot_ref[...].astype(F32) * slope
        sum_ref[...] = jnp.broadcast_to(jnp.sum(grad, axis=0, keepdims=True), (8, hid))
        grad = grad.astype(BF16)
        for k in range(cs):
            packs[k][:, :hid] = grad
            target = j ^ k
            if xw % LANES == 0:
                start = pl.multiple_of(target * xw, LANES)
                packs[k][:, hid:] = both[:, pl.ds(start, xw)]
            else:
                for d in range(cs):

                    @pl.when(target == d)
                    def _():
                        packs[k][:, hid:] = both[:, d * xw : (d + 1) * xw]

    return call(
        body,
        [shape((nd, hid), BF16), shape((8, hid), F32)] + [shape((nd, hid + xw), BF16)] * cs,
        [*parts, *own_feats, inverse, w_neigh, w_self, bias, cotangent],
        [pltpu.VMEM((nd, 2 * depth), BF16)],
        flops=4 * nd * depth * hid,
    )


def split_pair(total):
    high = total.astype(BF16).astype(F32)
    return jnp.concatenate([high, total - high], axis=0)


def weight_parts(packs, sums, rs, xr, nc, after):
    cs = len(packs)
    hid = sums.shape[1]
    nd, xw = packs[0].shape[0], packs[0].shape[1] - hid
    half = rs // 2

    def body(*refs):
        pack_refs = refs[:cs]
        sum_ref, keep_ref, send_ref, acc = refs[cs:]
        x_all = jnp.concatenate([r[:, hid:] for r in pack_refs], axis=0)
        g_all = jnp.concatenate([r[:, :hid] for r in pack_refs], axis=0)
        acc[...] = mm(x_all, g_all, 0, 0)
        i = lax.axis_index("row")
        z, c = i // 2, lax.rem(i, 2)
        for k in range(half):
            for core, ref in ((c, keep_ref), (1 - c, send_ref)):
                q = 2 * (z ^ k) + core
                row = pl.multiple_of((q // nc) * xr, xr)
                col = pl.multiple_of(lax.rem(q, nc) * LANES, LANES)
                ref[k, :xr, :] = acc[pl.ds(row, xr), pl.ds(col, LANES)].astype(ref.dtype)
                ref[k, xr:, :] = split_pair(sum_ref[:, pl.ds(col, LANES)]).astype(ref.dtype)

    dims = (half, xr + EXTRA, LANES)
    return call(
        body,
        [shape(dims, F32), shape(dims, BF16)],
        [*packs, sums],
        [pltpu.VMEM((xw, hid), F32)],
        flops=2 * cs * nd * xw * hid,
        after=after,
    )


def scaled_parts(packs, first, inverse, turned_neigh, turned_self, cs, rs, after=()):
    count = len(packs)
    nd = packs[0].shape[0]
    hid, depth = turned_neigh.shape

    def body(neigh_ref, own_ref, inv_ref, *refs):
        pack_refs, scaled_ref, self_ref = refs[:count], refs[count], refs[count + 1]
        i, j = lax.axis_index("row"), lax.axis_index("col")
        grads = jnp.concatenate([r[:, :hid] for r in pack_refs], axis=0)
        product = mm(grads, neigh_ref[...])
        for r in range(count):
            start = pl.multiple_of((j ^ (first + r)) * nd, nd)
            inv = inv_ref[pl.ds(start, nd), :]
            inv = jnp.concatenate([inv] * (depth // LANES), axis=1)
            rows = slice(r * nd, (r + 1) * nd)
            scaled_ref[rows, :] = (product[rows] * inv).astype(BF16)

        @pl.when(i * cs // rs == j)
        def _():
            self_ref[...] = mm(grads, own_ref[...])

    return call(
        body,
        [shape((count * nd, depth), BF16), shape((count * nd, depth), F32)],
        [turned_neigh, turned_self, inverse, *packs],
        flops=4 * count * nd * hid * depth,
        after=after,
    )


def halving_order(count):
    order = [0]
    step = count // 2
    while step:
        order = order + [d + step for d in order]
        step //= 2
    return order


def back_parts(turned, scaled, self_parts, nd, cs, rs, after):
    depth = scaled[0].shape[1]
    half = rs // 2
    count = len(scaled)
    each = cs // count

    def body(tile_ref, *refs):
        scaled_refs, self_refs = refs[:count], refs[count : 2 * count]
        keep_ref, send_ref, acc = refs[2 * count :]
        i, j = lax.axis_index("row"), lax.axis_index("col")
        z, c = i // 2, lax.rem(i, 2)
        acc[...] = mm(tile_ref[...], jnp.concatenate([r[...] for r in scaled_refs], axis=0))

        @pl.when(i * cs // rs == j)
        def _():
            for r in range(cs):
                q = i * cs - j * rs + (j ^ r)
                place = ((z ^ (q // 2)) + half * (lax.rem(q, 2) ^ c)) * nd
                rows = slice(r % each * nd, (r % each + 1) * nd)
                acc[pl.ds(pl.multiple_of(place, nd), nd), :] += self_refs[r // each][rows]

        for ref, base in ((send_ref, half), (keep_ref, 0)):
            for k, distance in enumerate(halving_order(half)):
                place = (base + distance) * nd
                ref[k] = acc[place : place + nd, :].astype(ref.dtype)

    dims = (half, nd, depth)
    return call(
        body,
        [shape(dims, F32), shape(dims, BF16)],
        [turned, *scaled, *self_parts],
        [pltpu.VMEM((rs * nd, depth), F32)],
        flops=2 * turned.size * depth,
        after=after,
    )


def fold(keep, came, after=()):
    count, rows, width = keep.shape
    half = count // 2

    def body(keep_ref, came_ref, *outs):
        total = keep_ref[...] + came_ref[...].astype(F32)
        if count == 1:
            outs[0][...] = total[0].astype(BF16)
        else:
            outs[0][...] = total[:half]
            outs[1][...] = total[half:].astype(BF16)

    if count == 1:
        return call(body, [shape((rows, width), BF16)], [keep, came], after=after)[0]
    dims = (half, rows, width)
    return call(body, [shape(dims, F32), shape(dims, BF16)], [keep, came], after=after)


def pair_sum(keep, came):
    half, rows, width = keep.shape
    main = rows - EXTRA

    def body(keep_ref, came_ref, *outs):
        for k in range(half):
            total = keep_ref[k] + came_ref[k].astype(F32)
            dtype = outs[k].dtype
            outs[k][:main, :] = total[:main].astype(dtype)
            merged = total[main : main + 8] + total[main + 8 :]
            outs[k][main:, :] = split_pair(merged).astype(dtype)

    return call(
        body,
        [shape((rows, width), BF16 if k else F32) for k in range(half)],
        [keep, came],
    )


def last_sum(parts):
    rows, width = parts[0].shape
    main = rows - EXTRA

    def body(*refs):
        out_ref = refs[-1]
        total = refs[0][...]
        for ref in refs[1:-1]:
            total = total + ref[...].astype(F32)
        out_ref[:main, :] = total[:main].astype(BF16)
        merged = total[main : main + 8] + total[main + 8 :]
        out_ref[main:, :] = split_pair(merged).astype(BF16)

    return call(body, [shape((rows, width), BF16)], parts)[0]


def assemble(pieces, begun, depth, hid, xr, nc, cs, factors, after):
    xw = 2 * depth // cs
    side = cs // 2
    copies = sum(len(where) for _, where, _ in pieces)
    arrays = [array for array, _, _ in pieces]
    inputs = arrays + list(begun)
    weight = shape((depth, hid), F32)

    def body(*refs):
        piece_refs = refs[: len(pieces)]
        self_ref, neigh_ref, bias_ref, staged, sems = refs[-5:]
        i, j = lax.axis_index("row"), lax.axis_index("col")
        z, c = i // 2, lax.rem(i, 2)
        if begun:
            bias_ref[...] = refs[len(inputs) - 1][...]
        else:
            bias_ref[...] = jnp.zeros_like(bias_ref)
        waits = []
        at = 0
        for ref, (_, where, mine) in zip(piece_refs, pieces):
            for t, (distance, column) in enumerate(where):
                owner = j ^ column
                first = owner < side
                q = 2 * (z ^ distance) + (c if mine else 1 - c)
                col = pl.multiple_of(lax.rem(q, nc) * LANES, LANES)
                turn = q // nc
                row = pl.multiple_of(lax.rem(owner, side) * xw + turn * xr, xr)
                scale = jnp.where(first, factors[0], factors[1])
                staged[at] = ref[t, :xr, :].astype(F32) * scale
                for target, here in ((self_ref, first), (neigh_ref, jnp.logical_not(first))):
                    copy = pltpu.make_async_copy(
                        staged.at[at],
                        target.at[pl.ds(row, xr), pl.ds(col, LANES)],
                        sems.at[at],
                    )
                    pl.when(here)(copy.start)
                    waits.append((here, copy))

                @pl.when(turn == 0)
                def _():
                    total = ref[t, xr:, :].astype(F32)
                    total = (total[:1] + total[8:9]) * factors[0]
                    bias_ref[:, pl.ds(col, LANES)] += total

                at += 1
        for here, copy in waits:
            pl.when(here)(copy.wait)

    def run(*refs):
        body(*refs[: len(inputs)], *refs[len(inputs) + len(after) :])

    somewhere = pl.BlockSpec(memory_space=pl.ANY)
    moved = 2 * copies * xr * LANES * 6
    return pl.pallas_call(
        run,
        out_shape=[weight, weight, shape((1, hid), F32)],
        in_specs=[VMEM] * len(arrays)
        + ([somewhere, somewhere, VMEM] if begun else [])
        + [somewhere] * len(after),
        out_specs=[somewhere, somewhere, VMEM],
        scratch_shapes=[
            pltpu.VMEM((copies, xr, LANES), F32),
            pltpu.SemaphoreType.DMA((copies,)),
        ],
        input_output_aliases={len(arrays): 0, len(arrays) + 1: 1} if begun else {},
        compiler_params=PARAMS,
        cost_estimate=pl.CostEstimate(flops=0, bytes_accessed=moved, transcendentals=0),
    )(*inputs, *after)


def local(
    features, w_neigh, w_self, bias, cotangent, block_rows, block_cols, block_vals, block_count
):
    rs = lax.axis_size("row")
    cs = lax.axis_size("col")
    nd, depth = features.shape
    hid = w_self.shape[1]
    rt = nd * cs
    half = rs // 2
    xw = 2 * depth // cs
    nc = min(rs, hid // LANES)
    nr = rs // nc
    xr = xw // nr

    def along_col(x, k):
        return lax.ppermute(x, "col", [(s, s ^ k) for s in range(cs)])

    def along_chips(x, k):
        return lax.ppermute(x, "row", [(s, s ^ (2 * k)) for s in range(rs)])

    def other_core(x):
        return lax.ppermute(x, "row", [(s, s ^ 1) for s in range(rs)])

    def gather_chips(x):
        return [x] + [along_chips(x, k) for k in range(1, half)]

    if rs == 2 * cs:

        def send_own(block, t):
            pairs = []
            for z in range(half):
                for core in range(2):
                    q = 2 * (z ^ t) + core
                    source = (2 * z + core) * cs + z
                    pairs.append((source, (2 * z + q // cs) * cs + q % cs))
            return lax.ppermute(block, ("row", "col"), pairs)

    else:
        swap = [((b % rs) * cs + b // rs, b) for b in range(rs * cs)]

        def send_own(block, t):
            return lax.ppermute(block, ("row", "col"), swap if t == 0 else [])

    blocks = gather_chips(features)
    theirs = [other_core(x) for x in blocks]
    own_feats = [send_own(blocks[0], 0)]
    turned_neigh, turned_self = turn([w_neigh, w_self], [theirs[0], own_feats[0]])
    tile, turned = densify(
        block_rows.reshape(-1),
        block_cols.reshape(-1),
        block_count.reshape(-1),
        block_vals[0, 0],
        nd,
        rs,
        cs,
        [turned_neigh],
    )
    mass = row_sums(tile, nd, cs, ())
    degree = mass
    for k in range(1, cs):
        degree = degree + along_col(mass, k)
    inverse = 1.0 / (degree[:1] + 1.0)

    def placed(distances):
        places = distances + [half + d for d in distances]
        return places, [blocks[d] for d in distances] + [theirs[d] for d in distances]

    begun = forward_first(tile, *placed([0, 1]), nd, [inverse])
    parts = forward_parts(begun, tile, *placed(list(range(2, half))), nd, cs)
    own_feats += [send_own(blocks[d], d) for d in range(1, half)]
    inverse = jnp.broadcast_to(inverse[0][:, None], (rt, LANES))
    parts = [parts[0]] + [along_col(parts[k], k) for k in range(1, cs)]
    output, sums, *packs = activation(
        parts, own_feats, inverse, w_neigh, w_self, bias[None, :], cotangent
    )
    packs = [packs[0]] + [along_col(packs[k], k) for k in range(1, cs)]

    mid = cs // 2
    scaled_args = (inverse, turned_neigh, turned_self, cs, rs)
    early = scaled_parts(packs[:mid], 0, *scaled_args)
    keep, send = weight_parts(packs, sums, rs, xr, nc, early[:1])
    came = other_core(send)
    late = scaled_parts(packs[mid:], mid, *scaled_args, [keep])
    scaled, self_parts = zip(early, late)
    chunks = pair_sum(keep, came)
    chunks = [chunks[0]] + [along_chips(chunks[k], k) for k in range(1, half)]
    line = gather_chips(last_sum(chunks))

    keep, send = back_parts(turned, scaled, self_parts, nd, cs, rs, chunks[1:])
    keep, send = fold(keep, other_core(send), line[1:])
    line = stack(line, after=[send])
    keep, send = fold(keep, along_chips(send, 1))
    folded = [keep]
    step = 2
    while step < half:
        last = fold(keep, along_chips(send, step))
        keep, send = last if 2 * step < half else (last, None)
        step *= 2
    grad_input = keep

    def at(where, k):
        return [(d, k) for d in where]

    distances = list(range(half))
    factor = 1.0 / math.sqrt(nd * rs * cs)
    sizes = (depth, hid, xr, nc, cs, (factor, 32.0 * factor))

    def both_cores(array, where):
        return [(array, where, True), (other_core(array), where, False)]

    if cs == 4:
        first, second = along_col(line, 1), along_col(line, 2)
        near = [line, first, second]
    else:
        near = [line] + [along_col(line, k) for k in range(1, cs - 1)]
    near = stack(near, joined=True, after=folded)
    near_where = sum((at(distances, k) for k in range(cs - 1)), [])
    begun = assemble(both_cores(near, near_where), (), *sizes, ())
    if cs == 4:
        mid = half // 2
        rest = [along_col(first[:mid], 2), along_col(second[mid:], 1)]
    else:
        rest = [along_col(line, cs - 1)]
    rest = stack(rest, joined=True, after=[begun[2], grad_input])
    pieces = both_cores(rest, at(distances, cs - 1))
    total_self, total_neigh, total_bias = assemble(pieces, begun, *sizes, ())
    return output, grad_input, total_self, total_neigh, total_bias.reshape(-1)


def solution(mesh):
    in_specs = (
        P(("col", "row"), None),
        P(),
        P(),
        P(),
        P(("row", "col"), None),
        P("row", "col", None),
        P("row", "col", None),
        P("row", "col", None, None, None),
        P("row", "col"),
    )
    out_specs = (P(("row", "col"), None), P(("col", "row"), None), P(), P(), P())
    return jax.shard_map(local, mesh=mesh, in_specs=in_specs, out_specs=out_specs, check_vma=False)
```

```python
import math

import jax
import jax.numpy as jnp
from jax import lax
from jax.experimental import pallas as pl
from jax.experimental.pallas import tpu as pltpu
from jax.sharding import PartitionSpec as P

F32 = jnp.float32
BF16 = jnp.bfloat16
LANES = 128
EXTRA = 16
VMEM = pl.BlockSpec(memory_space=pltpu.VMEM)
SMEM = pl.BlockSpec(memory_space=pltpu.SMEM)
PARAMS = pltpu.CompilerParams(vmem_limit_bytes=48 * 1024 * 1024)


def call(body, outs, args, scratch=(), smem=0, flops=0, after=()):
    count = len(args)
    moved = sum(math.prod(o.shape) * o.dtype.itemsize for o in outs)
    moved += sum(a.size * a.dtype.itemsize for a in args)

    def run(*refs):
        body(*refs[:count], *refs[count + len(after) :])

    return pl.pallas_call(
        run,
        out_shape=outs,
        in_specs=[SMEM] * smem
        + [VMEM] * (count - smem)
        + [pl.BlockSpec(memory_space=pl.ANY)] * len(after),
        out_specs=[VMEM] * len(outs),
        scratch_shapes=list(scratch),
        compiler_params=PARAMS,
        cost_estimate=pl.CostEstimate(flops=flops, bytes_accessed=moved, transcendentals=0),
    )(*args, *after)


def shape(dims, dtype):
    return jax.ShapeDtypeStruct(tuple(dims), dtype)


def mm(a, b, ca=1, cb=0):
    return lax.dot_general(a, b, (((ca,), (cb,)), ((), ())), preferred_element_type=F32)


def follow(x, after):
    def body(x_ref, out_ref):
        out_ref[...] = x_ref[...]

    return call(body, [shape(x.shape, x.dtype)], [x], after=after)[0]


def turn(weights, after):
    def body(*refs):
        for ref, out_ref in zip(refs, refs[len(weights) :]):
            out_ref[...] = ref[...].T

    return call(body, [shape(w.shape[::-1], w.dtype) for w in weights], weights, after=after)


def stack(parts, after):
    def body(*refs):
        for k, ref in enumerate(refs[:-1]):
            refs[-1][k] = ref[...]

    out = shape((len(parts), *parts[0].shape), parts[0].dtype)
    return call(body, [out], parts, after=after)[0]


def densify(rows, cols, count, values, nd, rs, cs, after):
    rt, ct, half = nd * cs, nd * rs, rs // 2

    def body(rows_ref, cols_ref, count_ref, values_ref, tile_ref, turned_ref, acc):
        i = lax.axis_index("row")
        z, c = i // 2, lax.rem(i, 2)
        acc[...] = jnp.zeros_like(acc)

        def add(s, carry):
            col = cols_ref[s]
            row = rows_ref[s]
            col = (z ^ (col // 2)) + half * (lax.rem(col, 2) ^ c)
            r = pl.multiple_of(row * nd, nd)
            c0 = pl.multiple_of(col * nd, nd)
            acc[pl.ds(r, nd), pl.ds(c0, nd)] += values_ref[s].astype(F32)
            return carry

        lax.fori_loop(0, count_ref[0], add, 0)
        tile_ref[...] = acc[...].astype(BF16)
        for k in range(rs):
            cut = acc[:, k * nd : (k + 1) * nd]
            turned_ref[k * nd : (k + 1) * nd, :] = cut.T.astype(BF16)

    return call(
        body,
        [shape((rt, ct), BF16), shape((ct, rt), BF16)],
        [rows, cols, count, values],
        [pltpu.VMEM((rt, ct), F32)],
        smem=3,
        flops=rt * ct,
        after=after,
    )


def tile_columns(tile_ref, places, nd):
    return jnp.concatenate([tile_ref[:, p * nd : (p + 1) * nd] for p in places], axis=1)


def forward_first(tile, places, blocks, nd, after):
    rt, ct = tile.shape
    width = blocks[0].shape[1]

    def body(*refs):
        tile_ref, feat_refs = refs[0], refs[1 : 1 + len(blocks)]
        sum_ref, mass_ref = refs[1 + len(blocks) :]
        feats = jnp.concatenate([r[...] for r in feat_refs], axis=0)
        sum_ref[...] = mm(tile_columns(tile_ref, places, nd), feats)
        mass_ref[...] = mm(jnp.ones((8, ct), BF16), tile_ref[...], 1, 1)

    return call(
        body,
        [shape((rt, width), F32), shape((8, rt), F32)],
        [tile, *blocks],
        flops=2 * rt * len(places) * nd * width,
        after=after,
    )


def forward_parts(begun, tile, places, blocks, nd, cs, after):
    rt = tile.shape[0]
    width = blocks[0].shape[1]

    def body(*refs):
        sum_ref, tile_ref, feat_refs = refs[0], refs[1], refs[2 : 2 + len(blocks)]
        *outs, acc = refs[2 + len(blocks) :]
        j = lax.axis_index("col")
        feats = jnp.concatenate([r[...] for r in feat_refs], axis=0)
        acc[...] = sum_ref[...] + mm(tile_columns(tile_ref, places, nd), feats)
        for k in range(cs):
            start = pl.multiple_of((j ^ k) * nd, nd)
            outs[k][...] = acc[pl.ds(start, nd), :].astype(outs[k].dtype)

    return call(
        body,
        [shape((nd, width), BF16 if k else F32) for k in range(cs)],
        [begun, tile, *blocks],
        [pltpu.VMEM((rt, width), F32)],
        flops=2 * rt * len(places) * nd * width,
        after=after,
    )


def activation(parts, inverse, own, own_feat, w_neigh, bias, cotangent, after):
    cs = len(parts)
    nd, hid = own.shape
    depth = own_feat.shape[1]
    xw = 2 * depth // cs

    def body(*refs):
        part_refs = refs[:cs]
        inv_ref, own_ref, feat_ref, w_ref, bias_ref, cot_ref = refs[cs : cs + 6]
        out_ref, sum_ref, packs, both = refs[cs + 6 :]
        j = lax.axis_index("col")
        inv = inv_ref[pl.ds(pl.multiple_of(j * nd, nd), nd), :]
        total = sum(r[...].astype(F32) for r in part_refs)
        mean = (total * jnp.concatenate([inv] * (depth // LANES), axis=1)).astype(BF16)
        both[:, :depth] = feat_ref[...]
        both[:, depth:] = mean
        pre = own_ref[...].astype(F32) + mm(mean, w_ref[...]) + bias_ref[...]
        slope = jnp.where(pre > 0, 1.0, jnp.exp(jnp.minimum(pre, 0.0)))
        out_ref[...] = jnp.where(pre > 0, pre, slope - 1.0).astype(BF16)
        grad = cot_ref[...].astype(F32) * slope
        sum_ref[...] = jnp.broadcast_to(jnp.sum(grad, axis=0, keepdims=True), (8, hid))
        grad = grad.astype(BF16)
        for k in range(cs):
            packs[k, :, :hid] = grad
            packs[k, :, hid:] = both[:, k * xw : (k + 1) * xw]

    return call(
        body,
        [shape((nd, hid), BF16), shape((8, hid), F32), shape((cs, nd, hid + xw), BF16)],
        [*parts, inverse, own, own_feat, w_neigh, bias, cotangent],
        [pltpu.VMEM((nd, 2 * depth), BF16)],
        flops=2 * own_feat.size * hid,
        after=after,
    )


def split_pair(total):
    high = total.astype(BF16).astype(F32)
    return jnp.concatenate([high, total - high], axis=0)


def weight_parts(packs, sums, rs, xr, nc):
    cs, nd, width = packs.shape
    hid = sums.shape[1]
    xw = width - hid
    half = rs // 2

    def body(pack_ref, sum_ref, *refs):
        keep_ref, send_ref, acc = refs
        x_all = jnp.concatenate([pack_ref[k, :, hid:] for k in range(cs)], axis=0)
        g_all = jnp.concatenate([pack_ref[k, :, :hid] for k in range(cs)], axis=0)
        acc[...] = mm(x_all, g_all, 0, 0)
        c = lax.rem(lax.axis_index("row"), 2)
        for k in range(half):
            for core, ref in ((c, keep_ref), (1 - c, send_ref)):
                q = 2 * k + core
                row = pl.multiple_of((q // nc) * xr, xr)
                col = pl.multiple_of(lax.rem(q, nc) * LANES, LANES)
                ref[k, :xr, :] = acc[pl.ds(row, xr), pl.ds(col, LANES)].astype(ref.dtype)
                ref[k, xr:, :] = split_pair(sum_ref[:, pl.ds(col, LANES)]).astype(ref.dtype)

    dims = (half, xr + EXTRA, LANES)
    return call(
        body,
        [shape(dims, F32), shape(dims, BF16)],
        [packs, sums],
        [pltpu.VMEM((xw, hid), F32)],
        flops=2 * cs * nd * xw * hid,
    )


def scaled_parts(packs, inverse, turned_neigh, turned_self, rs, after):
    cs, nd, _ = packs.shape
    hid, depth = turned_neigh.shape

    def body(pack_ref, neigh_ref, own_ref, inv_ref, scaled_ref, self_ref):
        i, j = lax.axis_index("row"), lax.axis_index("col")
        grads = jnp.concatenate([pack_ref[k, :, :hid] for k in range(cs)], axis=0)
        inv = jnp.concatenate([inv_ref[...]] * (depth // LANES), axis=1)
        scaled_ref[...] = (mm(grads, neigh_ref[...]) * inv).astype(BF16)

        @pl.when(i * cs // rs == j)
        def _():
            self_ref[...] = mm(grads, own_ref[...])

    return call(
        body,
        [shape((cs * nd, depth), BF16), shape((cs * nd, depth), F32)],
        [packs, turned_neigh, turned_self, inverse],
        flops=4 * cs * nd * hid * depth,
        after=after,
    )


def halving_order(count):
    order = [0]
    step = count // 2
    while step:
        order = order + [d + step for d in order]
        step //= 2
    return order


def back_parts(turned, scaled, self_part, nd, cs, rs, after):
    depth = scaled.shape[1]
    half = rs // 2

    def body(tile_ref, scaled_ref, self_ref, keep_ref, send_ref, acc):
        i, j = lax.axis_index("row"), lax.axis_index("col")
        z, c = i // 2, lax.rem(i, 2)
        acc[...] = mm(tile_ref[...], scaled_ref[...])

        @pl.when(i * cs // rs == j)
        def _():
            for r in range(cs):
                q = i * cs - j * rs + r
                place = ((z ^ (q // 2)) + half * (lax.rem(q, 2) ^ c)) * nd
                acc[pl.ds(pl.multiple_of(place, nd), nd), :] += self_ref[r * nd : (r + 1) * nd]

        for ref, base in ((send_ref, half), (keep_ref, 0)):
            for k, distance in enumerate(halving_order(half)):
                place = (base + distance) * nd
                ref[k] = acc[place : place + nd, :].astype(ref.dtype)

    dims = (half, nd, depth)
    return call(
        body,
        [shape(dims, F32), shape(dims, BF16)],
        [turned, scaled, self_part],
        [pltpu.VMEM((rs * nd, depth), F32)],
        flops=2 * turned.size * depth,
        after=after,
    )


def fold(keep, came, after=()):
    count, rows, width = keep.shape
    half = count // 2

    def body(keep_ref, came_ref, *outs):
        total = keep_ref[...] + came_ref[...].astype(F32)
        if count == 1:
            outs[0][...] = total[0].astype(BF16)
        else:
            outs[0][...] = total[:half]
            outs[1][...] = total[half:].astype(BF16)

    if count == 1:
        return call(body, [shape((rows, width), BF16)], [keep, came], after=after)[0]
    dims = (half, rows, width)
    return call(body, [shape(dims, F32), shape(dims, BF16)], [keep, came], after=after)


def pair_sum(keep, came):
    half, rows, width = keep.shape
    main = rows - EXTRA

    def body(keep_ref, came_ref, out_ref):
        for k in range(half):
            total = keep_ref[k] + came_ref[k].astype(F32)
            out_ref[k, :main, :] = total[:main].astype(BF16)
            merged = total[main : main + 8] + total[main + 8 :]
            out_ref[k, main:, :] = split_pair(merged).astype(BF16)

    return call(body, [shape(keep.shape, BF16)], [keep, came])[0]


def last_sum(came):
    half, rows, width = came.shape
    main = rows - EXTRA

    def body(came_ref, out_ref):
        total = sum(came_ref[k].astype(F32) for k in range(half))
        out_ref[:main, :] = total[:main].astype(BF16)
        merged = total[main : main + 8] + total[main + 8 :]
        out_ref[main:, :] = split_pair(merged).astype(BF16)

    return call(body, [shape((rows, width), BF16)], [came])[0]


def assemble(pieces, mine, begun, depth, hid, xr, nc, cs, factors, after):
    xw = 2 * depth // cs
    side = cs // 2
    copies = sum(len(distances) for _, distances, _ in pieces)
    arrays = [array for array, _, _ in pieces]
    inputs = arrays + list(begun)
    weight = shape((depth, hid), F32)

    def body(*refs):
        piece_refs = refs[: len(pieces)]
        self_ref, neigh_ref, bias_ref, staged, sems = refs[-5:]
        i, j = lax.axis_index("row"), lax.axis_index("col")
        z, c = i // 2, lax.rem(i, 2)
        if begun:
            bias_ref[...] = refs[len(inputs) - 1][...]
        else:
            bias_ref[...] = jnp.zeros_like(bias_ref)
        waits = []
        at = 0
        for ref, (_, distances, column) in zip(piece_refs, pieces):
            owner = j ^ column
            first = owner < side
            for t, distance in enumerate(distances):
                q = 2 * (z ^ distance) + (c if mine else 1 - c)
                col = pl.multiple_of(lax.rem(q, nc) * LANES, LANES)
                turn = q // nc
                row = pl.multiple_of(lax.rem(owner, side) * xw + turn * xr, xr)
                scale = jnp.where(first, factors[0], factors[1])
                staged[at] = ref[t, :xr, :].astype(F32) * scale
                for target, here in ((self_ref, first), (neigh_ref, jnp.logical_not(first))):
                    copy = pltpu.make_async_copy(
                        staged.at[at],
                        target.at[pl.ds(row, xr), pl.ds(col, LANES)],
                        sems.at[at],
                    )
                    pl.when(here)(copy.start)
                    waits.append((here, copy))

                @pl.when(turn == 0)
                def _():
                    total = ref[t, xr:, :].astype(F32)
                    total = (total[:1] + total[8:9]) * factors[0]
                    bias_ref[:, pl.ds(col, LANES)] += total

                at += 1
        for here, copy in waits:
            pl.when(here)(copy.wait)

    def run(*refs):
        body(*refs[: len(inputs)], *refs[len(inputs) + len(after) :])

    somewhere = pl.BlockSpec(memory_space=pl.ANY)
    moved = 2 * copies * xr * LANES * 6
    return pl.pallas_call(
        run,
        out_shape=[weight, weight, shape((1, hid), F32)],
        in_specs=[VMEM] * len(arrays)
        + ([somewhere, somewhere, VMEM] if begun else [])
        + [somewhere] * len(after),
        out_specs=[somewhere, somewhere, VMEM],
        scratch_shapes=[
            pltpu.VMEM((copies, xr, LANES), F32),
            pltpu.SemaphoreType.DMA((copies,)),
        ],
        input_output_aliases={len(arrays): 0, len(arrays) + 1: 1} if begun else {},
        compiler_params=PARAMS,
        cost_estimate=pl.CostEstimate(flops=0, bytes_accessed=moved, transcendentals=0),
    )(*inputs, *after)


def local(
    features, w_neigh, w_self, bias, cotangent, block_rows, block_cols, block_vals, block_count
):
    rs = lax.axis_size("row")
    cs = lax.axis_size("col")
    nd, depth = features.shape
    hid = w_self.shape[1]
    rt = nd * cs
    half = rs // 2
    xw = 2 * depth // cs
    nc = min(rs, hid // LANES)
    nr = rs // nc
    xr = xw // nr

    def along_col(x, k):
        return lax.ppermute(x, "col", [(s, s ^ k) for s in range(cs)])

    def along_chips(x, k):
        return lax.ppermute(x, "row", [(s, s ^ (2 * k)) for s in range(rs)])

    def other_core(x):
        return lax.ppermute(x, "row", [(s, s ^ 1) for s in range(rs)])

    def gather_chips(x):
        found = {0: x}
        step = half // 2
        while step:
            found.update({d + step: along_chips(found[d], step) for d in list(found)})
            step //= 2
        return [found[d] for d in range(half)]

    if rs == 2 * cs:

        def send_own(block, t):
            pairs = []
            for z in range(half):
                for core in range(2):
                    q = 2 * (z ^ t) + core
                    source = (2 * z + core) * cs + z
                    pairs.append((source, (2 * z + q // cs) * cs + q % cs))
            return lax.ppermute(block, ("row", "col"), pairs)

    else:
        swap = [((b % rs) * cs + b // rs, b) for b in range(rs * cs)]

        def send_own(block, t):
            return lax.ppermute(block, ("row", "col"), swap if t == 0 else [])

    near = along_chips(features, 1)
    mine_first = {0: features, 1: near}
    step = half // 2
    while step > 1:
        evens = [d for d in mine_first if d % 2 == 0]
        mine_first.update({d + step: along_chips(mine_first[d], step) for d in evens})
        step //= 2
    theirs_first = {0: other_core(features), 1: other_core(near)}
    own_feats = {0: send_own(features, 0)}
    tile, turned = densify(
        block_rows.reshape(-1),
        block_cols.reshape(-1),
        block_count.reshape(-1),
        block_vals[0, 0],
        nd,
        rs,
        cs,
        [near, theirs_first[0], own_feats[0]],
    )
    mine_first.update(
        {d: follow(x, [tile, theirs_first[1]]) for d, x in mine_first.items() if d > 1}
    )
    mine_last = {d + 1: along_chips(x, 1) for d, x in mine_first.items() if d > 1}
    theirs_first.update({d: other_core(x) for d, x in mine_first.items() if d > 1})
    theirs_last = {d: other_core(x) for d, x in mine_last.items()}
    own_feats.update({d: send_own(x, d) for d, x in mine_first.items() if d})
    own_feats.update({d: send_own(x, d) for d, x in mine_last.items()})

    def placed(mine, theirs):
        places = list(mine) + [half + d for d in theirs]
        return places, [*mine.values(), *theirs.values()]

    begun, mass = forward_first(
        tile, *placed(mine_first, theirs_first), nd, [own_feats[1]]
    )
    evens = [x for d, x in own_feats.items() if d and d % 2 == 0]
    parts = forward_parts(begun, tile, *placed(mine_last, theirs_last), nd, cs, evens)
    own_feat = sum(list(own_feats.values())[1:], own_feats[0])
    degree = mass
    for k in range(1, cs):
        degree = degree + along_col(mass, k)
    inverse = 1.0 / (degree[0] + 1.0)
    inverse = jnp.broadcast_to(inverse[:, None], (rt, LANES))
    own = jnp.dot(own_feat, w_self, preferred_element_type=F32).astype(BF16)

    turned_neigh, turned_self = turn([w_neigh, w_self], parts[:1])
    parts = [parts[0]] + [along_col(parts[k], k) for k in range(1, cs)]
    output, sums, packs = activation(
        parts,
        inverse,
        own,
        own_feat,
        w_neigh,
        bias[None, :],
        cotangent,
        [turned_neigh],
    )
    packs = lax.all_to_all(packs, "col", 0, 0)

    keep, send = weight_parts(packs, sums, rs, xr, nc)
    came = other_core(send)
    scaled, self_part = scaled_parts(packs, inverse, turned_neigh, turned_self, rs, [keep])
    chunks = pair_sum(keep, came)
    groups = [[2 * z + core for z in range(half)] for core in range(2)]
    arrived = lax.all_to_all(chunks, "row", 0, 0, axis_index_groups=groups)
    line = gather_chips(last_sum(arrived))

    keep, send = back_parts(turned, scaled, self_part, nd, cs, rs, [chunks])
    keep, send = fold(keep, other_core(send), line[1:])
    line = stack(line, [send])
    step = 1
    while step < half:
        folded = fold(keep, along_chips(send, step))
        keep, send = folded if 2 * step < half else (folded, None)
        step *= 2
    grad_input = keep

    distances = list(range(half))
    mine = [(line, distances, 0)]
    if cs == 4 and half % 2 == 0:
        mid = half // 2
        first, second = along_col(line, 1), along_col(line, 2)
        mine += [
            (first, distances, 1),
            (second, distances, 2),
            (along_col(first[:mid], 2), distances[:mid], 3),
            (along_col(second[mid:], 1), distances[mid:], 3),
        ]
    else:
        mine += [(along_col(line, k), distances, k) for k in range(1, cs)]
    theirs = [(other_core(array), where, column) for array, where, column in mine]
    factor = 1.0 / math.sqrt(nd * rs * cs)
    sizes = (depth, hid, xr, nc, cs, (factor, 32.0 * factor))
    begun = assemble(mine, True, (), *sizes, ())
    total_self, total_neigh, total_bias = assemble(theirs, False, begun, *sizes, [grad_input])
    return output, grad_input, total_self, total_neigh, total_bias.reshape(-1)


def solution(mesh):
    in_specs = (
        P(("col", "row"), None),
        P(),
        P(),
        P(),
        P(("row", "col"), None),
        P("row", "col", None),
        P("row", "col", None),
        P("row", "col", None, None, None),
        P("row", "col"),
    )
    out_specs = (P(("row", "col"), None), P(("col", "row"), None), P(), P(), P())
    return jax.shard_map(local, mesh=mesh, in_specs=in_specs, out_specs=out_specs, check_vma=False)
```

```python
import math

import jax
import jax.numpy as jnp
from jax import lax
from jax.experimental import pallas as pl
from jax.experimental.pallas import tpu as pltpu
from jax.sharding import PartitionSpec as P

F32 = jnp.float32
BF16 = jnp.bfloat16
LANES = 128
EXTRA = 16
VMEM = pl.BlockSpec(memory_space=pltpu.VMEM)
SMEM = pl.BlockSpec(memory_space=pltpu.SMEM)
PARAMS = pltpu.CompilerParams(vmem_limit_bytes=48 * 1024 * 1024)


def call(body, outs, args, scratch=(), smem=0, flops=0, after=()):
    count = len(args)
    moved = sum(math.prod(o.shape) * o.dtype.itemsize for o in outs)
    moved += sum(a.size * a.dtype.itemsize for a in args)

    def run(*refs):
        body(*refs[:count], *refs[count + len(after) :])

    return pl.pallas_call(
        run,
        out_shape=outs,
        in_specs=[SMEM] * smem
        + [VMEM] * (count - smem)
        + [pl.BlockSpec(memory_space=pl.ANY)] * len(after),
        out_specs=[VMEM] * len(outs),
        scratch_shapes=list(scratch),
        compiler_params=PARAMS,
        cost_estimate=pl.CostEstimate(flops=flops, bytes_accessed=moved, transcendentals=0),
    )(*args, *after)


def shape(dims, dtype):
    return jax.ShapeDtypeStruct(tuple(dims), dtype)


def mm(a, b, ca=1, cb=0):
    return lax.dot_general(a, b, (((ca,), (cb,)), ((), ())), preferred_element_type=F32)


def follow(x, after):
    def body(x_ref, out_ref):
        out_ref[...] = x_ref[...]

    return call(body, [shape(x.shape, x.dtype)], [x], after=after)[0]


def turn(weights, after):
    def body(*refs):
        for ref, out_ref in zip(refs, refs[len(weights) :]):
            out_ref[...] = ref[...].T

    return call(body, [shape(w.shape[::-1], w.dtype) for w in weights], weights, after=after)


def stack(parts, joined=False, after=()):
    count = parts[0].shape[0] if joined else 1

    def body(*refs):
        for k, ref in enumerate(refs[:-1]):
            if joined:
                refs[-1][k * count : (k + 1) * count] = ref[...]
            else:
                refs[-1][k] = ref[...]

    dims = parts[0].shape[1:] if joined else parts[0].shape
    out = shape((len(parts) * count, *dims), parts[0].dtype)
    return call(body, [out], parts, after=after)[0]


def densify(rows, cols, count, values, nd, rs, cs, after):
    rt, ct, half = nd * cs, nd * rs, rs // 2

    def body(rows_ref, cols_ref, count_ref, values_ref, tile_ref, turned_ref, acc):
        i, j = lax.axis_index("row"), lax.axis_index("col")
        z, c = i // 2, lax.rem(i, 2)
        acc[...] = jnp.zeros_like(acc)

        def add(s, carry):
            col = cols_ref[s]
            row = rows_ref[s] ^ j
            col = (z ^ (col // 2)) + half * (lax.rem(col, 2) ^ c)
            r = pl.multiple_of(row * nd, nd)
            c0 = pl.multiple_of(col * nd, nd)
            acc[pl.ds(r, nd), pl.ds(c0, nd)] += values_ref[s].astype(F32)
            return carry

        lax.fori_loop(0, count_ref[0], add, 0)
        tile_ref[...] = acc[...].astype(BF16)
        for k in range(rs):
            cut = acc[:, k * nd : (k + 1) * nd]
            turned_ref[k * nd : (k + 1) * nd, :] = cut.T.astype(BF16)

    return call(
        body,
        [shape((rt, ct), BF16), shape((ct, rt), BF16)],
        [rows, cols, count, values],
        [pltpu.VMEM((rt, ct), F32)],
        smem=3,
        flops=rt * ct,
        after=after,
    )


def tile_columns(tile_ref, places, nd):
    return jnp.concatenate([tile_ref[:, p * nd : (p + 1) * nd] for p in places], axis=1)


def row_sums(tile, nd, cs):
    rt, ct = tile.shape

    def body(tile_ref, mass_ref):
        j = lax.axis_index("col")
        ones = jnp.ones((8, ct), BF16)
        for k in range(cs):
            place = pl.multiple_of((j ^ k) * nd, nd)
            mass_ref[:, pl.ds(place, nd)] = mm(ones, tile_ref[k * nd : (k + 1) * nd, :], 1, 1)

    return call(body, [shape((8, rt), F32)], [tile], flops=16 * tile.size)[0]


def forward_first(tile, places, blocks, nd, after):
    rt = tile.shape[0]
    width = blocks[0].shape[1]

    def body(*refs):
        tile_ref, feat_refs = refs[0], refs[1 : 1 + len(blocks)]
        sum_ref = refs[1 + len(blocks)]
        feats = jnp.concatenate([r[...] for r in feat_refs], axis=0)
        sum_ref[...] = mm(tile_columns(tile_ref, places, nd), feats)

    return call(
        body,
        [shape((rt, width), F32)],
        [tile, *blocks],
        flops=2 * rt * len(places) * nd * width,
        after=after,
    )[0]


def forward_parts(begun, tile, places, blocks, nd, cs, after):
    width = blocks[0].shape[1]

    def body(*refs):
        sum_ref, tile_ref, feat_refs = refs[0], refs[1], refs[2 : 2 + len(blocks)]
        outs = refs[2 + len(blocks) :]
        feats = jnp.concatenate([r[...] for r in feat_refs], axis=0)
        parts = sum_ref[...] + mm(tile_columns(tile_ref, places, nd), feats)
        for k in range(cs):
            outs[k][...] = parts[k * nd : (k + 1) * nd].astype(outs[k].dtype)

    return call(
        body,
        [shape((nd, width), BF16 if k else F32) for k in range(cs)],
        [begun, tile, *blocks],
        flops=2 * tile.shape[0] * len(places) * nd * width,
        after=after,
    )


def activation(parts, masses, own, own_feat, w_neigh, bias, cotangent, after):
    cs = len(parts)
    nd, hid = own.shape
    depth = own_feat.shape[1]
    xw = 2 * depth // cs

    def body(*refs):
        part_refs = refs[:cs]
        mass_refs = refs[cs : cs + 2]
        own_ref, feat_ref, w_ref, bias_ref, cot_ref = refs[cs + 2 : cs + 7]
        out_ref, sum_ref, *packs = refs[cs + 7 : -1]
        both = refs[-1]
        j = lax.axis_index("col")
        here = pl.ds(pl.multiple_of(j * nd, nd), nd)
        inv = 1.0 / (mass_refs[0][:, here] + mass_refs[1][:, here] + 1.0)
        inv = jnp.broadcast_to(inv.T[:, :1], (nd, LANES))
        total = sum(r[...].astype(F32) for r in part_refs)
        mean = (total * jnp.concatenate([inv] * (depth // LANES), axis=1)).astype(BF16)
        both[:, :depth] = feat_ref[...]
        both[:, depth:] = mean
        pre = own_ref[...].astype(F32) + mm(mean, w_ref[...]) + bias_ref[...]
        slope = jnp.where(pre > 0, 1.0, jnp.exp(jnp.minimum(pre, 0.0)))
        out_ref[...] = jnp.where(pre > 0, pre, slope - 1.0).astype(BF16)
        grad = cot_ref[...].astype(F32) * slope
        sum_ref[...] = jnp.broadcast_to(jnp.sum(grad, axis=0, keepdims=True), (8, hid))
        grad = grad.astype(BF16)
        for k in range(cs):
            packs[k][:, :hid] = grad
            target = j ^ k
            if xw % LANES == 0:
                start = pl.multiple_of(target * xw, LANES)
                packs[k][:, hid:] = both[:, pl.ds(start, xw)]
            else:
                for d in range(cs):

                    @pl.when(target == d)
                    def _():
                        packs[k][:, hid:] = both[:, d * xw : (d + 1) * xw]

    return call(
        body,
        [shape((nd, hid), BF16), shape((8, hid), F32)] + [shape((nd, hid + xw), BF16)] * cs,
        [*parts, *masses, own, own_feat, w_neigh, bias, cotangent],
        [pltpu.VMEM((nd, 2 * depth), BF16)],
        flops=2 * own_feat.size * hid,
        after=after,
    )


def split_pair(total):
    high = total.astype(BF16).astype(F32)
    return jnp.concatenate([high, total - high], axis=0)


def weight_parts(packs, sums, rs, xr, nc, after):
    cs = len(packs)
    hid = sums.shape[1]
    nd, xw = packs[0].shape[0], packs[0].shape[1] - hid
    half = rs // 2

    def body(*refs):
        pack_refs = refs[:cs]
        sum_ref, keep_ref, send_ref, acc = refs[cs:]
        x_all = jnp.concatenate([r[:, hid:] for r in pack_refs], axis=0)
        g_all = jnp.concatenate([r[:, :hid] for r in pack_refs], axis=0)
        acc[...] = mm(x_all, g_all, 0, 0)
        i = lax.axis_index("row")
        z, c = i // 2, lax.rem(i, 2)
        for k in range(half):
            for core, ref in ((c, keep_ref), (1 - c, send_ref)):
                q = 2 * (z ^ k) + core
                row = pl.multiple_of((q // nc) * xr, xr)
                col = pl.multiple_of(lax.rem(q, nc) * LANES, LANES)
                ref[k, :xr, :] = acc[pl.ds(row, xr), pl.ds(col, LANES)].astype(ref.dtype)
                ref[k, xr:, :] = split_pair(sum_ref[:, pl.ds(col, LANES)]).astype(ref.dtype)

    dims = (half, xr + EXTRA, LANES)
    return call(
        body,
        [shape(dims, F32), shape(dims, BF16)],
        [*packs, sums],
        [pltpu.VMEM((xw, hid), F32)],
        flops=2 * cs * nd * xw * hid,
        after=after,
    )


def scaled_parts(packs, first, inverse, turned_neigh, turned_self, cs, rs, after=()):
    count = len(packs)
    nd = packs[0].shape[0]
    hid, depth = turned_neigh.shape

    def body(neigh_ref, own_ref, inv_ref, *refs):
        pack_refs, scaled_ref, self_ref = refs[:count], refs[count], refs[count + 1]
        i, j = lax.axis_index("row"), lax.axis_index("col")
        grads = jnp.concatenate([r[:, :hid] for r in pack_refs], axis=0)
        product = mm(grads, neigh_ref[...])
        for r in range(count):
            start = pl.multiple_of((j ^ (first + r)) * nd, nd)
            inv = inv_ref[pl.ds(start, nd), :]
            inv = jnp.concatenate([inv] * (depth // LANES), axis=1)
            rows = slice(r * nd, (r + 1) * nd)
            scaled_ref[rows, :] = (product[rows] * inv).astype(BF16)

        @pl.when(i * cs // rs == j)
        def _():
            self_ref[...] = mm(grads, own_ref[...])

    return call(
        body,
        [shape((count * nd, depth), BF16), shape((count * nd, depth), F32)],
        [turned_neigh, turned_self, inverse, *packs],
        flops=4 * count * nd * hid * depth,
        after=after,
    )


def halving_order(count):
    order = [0]
    step = count // 2
    while step:
        order = order + [d + step for d in order]
        step //= 2
    return order


def back_parts(turned, scaled, self_parts, nd, cs, rs, after):
    depth = scaled[0].shape[1]
    half = rs // 2
    count = len(scaled)
    each = cs // count

    def body(tile_ref, *refs):
        scaled_refs, self_refs = refs[:count], refs[count : 2 * count]
        keep_ref, send_ref, acc = refs[2 * count :]
        i, j = lax.axis_index("row"), lax.axis_index("col")
        z, c = i // 2, lax.rem(i, 2)
        acc[...] = mm(tile_ref[...], jnp.concatenate([r[...] for r in scaled_refs], axis=0))

        @pl.when(i * cs // rs == j)
        def _():
            for r in range(cs):
                q = i * cs - j * rs + (j ^ r)
                place = ((z ^ (q // 2)) + half * (lax.rem(q, 2) ^ c)) * nd
                rows = slice(r % each * nd, (r % each + 1) * nd)
                acc[pl.ds(pl.multiple_of(place, nd), nd), :] += self_refs[r // each][rows]

        for ref, base in ((send_ref, half), (keep_ref, 0)):
            for k, distance in enumerate(halving_order(half)):
                place = (base + distance) * nd
                ref[k] = acc[place : place + nd, :].astype(ref.dtype)

    dims = (half, nd, depth)
    return call(
        body,
        [shape(dims, F32), shape(dims, BF16)],
        [turned, *scaled, *self_parts],
        [pltpu.VMEM((rs * nd, depth), F32)],
        flops=2 * turned.size * depth,
        after=after,
    )


def fold(keep, came, after=()):
    count, rows, width = keep.shape
    half = count // 2

    def body(keep_ref, came_ref, *outs):
        total = keep_ref[...] + came_ref[...].astype(F32)
        if count == 1:
            outs[0][...] = total[0].astype(BF16)
        else:
            outs[0][...] = total[:half]
            outs[1][...] = total[half:].astype(BF16)

    if count == 1:
        return call(body, [shape((rows, width), BF16)], [keep, came], after=after)[0]
    dims = (half, rows, width)
    return call(body, [shape(dims, F32), shape(dims, BF16)], [keep, came], after=after)


def pair_sum(keep, came):
    half, rows, width = keep.shape
    main = rows - EXTRA

    def body(keep_ref, came_ref, *outs):
        for k in range(half):
            total = keep_ref[k] + came_ref[k].astype(F32)
            dtype = outs[k].dtype
            outs[k][:main, :] = total[:main].astype(dtype)
            merged = total[main : main + 8] + total[main + 8 :]
            outs[k][main:, :] = split_pair(merged).astype(dtype)

    return call(
        body,
        [shape((rows, width), BF16 if k else F32) for k in range(half)],
        [keep, came],
    )


def last_sum(parts):
    rows, width = parts[0].shape
    main = rows - EXTRA

    def body(*refs):
        out_ref = refs[-1]
        total = refs[0][...]
        for ref in refs[1:-1]:
            total = total + ref[...].astype(F32)
        out_ref[:main, :] = total[:main].astype(BF16)
        merged = total[main : main + 8] + total[main + 8 :]
        out_ref[main:, :] = split_pair(merged).astype(BF16)

    return call(body, [shape((rows, width), BF16)], parts)[0]


def assemble(pieces, begun, depth, hid, xr, nc, cs, factors, after):
    xw = 2 * depth // cs
    side = cs // 2
    copies = sum(len(where) for _, where, _ in pieces)
    arrays = [array for array, _, _ in pieces]
    inputs = arrays + list(begun)
    weight = shape((depth, hid), F32)

    def body(*refs):
        piece_refs = refs[: len(pieces)]
        self_ref, neigh_ref, bias_ref, staged, sems = refs[-5:]
        i, j = lax.axis_index("row"), lax.axis_index("col")
        z, c = i // 2, lax.rem(i, 2)
        if begun:
            bias_ref[...] = refs[len(inputs) - 1][...]
        else:
            bias_ref[...] = jnp.zeros_like(bias_ref)
        waits = []
        at = 0
        for ref, (_, where, mine) in zip(piece_refs, pieces):
            for t, (distance, column) in enumerate(where):
                owner = j ^ column
                first = owner < side
                q = 2 * (z ^ distance) + (c if mine else 1 - c)
                col = pl.multiple_of(lax.rem(q, nc) * LANES, LANES)
                turn = q // nc
                row = pl.multiple_of(lax.rem(owner, side) * xw + turn * xr, xr)
                scale = jnp.where(first, factors[0], factors[1])
                staged[at] = ref[t, :xr, :].astype(F32) * scale
                for target, here in ((self_ref, first), (neigh_ref, jnp.logical_not(first))):
                    copy = pltpu.make_async_copy(
                        staged.at[at],
                        target.at[pl.ds(row, xr), pl.ds(col, LANES)],
                        sems.at[at],
                    )
                    pl.when(here)(copy.start)
                    waits.append((here, copy))

                @pl.when(turn == 0)
                def _():
                    total = ref[t, xr:, :].astype(F32)
                    total = (total[:1] + total[8:9]) * factors[0]
                    bias_ref[:, pl.ds(col, LANES)] += total

                at += 1
        for here, copy in waits:
            pl.when(here)(copy.wait)

    def run(*refs):
        body(*refs[: len(inputs)], *refs[len(inputs) + len(after) :])

    somewhere = pl.BlockSpec(memory_space=pl.ANY)
    moved = 2 * copies * xr * LANES * 6
    return pl.pallas_call(
        run,
        out_shape=[weight, weight, shape((1, hid), F32)],
        in_specs=[VMEM] * len(arrays)
        + ([somewhere, somewhere, VMEM] if begun else [])
        + [somewhere] * len(after),
        out_specs=[somewhere, somewhere, VMEM],
        scratch_shapes=[
            pltpu.VMEM((copies, xr, LANES), F32),
            pltpu.SemaphoreType.DMA((copies,)),
        ],
        input_output_aliases={len(arrays): 0, len(arrays) + 1: 1} if begun else {},
        compiler_params=PARAMS,
        cost_estimate=pl.CostEstimate(flops=0, bytes_accessed=moved, transcendentals=0),
    )(*inputs, *after)


def local(
    features, w_neigh, w_self, bias, cotangent, block_rows, block_cols, block_vals, block_count
):
    rs = lax.axis_size("row")
    cs = lax.axis_size("col")
    nd, depth = features.shape
    hid = w_self.shape[1]
    rt = nd * cs
    half = rs // 2
    xw = 2 * depth // cs
    nc = min(rs, hid // LANES)
    nr = rs // nc
    xr = xw // nr

    def along_col(x, k):
        return lax.ppermute(x, "col", [(s, s ^ k) for s in range(cs)])

    def along_chips(x, k):
        return lax.ppermute(x, "row", [(s, s ^ (2 * k)) for s in range(rs)])

    def other_core(x):
        return lax.ppermute(x, "row", [(s, s ^ 1) for s in range(rs)])

    def gather_chips(x):
        return [x] + [along_chips(x, k) for k in range(1, half)]

    if rs == 2 * cs:

        def send_own(block, t):
            pairs = []
            for z in range(half):
                for core in range(2):
                    q = 2 * (z ^ t) + core
                    source = (2 * z + core) * cs + z
                    pairs.append((source, (2 * z + q // cs) * cs + q % cs))
            return lax.ppermute(block, ("row", "col"), pairs)

    else:
        swap = [((b % rs) * cs + b // rs, b) for b in range(rs * cs)]

        def send_own(block, t):
            return lax.ppermute(block, ("row", "col"), swap if t == 0 else [])

    near = along_chips(features, 1)
    mine_first = {0: features, 1: near}
    step = half // 2
    while step > 1:
        evens = [d for d in mine_first if d % 2 == 0]
        mine_first.update({d + step: along_chips(mine_first[d], step) for d in evens})
        step //= 2
    theirs_first = {0: other_core(features), 1: other_core(near)}
    own_feats = {0: send_own(features, 0)}
    tile, turned = densify(
        block_rows.reshape(-1),
        block_cols.reshape(-1),
        block_count.reshape(-1),
        block_vals[0, 0],
        nd,
        rs,
        cs,
        [],
    )
    mine_last = {d + 1: along_chips(x, 1) for d, x in mine_first.items() if d > 1}
    theirs_first.update({d: other_core(x) for d, x in mine_first.items() if d > 1})
    theirs_last = {d: other_core(x) for d, x in mine_last.items()}
    own_feats[1] = send_own(near, 1)

    def placed(mine, theirs):
        places = list(mine) + [half + d for d in theirs]
        return places, [*mine.values(), *theirs.values()]

    begun = forward_first(
        tile, *placed(mine_first, theirs_first), nd, [own_feats[0], own_feats[1]]
    )
    degree = row_sums(tile, nd, cs)
    step = 1
    while step < cs:
        masses = [degree, along_col(degree, step)]
        degree = masses[0] + masses[1]
        step *= 2
    evens = {d: send_own(follow(x, [begun, masses[0]]), d) for d, x in mine_first.items() if d > 1}
    own_feats.update(evens)
    own_feats.update({d: send_own(x, d) for d, x in mine_last.items()})
    parts = forward_parts(begun, tile, *placed(mine_last, theirs_last), nd, cs, list(evens.values()))
    own_feat = sum(list(own_feats.values())[1:], own_feats[0])
    inverse = 1.0 / (degree[0] + 1.0)
    inverse = jnp.broadcast_to(inverse[:, None], (rt, LANES))
    own = jnp.dot(own_feat, w_self, preferred_element_type=F32).astype(BF16)

    turned_neigh, turned_self = turn([w_neigh, w_self], [parts[0]])
    parts = [parts[0]] + [along_col(parts[k], k) for k in range(1, cs)]
    output, sums, *packs = activation(
        parts, masses, own, own_feat, w_neigh, bias[None, :], cotangent, [turned_neigh]
    )
    packs = [packs[0]] + [along_col(packs[k], k) for k in range(1, cs)]

    mid = cs // 2
    scaled_args = (inverse, turned_neigh, turned_self, cs, rs)
    early = scaled_parts(packs[:mid], 0, *scaled_args)
    keep, send = weight_parts(packs, sums, rs, xr, nc, early[:1])
    came = other_core(send)
    late = scaled_parts(packs[mid:], mid, *scaled_args, [keep])
    scaled, self_parts = zip(early, late)
    chunks = pair_sum(keep, came)
    chunks = [chunks[0]] + [along_chips(chunks[k], k) for k in range(1, half)]
    line = gather_chips(last_sum(chunks))

    keep, send = back_parts(turned, scaled, self_parts, nd, cs, rs, chunks[1:])
    keep, send = fold(keep, other_core(send), line[1:])
    line = stack(line, after=[send])
    step = 1
    while step < half:
        folded = fold(keep, along_chips(send, step))
        keep, send = folded if 2 * step < half else (folded, None)
        step *= 2
    grad_input = keep

    def piece(array, first, column, mine):
        return array, [(first + t, column) for t in range(array.shape[0])], mine

    mid = half // 2
    if cs == 4 and mid:
        first, second = along_col(line, 1), along_col(line, 2)
        near = [(line, 0, 0), (first, 0, 1), (second, 0, 2)]
        rest = [(along_col(first[:mid], 2), 0, 3), (along_col(second[mid:], 1), mid, 3)]
    else:
        near = [(line, 0, 0)] + [(along_col(line, k), 0, k) for k in range(1, cs - 1)]
        rest = [(along_col(line, cs - 1), 0, cs - 1)]
    factor = 1.0 / math.sqrt(nd * rs * cs)
    sizes = (depth, hid, xr, nc, cs, (factor, 32.0 * factor))
    begun = assemble([piece(*x, True) for x in near], (), *sizes, ())
    pieces = [piece(*x, True) for x in rest]
    near = [(follow(x, [begun[2]]) if n == 1 else x, *where) for n, (x, *where) in enumerate(near)]
    pieces += [piece(other_core(x), *where, False) for x, *where in near + rest]
    total_self, total_neigh, total_bias = assemble(pieces, begun, *sizes, [grad_input])
    return output, grad_input, total_self, total_neigh, total_bias.reshape(-1)


def solution(mesh):
    in_specs = (
        P(("col", "row"), None),
        P(),
        P(),
        P(),
        P(("row", "col"), None),
        P("row", "col", None),
        P("row", "col", None),
        P("row", "col", None, None, None),
        P("row", "col"),
    )
    out_specs = (P(("row", "col"), None), P(("col", "row"), None), P(), P(), P())
    return jax.shard_map(local, mesh=mesh, in_specs=in_specs, out_specs=out_specs, check_vma=False)
```

```python
import math

import jax
import jax.numpy as jnp
from jax import lax
from jax.experimental import pallas as pl
from jax.experimental.pallas import tpu as pltpu
from jax.sharding import PartitionSpec as P

F32 = jnp.float32
BF16 = jnp.bfloat16
LANES = 128
EXTRA = 16
VMEM = pl.BlockSpec(memory_space=pltpu.VMEM)
SMEM = pl.BlockSpec(memory_space=pltpu.SMEM)
PARAMS = pltpu.CompilerParams(vmem_limit_bytes=48 * 1024 * 1024)


def call(body, outs, args, scratch=(), smem=0, flops=0, after=()):
    count = len(args)
    moved = sum(math.prod(o.shape) * o.dtype.itemsize for o in outs)
    moved += sum(a.size * a.dtype.itemsize for a in args)

    def run(*refs):
        body(*refs[:count], *refs[count + len(after) :])

    return pl.pallas_call(
        run,
        out_shape=outs,
        in_specs=[SMEM] * smem
        + [VMEM] * (count - smem)
        + [pl.BlockSpec(memory_space=pl.ANY)] * len(after),
        out_specs=[VMEM] * len(outs),
        scratch_shapes=list(scratch),
        compiler_params=PARAMS,
        cost_estimate=pl.CostEstimate(flops=flops, bytes_accessed=moved, transcendentals=0),
    )(*args, *after)


def shape(dims, dtype):
    return jax.ShapeDtypeStruct(tuple(dims), dtype)


def mm(a, b, ca=1, cb=0):
    return lax.dot_general(a, b, (((ca,), (cb,)), ((), ())), preferred_element_type=F32)


def follow(x, after):
    def body(x_ref, out_ref):
        out_ref[...] = x_ref[...]

    return call(body, [shape(x.shape, x.dtype)], [x], after=after)[0]


def turn(weights, after):
    def body(*refs):
        for ref, out_ref in zip(refs, refs[len(weights) :]):
            out_ref[...] = ref[...].T

    return call(body, [shape(w.shape[::-1], w.dtype) for w in weights], weights, after=after)


def stack(parts, joined=False, after=()):
    count = parts[0].shape[0] if joined else 1

    def body(*refs):
        for k, ref in enumerate(refs[:-1]):
            if joined:
                refs[-1][k * count : (k + 1) * count] = ref[...]
            else:
                refs[-1][k] = ref[...]

    dims = parts[0].shape[1:] if joined else parts[0].shape
    out = shape((len(parts) * count, *dims), parts[0].dtype)
    return call(body, [out], parts, after=after)[0]


def densify(rows, cols, count, values, nd, rs, cs, after):
    rt, ct, half = nd * cs, nd * rs, rs // 2

    def body(rows_ref, cols_ref, count_ref, values_ref, tile_ref, turned_ref, acc):
        i, j = lax.axis_index("row"), lax.axis_index("col")
        z, c = i // 2, lax.rem(i, 2)
        acc[...] = jnp.zeros_like(acc)

        def add(s, carry):
            col = cols_ref[s]
            row = rows_ref[s] ^ j
            col = (z ^ (col // 2)) + half * (lax.rem(col, 2) ^ c)
            r = pl.multiple_of(row * nd, nd)
            c0 = pl.multiple_of(col * nd, nd)
            acc[pl.ds(r, nd), pl.ds(c0, nd)] += values_ref[s].astype(F32)
            return carry

        lax.fori_loop(0, count_ref[0], add, 0)
        tile_ref[...] = acc[...].astype(BF16)
        for k in range(rs):
            cut = acc[:, k * nd : (k + 1) * nd]
            turned_ref[k * nd : (k + 1) * nd, :] = cut.T.astype(BF16)

    return call(
        body,
        [shape((rt, ct), BF16), shape((ct, rt), BF16)],
        [rows, cols, count, values],
        [pltpu.VMEM((rt, ct), F32)],
        smem=3,
        flops=rt * ct,
        after=after,
    )


def tile_columns(tile_ref, places, nd):
    return jnp.concatenate([tile_ref[:, p * nd : (p + 1) * nd] for p in places], axis=1)


def row_sums(tile, nd, cs):
    rt, ct = tile.shape

    def body(tile_ref, mass_ref):
        j = lax.axis_index("col")
        ones = jnp.ones((8, ct), BF16)
        for k in range(cs):
            place = pl.multiple_of((j ^ k) * nd, nd)
            mass_ref[:, pl.ds(place, nd)] = mm(ones, tile_ref[k * nd : (k + 1) * nd, :], 1, 1)

    return call(body, [shape((8, rt), F32)], [tile], flops=16 * tile.size)[0]


def forward_first(tile, places, blocks, nd, after):
    rt = tile.shape[0]
    width = blocks[0].shape[1]

    def body(*refs):
        tile_ref, feat_refs = refs[0], refs[1 : 1 + len(blocks)]
        sum_ref = refs[1 + len(blocks)]
        feats = jnp.concatenate([r[...] for r in feat_refs], axis=0)
        sum_ref[...] = mm(tile_columns(tile_ref, places, nd), feats)

    return call(
        body,
        [shape((rt, width), F32)],
        [tile, *blocks],
        flops=2 * rt * len(places) * nd * width,
        after=after,
    )[0]


def forward_parts(begun, tile, places, blocks, nd, cs, after):
    width = blocks[0].shape[1]

    def body(*refs):
        sum_ref, tile_ref, feat_refs = refs[0], refs[1], refs[2 : 2 + len(blocks)]
        outs = refs[2 + len(blocks) :]
        feats = jnp.concatenate([r[...] for r in feat_refs], axis=0)
        parts = sum_ref[...] + mm(tile_columns(tile_ref, places, nd), feats)
        for k in range(cs):
            outs[k][...] = parts[k * nd : (k + 1) * nd].astype(outs[k].dtype)

    return call(
        body,
        [shape((nd, width), BF16 if k else F32) for k in range(cs)],
        [begun, tile, *blocks],
        flops=2 * tile.shape[0] * len(places) * nd * width,
        after=after,
    )


def activation(parts, masses, own, own_feat, w_neigh, bias, cotangent, after):
    cs = len(parts)
    nd, hid = own.shape
    depth = own_feat.shape[1]
    xw = 2 * depth // cs

    def body(*refs):
        part_refs = refs[:cs]
        mass_refs = refs[cs : cs + 2]
        own_ref, feat_ref, w_ref, bias_ref, cot_ref = refs[cs + 2 : cs + 7]
        out_ref, sum_ref, *packs = refs[cs + 7 : -1]
        both = refs[-1]
        j = lax.axis_index("col")
        here = pl.ds(pl.multiple_of(j * nd, nd), nd)
        inv = 1.0 / (mass_refs[0][:, here] + mass_refs[1][:, here] + 1.0)
        inv = jnp.broadcast_to(inv.T[:, :1], (nd, LANES))
        total = sum(r[...].astype(F32) for r in part_refs)
        mean = (total * jnp.concatenate([inv] * (depth // LANES), axis=1)).astype(BF16)
        both[:, :depth] = feat_ref[...]
        both[:, depth:] = mean
        pre = own_ref[...].astype(F32) + mm(mean, w_ref[...]) + bias_ref[...]
        slope = jnp.where(pre > 0, 1.0, jnp.exp(jnp.minimum(pre, 0.0)))
        out_ref[...] = jnp.where(pre > 0, pre, slope - 1.0).astype(BF16)
        grad = cot_ref[...].astype(F32) * slope
        sum_ref[...] = jnp.broadcast_to(jnp.sum(grad, axis=0, keepdims=True), (8, hid))
        grad = grad.astype(BF16)
        for k in range(cs):
            packs[k][:, :hid] = grad
            target = j ^ k
            if xw % LANES == 0:
                start = pl.multiple_of(target * xw, LANES)
                packs[k][:, hid:] = both[:, pl.ds(start, xw)]
            else:
                for d in range(cs):

                    @pl.when(target == d)
                    def _():
                        packs[k][:, hid:] = both[:, d * xw : (d + 1) * xw]

    return call(
        body,
        [shape((nd, hid), BF16), shape((8, hid), F32)] + [shape((nd, hid + xw), BF16)] * cs,
        [*parts, *masses, own, own_feat, w_neigh, bias, cotangent],
        [pltpu.VMEM((nd, 2 * depth), BF16)],
        flops=2 * own_feat.size * hid,
        after=after,
    )


def split_pair(total):
    high = total.astype(BF16).astype(F32)
    return jnp.concatenate([high, total - high], axis=0)


def weight_parts(packs, sums, rs, xr, nc, after):
    cs = len(packs)
    hid = sums.shape[1]
    nd, xw = packs[0].shape[0], packs[0].shape[1] - hid
    half = rs // 2

    def body(*refs):
        pack_refs = refs[:cs]
        sum_ref, keep_ref, send_ref, acc = refs[cs:]
        x_all = jnp.concatenate([r[:, hid:] for r in pack_refs], axis=0)
        g_all = jnp.concatenate([r[:, :hid] for r in pack_refs], axis=0)
        acc[...] = mm(x_all, g_all, 0, 0)
        i = lax.axis_index("row")
        z, c = i // 2, lax.rem(i, 2)
        for k in range(half):
            for core, ref in ((c, keep_ref), (1 - c, send_ref)):
                q = 2 * (z ^ k) + core
                row = pl.multiple_of((q // nc) * xr, xr)
                col = pl.multiple_of(lax.rem(q, nc) * LANES, LANES)
                ref[k, :xr, :] = acc[pl.ds(row, xr), pl.ds(col, LANES)].astype(ref.dtype)
                ref[k, xr:, :] = split_pair(sum_ref[:, pl.ds(col, LANES)]).astype(ref.dtype)

    dims = (half, xr + EXTRA, LANES)
    return call(
        body,
        [shape(dims, F32), shape(dims, BF16)],
        [*packs, sums],
        [pltpu.VMEM((xw, hid), F32)],
        flops=2 * cs * nd * xw * hid,
        after=after,
    )


def scaled_parts(packs, first, inverse, turned_neigh, turned_self, cs, rs, after=()):
    count = len(packs)
    nd = packs[0].shape[0]
    hid, depth = turned_neigh.shape

    def body(neigh_ref, own_ref, inv_ref, *refs):
        pack_refs, scaled_ref, self_ref = refs[:count], refs[count], refs[count + 1]
        i, j = lax.axis_index("row"), lax.axis_index("col")
        grads = jnp.concatenate([r[:, :hid] for r in pack_refs], axis=0)
        product = mm(grads, neigh_ref[...])
        for r in range(count):
            start = pl.multiple_of((j ^ (first + r)) * nd, nd)
            inv = inv_ref[pl.ds(start, nd), :]
            inv = jnp.concatenate([inv] * (depth // LANES), axis=1)
            rows = slice(r * nd, (r + 1) * nd)
            scaled_ref[rows, :] = (product[rows] * inv).astype(BF16)

        @pl.when(i * cs // rs == j)
        def _():
            self_ref[...] = mm(grads, own_ref[...])

    return call(
        body,
        [shape((count * nd, depth), BF16), shape((count * nd, depth), F32)],
        [turned_neigh, turned_self, inverse, *packs],
        flops=4 * count * nd * hid * depth,
        after=after,
    )


def halving_order(count):
    order = [0]
    step = count // 2
    while step:
        order = order + [d + step for d in order]
        step //= 2
    return order


def back_parts(turned, scaled, self_parts, nd, cs, rs, after):
    depth = scaled[0].shape[1]
    half = rs // 2
    count = len(scaled)
    each = cs // count

    def body(tile_ref, *refs):
        scaled_refs, self_refs = refs[:count], refs[count : 2 * count]
        keep_ref, send_ref, acc = refs[2 * count :]
        i, j = lax.axis_index("row"), lax.axis_index("col")
        z, c = i // 2, lax.rem(i, 2)
        acc[...] = mm(tile_ref[...], jnp.concatenate([r[...] for r in scaled_refs], axis=0))

        @pl.when(i * cs // rs == j)
        def _():
            for r in range(cs):
                q = i * cs - j * rs + (j ^ r)
                place = ((z ^ (q // 2)) + half * (lax.rem(q, 2) ^ c)) * nd
                rows = slice(r % each * nd, (r % each + 1) * nd)
                acc[pl.ds(pl.multiple_of(place, nd), nd), :] += self_refs[r // each][rows]

        for ref, base in ((send_ref, half), (keep_ref, 0)):
            for k, distance in enumerate(halving_order(half)):
                place = (base + distance) * nd
                ref[k] = acc[place : place + nd, :].astype(ref.dtype)

    dims = (half, nd, depth)
    return call(
        body,
        [shape(dims, F32), shape(dims, BF16)],
        [turned, *scaled, *self_parts],
        [pltpu.VMEM((rs * nd, depth), F32)],
        flops=2 * turned.size * depth,
        after=after,
    )


def fold(keep, came, after=()):
    count, rows, width = keep.shape
    half = count // 2

    def body(keep_ref, came_ref, *outs):
        total = keep_ref[...] + came_ref[...].astype(F32)
        if count == 1:
            outs[0][...] = total[0].astype(BF16)
        else:
            outs[0][...] = total[:half]
            outs[1][...] = total[half:].astype(BF16)

    if count == 1:
        return call(body, [shape((rows, width), BF16)], [keep, came], after=after)[0]
    dims = (half, rows, width)
    return call(body, [shape(dims, F32), shape(dims, BF16)], [keep, came], after=after)


def pair_sum(keep, came):
    half, rows, width = keep.shape
    main = rows - EXTRA

    def body(keep_ref, came_ref, *outs):
        for k in range(half):
            total = keep_ref[k] + came_ref[k].astype(F32)
            dtype = outs[k].dtype
            outs[k][:main, :] = total[:main].astype(dtype)
            merged = total[main : main + 8] + total[main + 8 :]
            outs[k][main:, :] = split_pair(merged).astype(dtype)

    return call(
        body,
        [shape((rows, width), BF16 if k else F32) for k in range(half)],
        [keep, came],
    )


def last_sum(parts):
    rows, width = parts[0].shape
    main = rows - EXTRA

    def body(*refs):
        out_ref = refs[-1]
        total = refs[0][...]
        for ref in refs[1:-1]:
            total = total + ref[...].astype(F32)
        out_ref[:main, :] = total[:main].astype(BF16)
        merged = total[main : main + 8] + total[main + 8 :]
        out_ref[main:, :] = split_pair(merged).astype(BF16)

    return call(body, [shape((rows, width), BF16)], parts)[0]


def assemble(pieces, begun, depth, hid, xr, nc, cs, factors, after):
    xw = 2 * depth // cs
    side = cs // 2
    copies = sum(len(where) for _, where, _ in pieces)
    arrays = [array for array, _, _ in pieces]
    inputs = arrays + list(begun)
    weight = shape((depth, hid), F32)

    def body(*refs):
        piece_refs = refs[: len(pieces)]
        self_ref, neigh_ref, bias_ref, staged, sems = refs[-5:]
        i, j = lax.axis_index("row"), lax.axis_index("col")
        z, c = i // 2, lax.rem(i, 2)
        if begun:
            bias_ref[...] = refs[len(inputs) - 1][...]
        else:
            bias_ref[...] = jnp.zeros_like(bias_ref)
        waits = []
        at = 0
        for ref, (_, where, mine) in zip(piece_refs, pieces):
            for t, (distance, column) in enumerate(where):
                owner = j ^ column
                first = owner < side
                q = 2 * (z ^ distance) + (c if mine else 1 - c)
                col = pl.multiple_of(lax.rem(q, nc) * LANES, LANES)
                turn = q // nc
                row = pl.multiple_of(lax.rem(owner, side) * xw + turn * xr, xr)
                scale = jnp.where(first, factors[0], factors[1])
                staged[at] = ref[t, :xr, :].astype(F32) * scale
                for target, here in ((self_ref, first), (neigh_ref, jnp.logical_not(first))):
                    copy = pltpu.make_async_copy(
                        staged.at[at],
                        target.at[pl.ds(row, xr), pl.ds(col, LANES)],
                        sems.at[at],
                    )
                    pl.when(here)(copy.start)
                    waits.append((here, copy))

                @pl.when(turn == 0)
                def _():
                    total = ref[t, xr:, :].astype(F32)
                    total = (total[:1] + total[8:9]) * factors[0]
                    bias_ref[:, pl.ds(col, LANES)] += total

                at += 1
        for here, copy in waits:
            pl.when(here)(copy.wait)

    def run(*refs):
        body(*refs[: len(inputs)], *refs[len(inputs) + len(after) :])

    somewhere = pl.BlockSpec(memory_space=pl.ANY)
    moved = 2 * copies * xr * LANES * 6
    return pl.pallas_call(
        run,
        out_shape=[weight, weight, shape((1, hid), F32)],
        in_specs=[VMEM] * len(arrays)
        + ([somewhere, somewhere, VMEM] if begun else [])
        + [somewhere] * len(after),
        out_specs=[somewhere, somewhere, VMEM],
        scratch_shapes=[
            pltpu.VMEM((copies, xr, LANES), F32),
            pltpu.SemaphoreType.DMA((copies,)),
        ],
        input_output_aliases={len(arrays): 0, len(arrays) + 1: 1} if begun else {},
        compiler_params=PARAMS,
        cost_estimate=pl.CostEstimate(flops=0, bytes_accessed=moved, transcendentals=0),
    )(*inputs, *after)


def local(
    features, w_neigh, w_self, bias, cotangent, block_rows, block_cols, block_vals, block_count
):
    rs = lax.axis_size("row")
    cs = lax.axis_size("col")
    nd, depth = features.shape
    hid = w_self.shape[1]
    rt = nd * cs
    half = rs // 2
    xw = 2 * depth // cs
    nc = min(rs, hid // LANES)
    nr = rs // nc
    xr = xw // nr

    def along_col(x, k):
        return lax.ppermute(x, "col", [(s, s ^ k) for s in range(cs)])

    def along_chips(x, k):
        return lax.ppermute(x, "row", [(s, s ^ (2 * k)) for s in range(rs)])

    def other_core(x):
        return lax.ppermute(x, "row", [(s, s ^ 1) for s in range(rs)])

    def gather_chips(x):
        found = {0: x}
        step = half // 2
        while step:
            found.update({d + step: along_chips(found[d], step) for d in list(found)})
            step //= 2
        return [found[d] for d in range(half)]

    if rs == 2 * cs:

        def send_own(block, t):
            pairs = []
            for z in range(half):
                for core in range(2):
                    q = 2 * (z ^ t) + core
                    source = (2 * z + core) * cs + z
                    pairs.append((source, (2 * z + q // cs) * cs + q % cs))
            return lax.ppermute(block, ("row", "col"), pairs)

    else:
        swap = [((b % rs) * cs + b // rs, b) for b in range(rs * cs)]

        def send_own(block, t):
            return lax.ppermute(block, ("row", "col"), swap if t == 0 else [])

    near = along_chips(features, 1)
    mine_first = {0: features, 1: near}
    step = half // 2
    while step > 1:
        evens = [d for d in mine_first if d % 2 == 0]
        mine_first.update({d + step: along_chips(mine_first[d], step) for d in evens})
        step //= 2
    theirs_first = {0: other_core(features), 1: other_core(near)}
    own_feats = {0: send_own(features, 0)}
    tile, turned = densify(
        block_rows.reshape(-1),
        block_cols.reshape(-1),
        block_count.reshape(-1),
        block_vals[0, 0],
        nd,
        rs,
        cs,
        [],
    )
    mine_last = {d + 1: along_chips(x, 1) for d, x in mine_first.items() if d > 1}
    theirs_first.update({d: other_core(x) for d, x in mine_first.items() if d > 1})
    theirs_last = {d: other_core(x) for d, x in mine_last.items()}
    own_feats[1] = send_own(near, 1)

    def placed(mine, theirs):
        places = list(mine) + [half + d for d in theirs]
        return places, [*mine.values(), *theirs.values()]

    begun = forward_first(
        tile, *placed(mine_first, theirs_first), nd, [own_feats[0], own_feats[1]]
    )
    degree = row_sums(tile, nd, cs)
    step = 1
    while step < cs:
        masses = [degree, along_col(degree, step)]
        degree = masses[0] + masses[1]
        step *= 2
    evens = {d: send_own(follow(x, [begun, masses[0]]), d) for d, x in mine_first.items() if d > 1}
    own_feats.update(evens)
    own_feats.update({d: send_own(x, d) for d, x in mine_last.items()})
    parts = forward_parts(begun, tile, *placed(mine_last, theirs_last), nd, cs, list(evens.values()))
    own_feat = sum(list(own_feats.values())[1:], own_feats[0])
    inverse = 1.0 / (degree[0] + 1.0)
    inverse = jnp.broadcast_to(inverse[:, None], (rt, LANES))
    own = jnp.dot(own_feat, w_self, preferred_element_type=F32).astype(BF16)

    turned_neigh, turned_self = turn([w_neigh, w_self], [parts[0]])
    parts = [parts[0]] + [along_col(parts[k], k) for k in range(1, cs)]
    output, sums, *packs = activation(
        parts, masses, own, own_feat, w_neigh, bias[None, :], cotangent, [turned_neigh]
    )
    packs = [packs[0]] + [along_col(packs[k], k) for k in range(1, cs)]

    mid = cs // 2
    scaled_args = (inverse, turned_neigh, turned_self, cs, rs)
    early = scaled_parts(packs[:mid], 0, *scaled_args)
    keep, send = weight_parts(packs, sums, rs, xr, nc, early[:1])
    came = other_core(send)
    late = scaled_parts(packs[mid:], mid, *scaled_args, [keep])
    scaled, self_parts = zip(early, late)
    chunks = pair_sum(keep, came)
    chunks = [chunks[0]] + [along_chips(chunks[k], k) for k in range(1, half)]
    line = gather_chips(last_sum(chunks))

    keep, send = back_parts(turned, scaled, self_parts, nd, cs, rs, chunks[1:])
    keep, send = fold(keep, other_core(send), line[1:])
    line = stack(line, after=[send])
    step = 1
    while step < half:
        folded = fold(keep, along_chips(send, step))
        keep, send = folded if 2 * step < half else (folded, None)
        step *= 2
    grad_input = keep

    def piece(array, first, column, mine):
        return array, [(first + t, column) for t in range(array.shape[0])], mine

    mid = half // 2
    if cs == 4 and mid:
        first, second = along_col(line, 1), along_col(line, 2)
        near = [(line, 0, 0), (first, 0, 1), (second, 0, 2)]
        rest = [(along_col(first[:mid], 2), 0, 3), (along_col(second[mid:], 1), mid, 3)]
    else:
        near = [(line, 0, 0)] + [(along_col(line, k), 0, k) for k in range(1, cs - 1)]
        rest = [(along_col(line, cs - 1), 0, cs - 1)]
    factor = 1.0 / math.sqrt(nd * rs * cs)
    sizes = (depth, hid, xr, nc, cs, (factor, 32.0 * factor))
    begun = assemble([piece(*x, True) for x in near + rest], (), *sizes, ())
    pieces = [piece(other_core(x), *where, False) for x, *where in near + rest]
    total_self, total_neigh, total_bias = assemble(pieces, begun, *sizes, [grad_input])
    return output, grad_input, total_self, total_neigh, total_bias.reshape(-1)


def solution(mesh):
    in_specs = (
        P(("col", "row"), None),
        P(),
        P(),
        P(),
        P(("row", "col"), None),
        P("row", "col", None),
        P("row", "col", None),
        P("row", "col", None, None, None),
        P("row", "col"),
    )
    out_specs = (P(("row", "col"), None), P(("col", "row"), None), P(), P(), P())
    return jax.shard_map(local, mesh=mesh, in_specs=in_specs, out_specs=out_specs, check_vma=False)
```

```python
import math

import jax
import jax.numpy as jnp
from jax import lax
from jax.experimental import pallas as pl
from jax.experimental.pallas import tpu as pltpu
from jax.sharding import PartitionSpec as P

F32 = jnp.float32
BF16 = jnp.bfloat16
LANES = 128
EXTRA = 16
VMEM = pl.BlockSpec(memory_space=pltpu.VMEM)
SMEM = pl.BlockSpec(memory_space=pltpu.SMEM)
MIB = 1024 * 1024


def limits(arrays, scratch=0):
    held = sum(math.prod(a.shape) * a.dtype.itemsize for a in arrays) + scratch
    return pltpu.CompilerParams(vmem_limit_bytes=min(56 * MIB, 2 * held + 12 * MIB))


def call(body, outs, args, scratch=(), smem=0, flops=0, after=()):
    count = len(args)
    moved = sum(math.prod(a.shape) * a.dtype.itemsize for a in (*outs, *args))
    held = sum(math.prod(x.shape) * x.dtype.itemsize for x in scratch)

    def run(*refs):
        body(*refs[:count], *refs[count + len(after) :])

    return pl.pallas_call(
        run,
        out_shape=outs,
        in_specs=[SMEM] * smem
        + [VMEM] * (count - smem)
        + [pl.BlockSpec(memory_space=pl.ANY)] * len(after),
        out_specs=[VMEM] * len(outs),
        scratch_shapes=list(scratch),
        compiler_params=limits([*outs, *args], held),
        cost_estimate=pl.CostEstimate(flops=flops, bytes_accessed=moved, transcendentals=0),
    )(*args, *after)


def shape(dims, dtype):
    return jax.ShapeDtypeStruct(tuple(dims), dtype)


def mm(a, b, ca=1, cb=0):
    return lax.dot_general(a, b, (((ca,), (cb,)), ((), ())), preferred_element_type=F32)


def follow(x, after):
    def body(x_ref, out_ref):
        out_ref[...] = x_ref[...]

    return call(body, [shape(x.shape, x.dtype)], [x], after=after)[0]


def turn(weights, after):
    def body(*refs):
        for ref, out_ref in zip(refs, refs[len(weights) :]):
            out_ref[...] = ref[...].T

    return call(body, [shape(w.shape[::-1], w.dtype) for w in weights], weights, after=after)


def stack(parts, joined=False, after=()):
    count = parts[0].shape[0] if joined else 1

    def body(*refs):
        for k, ref in enumerate(refs[:-1]):
            if joined:
                refs[-1][k * count : (k + 1) * count] = ref[...]
            else:
                refs[-1][k] = ref[...]

    dims = parts[0].shape[1:] if joined else parts[0].shape
    out = shape((len(parts) * count, *dims), parts[0].dtype)
    return call(body, [out], parts, after=after)[0]


def densify(rows, cols, count, values, nd, rs, cs, after):
    rt, ct, half = nd * cs, nd * rs, rs // 2

    def body(rows_ref, cols_ref, count_ref, values_ref, tile_ref, turned_ref, acc):
        i, j = lax.axis_index("row"), lax.axis_index("col")
        z, c = i // 2, lax.rem(i, 2)
        acc[...] = jnp.zeros_like(acc)

        def add(s, carry):
            col = cols_ref[s]
            row = rows_ref[s] ^ j
            col = (z ^ (col // 2)) + half * (lax.rem(col, 2) ^ c)
            r = pl.multiple_of(row * nd, nd)
            c0 = pl.multiple_of(col * nd, nd)
            acc[pl.ds(r, nd), pl.ds(c0, nd)] += values_ref[s].astype(F32)
            return carry

        lax.fori_loop(0, count_ref[0], add, 0)
        tile_ref[...] = acc[...].astype(BF16)
        for k in range(rs):
            cut = acc[:, k * nd : (k + 1) * nd]
            turned_ref[k * nd : (k + 1) * nd, :] = cut.T.astype(BF16)

    return call(
        body,
        [shape((rt, ct), BF16), shape((ct, rt), BF16)],
        [rows, cols, count, values],
        [pltpu.VMEM((rt, ct), F32)],
        smem=3,
        flops=rt * ct,
        after=after,
    )


def tile_columns(tile_ref, places, nd):
    return jnp.concatenate([tile_ref[:, p * nd : (p + 1) * nd] for p in places], axis=1)


def row_sums(tile, nd, cs):
    rt, ct = tile.shape

    def body(tile_ref, mass_ref):
        j = lax.axis_index("col")
        ones = jnp.ones((8, ct), BF16)
        for k in range(cs):
            place = pl.multiple_of((j ^ k) * nd, nd)
            mass_ref[:, pl.ds(place, nd)] = mm(ones, tile_ref[k * nd : (k + 1) * nd, :], 1, 1)

    return call(body, [shape((8, rt), F32)], [tile], flops=16 * tile.size)[0]


def forward_first(tile, places, blocks, nd, after):
    rt = tile.shape[0]
    width = blocks[0].shape[1]

    def body(*refs):
        tile_ref, feat_refs = refs[0], refs[1 : 1 + len(blocks)]
        sum_ref = refs[1 + len(blocks)]
        feats = jnp.concatenate([r[...] for r in feat_refs], axis=0)
        sum_ref[...] = mm(tile_columns(tile_ref, places, nd), feats)

    return call(
        body,
        [shape((rt, width), F32)],
        [tile, *blocks],
        flops=2 * rt * len(places) * nd * width,
        after=after,
    )[0]


def forward_parts(begun, tile, places, blocks, nd, cs, after):
    width = blocks[0].shape[1]

    def body(*refs):
        sum_ref, tile_ref, feat_refs = refs[0], refs[1], refs[2 : 2 + len(blocks)]
        outs = refs[2 + len(blocks) :]
        feats = jnp.concatenate([r[...] for r in feat_refs], axis=0)
        parts = sum_ref[...] + mm(tile_columns(tile_ref, places, nd), feats)
        for k in range(cs):
            outs[k][...] = parts[k * nd : (k + 1) * nd].astype(outs[k].dtype)

    return call(
        body,
        [shape((nd, width), BF16 if k else F32) for k in range(cs)],
        [begun, tile, *blocks],
        flops=2 * tile.shape[0] * len(places) * nd * width,
        after=after,
    )


def activation(parts, masses, own, own_feat, w_neigh, bias, cotangent, after):
    cs = len(parts)
    nd, hid = own.shape
    depth = own_feat.shape[1]
    xw = 2 * depth // cs

    def body(*refs):
        part_refs = refs[:cs]
        mass_refs = refs[cs : cs + 2]
        own_ref, feat_ref, w_ref, bias_ref, cot_ref = refs[cs + 2 : cs + 7]
        out_ref, sum_ref, *packs = refs[cs + 7 : -1]
        both = refs[-1]
        j = lax.axis_index("col")
        here = pl.ds(pl.multiple_of(j * nd, nd), nd)
        inv = 1.0 / (mass_refs[0][:, here] + mass_refs[1][:, here] + 1.0)
        inv = jnp.broadcast_to(inv.T[:, :1], (nd, LANES))
        total = sum(r[...].astype(F32) for r in part_refs)
        mean = (total * jnp.concatenate([inv] * (depth // LANES), axis=1)).astype(BF16)
        both[:, :depth] = feat_ref[...]
        both[:, depth:] = mean
        pre = own_ref[...].astype(F32) + mm(mean, w_ref[...]) + bias_ref[...]
        slope = jnp.where(pre > 0, 1.0, jnp.exp(jnp.minimum(pre, 0.0)))
        out_ref[...] = jnp.where(pre > 0, pre, slope - 1.0).astype(BF16)
        grad = cot_ref[...].astype(F32) * slope
        sum_ref[...] = jnp.broadcast_to(jnp.sum(grad, axis=0, keepdims=True), (8, hid))
        grad = grad.astype(BF16)
        for k in range(cs):
            packs[k][:, :hid] = grad
            target = j ^ k
            if xw % LANES == 0:
                start = pl.multiple_of(target * xw, LANES)
                packs[k][:, hid:] = both[:, pl.ds(start, xw)]
            else:
                for d in range(cs):

                    @pl.when(target == d)
                    def _():
                        packs[k][:, hid:] = both[:, d * xw : (d + 1) * xw]

    return call(
        body,
        [shape((nd, hid), BF16), shape((8, hid), F32)] + [shape((nd, hid + xw), BF16)] * cs,
        [*parts, *masses, own, own_feat, w_neigh, bias, cotangent],
        [pltpu.VMEM((nd, 2 * depth), BF16)],
        flops=2 * own_feat.size * hid,
        after=after,
    )


def split_pair(total):
    high = total.astype(BF16).astype(F32)
    return jnp.concatenate([high, total - high], axis=0)


def weight_parts(packs, sums, rs, xr, nc, after):
    cs = len(packs)
    hid = sums.shape[1]
    nd, xw = packs[0].shape[0], packs[0].shape[1] - hid
    half = rs // 2

    def body(*refs):
        pack_refs = refs[:cs]
        sum_ref, keep_ref, send_ref, acc = refs[cs:]
        x_all = jnp.concatenate([r[:, hid:] for r in pack_refs], axis=0)
        g_all = jnp.concatenate([r[:, :hid] for r in pack_refs], axis=0)
        acc[...] = mm(x_all, g_all, 0, 0)
        i = lax.axis_index("row")
        z, c = i // 2, lax.rem(i, 2)
        for k in range(half):
            for core, ref in ((c, keep_ref), (1 - c, send_ref)):
                q = 2 * (z ^ k) + core
                row = pl.multiple_of((q // nc) * xr, xr)
                col = pl.multiple_of(lax.rem(q, nc) * LANES, LANES)
                ref[k, :xr, :] = acc[pl.ds(row, xr), pl.ds(col, LANES)].astype(ref.dtype)
                ref[k, xr:, :] = split_pair(sum_ref[:, pl.ds(col, LANES)]).astype(ref.dtype)

    dims = (half, xr + EXTRA, LANES)
    return call(
        body,
        [shape(dims, F32), shape(dims, BF16)],
        [*packs, sums],
        [pltpu.VMEM((xw, hid), F32)],
        flops=2 * cs * nd * xw * hid,
        after=after,
    )


def scaled_parts(packs, first, inverse, turned_neigh, turned_self, cs, rs, after=()):
    count = len(packs)
    nd = packs[0].shape[0]
    hid, depth = turned_neigh.shape

    def body(neigh_ref, own_ref, inv_ref, *refs):
        pack_refs, scaled_ref, self_ref = refs[:count], refs[count], refs[count + 1]
        i, j = lax.axis_index("row"), lax.axis_index("col")
        grads = jnp.concatenate([r[:, :hid] for r in pack_refs], axis=0)
        product = mm(grads, neigh_ref[...])
        for r in range(count):
            start = pl.multiple_of((j ^ (first + r)) * nd, nd)
            inv = inv_ref[pl.ds(start, nd), :]
            inv = jnp.concatenate([inv] * (depth // LANES), axis=1)
            rows = slice(r * nd, (r + 1) * nd)
            scaled_ref[rows, :] = (product[rows] * inv).astype(BF16)

        @pl.when(i * cs // rs == j)
        def _():
            self_ref[...] = mm(grads, own_ref[...])

    return call(
        body,
        [shape((count * nd, depth), BF16), shape((count * nd, depth), F32)],
        [turned_neigh, turned_self, inverse, *packs],
        flops=4 * count * nd * hid * depth,
        after=after,
    )


def halving_order(count):
    order = [0]
    step = count // 2
    while step:
        order = order + [d + step for d in order]
        step //= 2
    return order


def back_parts(turned, scaled, self_parts, nd, cs, rs, after):
    depth = scaled[0].shape[1]
    half = rs // 2
    count = len(scaled)
    each = cs // count

    def body(tile_ref, *refs):
        scaled_refs, self_refs = refs[:count], refs[count : 2 * count]
        keep_ref, send_ref, acc = refs[2 * count :]
        i, j = lax.axis_index("row"), lax.axis_index("col")
        z, c = i // 2, lax.rem(i, 2)
        acc[...] = mm(tile_ref[...], jnp.concatenate([r[...] for r in scaled_refs], axis=0))

        @pl.when(i * cs // rs == j)
        def _():
            for r in range(cs):
                q = i * cs - j * rs + (j ^ r)
                place = ((z ^ (q // 2)) + half * (lax.rem(q, 2) ^ c)) * nd
                rows = slice(r % each * nd, (r % each + 1) * nd)
                acc[pl.ds(pl.multiple_of(place, nd), nd), :] += self_refs[r // each][rows]

        for ref, base in ((send_ref, half), (keep_ref, 0)):
            for k, distance in enumerate(halving_order(half)):
                place = (base + distance) * nd
                ref[k] = acc[place : place + nd, :].astype(ref.dtype)

    dims = (half, nd, depth)
    return call(
        body,
        [shape(dims, F32), shape(dims, BF16)],
        [turned, *scaled, *self_parts],
        [pltpu.VMEM((rs * nd, depth), F32)],
        flops=2 * turned.size * depth,
        after=after,
    )


def fold(keep, came, after=()):
    count, rows, width = keep.shape
    half = count // 2

    def body(keep_ref, came_ref, *outs):
        total = keep_ref[...] + came_ref[...].astype(F32)
        if count == 1:
            outs[0][...] = total[0].astype(BF16)
        else:
            outs[0][...] = total[:half]
            outs[1][...] = total[half:].astype(BF16)

    if count == 1:
        return call(body, [shape((rows, width), BF16)], [keep, came], after=after)[0]
    dims = (half, rows, width)
    return call(body, [shape(dims, F32), shape(dims, BF16)], [keep, came], after=after)


def pair_sum(keep, came):
    half, rows, width = keep.shape
    main = rows - EXTRA

    def body(keep_ref, came_ref, *outs):
        for k in range(half):
            total = keep_ref[k] + came_ref[k].astype(F32)
            dtype = outs[k].dtype
            outs[k][:main, :] = total[:main].astype(dtype)
            merged = total[main : main + 8] + total[main + 8 :]
            outs[k][main:, :] = split_pair(merged).astype(dtype)

    return call(
        body,
        [shape((rows, width), BF16 if k else F32) for k in range(half)],
        [keep, came],
    )


def last_sum(parts):
    rows, width = parts[0].shape
    main = rows - EXTRA

    def body(*refs):
        out_ref = refs[-1]
        total = refs[0][...]
        for ref in refs[1:-1]:
            total = total + ref[...].astype(F32)
        out_ref[:main, :] = total[:main].astype(BF16)
        merged = total[main : main + 8] + total[main + 8 :]
        out_ref[main:, :] = split_pair(merged).astype(BF16)

    return call(body, [shape((rows, width), BF16)], parts)[0]


def assemble(pieces, begun, depth, hid, xr, nc, cs, factors, after):
    xw = 2 * depth // cs
    side = cs // 2
    copies = sum(len(where) for _, where, _ in pieces)
    arrays = [array for array, _, _ in pieces]
    inputs = arrays + list(begun)
    weight = shape((depth, hid), F32)

    def body(*refs):
        piece_refs = refs[: len(pieces)]
        self_ref, neigh_ref, bias_ref, staged, sems = refs[-5:]
        i, j = lax.axis_index("row"), lax.axis_index("col")
        z, c = i // 2, lax.rem(i, 2)
        if begun:
            bias_ref[...] = refs[len(inputs) - 1][...]
        else:
            bias_ref[...] = jnp.zeros_like(bias_ref)
        waits = []
        at = 0
        for ref, (_, where, mine) in zip(piece_refs, pieces):
            for t, (distance, column) in enumerate(where):
                owner = j ^ column
                first = owner < side
                q = 2 * (z ^ distance) + (c if mine else 1 - c)
                col = pl.multiple_of(lax.rem(q, nc) * LANES, LANES)
                turn = q // nc
                row = pl.multiple_of(lax.rem(owner, side) * xw + turn * xr, xr)
                scale = jnp.where(first, factors[0], factors[1])
                staged[at] = ref[t, :xr, :].astype(F32) * scale
                for target, here in ((self_ref, first), (neigh_ref, jnp.logical_not(first))):
                    copy = pltpu.make_async_copy(
                        staged.at[at],
                        target.at[pl.ds(row, xr), pl.ds(col, LANES)],
                        sems.at[at],
                    )
                    pl.when(here)(copy.start)
                    waits.append((here, copy))

                @pl.when(turn == 0)
                def _():
                    total = ref[t, xr:, :].astype(F32)
                    total = (total[:1] + total[8:9]) * factors[0]
                    bias_ref[:, pl.ds(col, LANES)] += total

                at += 1
        for here, copy in waits:
            pl.when(here)(copy.wait)

    def run(*refs):
        body(*refs[: len(inputs)], *refs[len(inputs) + len(after) :])

    somewhere = pl.BlockSpec(memory_space=pl.ANY)
    moved = 2 * copies * xr * LANES * 6
    return pl.pallas_call(
        run,
        out_shape=[weight, weight, shape((1, hid), F32)],
        in_specs=[VMEM] * len(arrays)
        + ([somewhere, somewhere, VMEM] if begun else [])
        + [somewhere] * len(after),
        out_specs=[somewhere, somewhere, VMEM],
        scratch_shapes=[
            pltpu.VMEM((copies, xr, LANES), F32),
            pltpu.SemaphoreType.DMA((copies,)),
        ],
        input_output_aliases={len(arrays): 0, len(arrays) + 1: 1} if begun else {},
        compiler_params=limits(arrays, copies * xr * LANES * 4),
        cost_estimate=pl.CostEstimate(flops=0, bytes_accessed=moved, transcendentals=0),
    )(*inputs, *after)


def local(
    features, w_neigh, w_self, bias, cotangent, block_rows, block_cols, block_vals, block_count
):
    rs = lax.axis_size("row")
    cs = lax.axis_size("col")
    nd, depth = features.shape
    hid = w_self.shape[1]
    rt = nd * cs
    half = rs // 2
    xw = 2 * depth // cs
    nc = min(rs, hid // LANES)
    nr = rs // nc
    xr = xw // nr

    def along_col(x, k):
        return lax.ppermute(x, "col", [(s, s ^ k) for s in range(cs)])

    def along_chips(x, k):
        return lax.ppermute(x, "row", [(s, s ^ (2 * k)) for s in range(rs)])

    def other_core(x):
        return lax.ppermute(x, "row", [(s, s ^ 1) for s in range(rs)])

    def gather_chips(x):
        found = {0: x}
        step = half // 2
        while step:
            found.update({d + step: along_chips(found[d], step) for d in list(found)})
            step //= 2
        return [found[d] for d in range(half)]

    if rs == 2 * cs:

        def send_own(block, t):
            pairs = []
            for z in range(half):
                for core in range(2):
                    q = 2 * (z ^ t) + core
                    source = (2 * z + core) * cs + z
                    pairs.append((source, (2 * z + q // cs) * cs + q % cs))
            return lax.ppermute(block, ("row", "col"), pairs)

    else:
        swap = [((b % rs) * cs + b // rs, b) for b in range(rs * cs)]

        def send_own(block, t):
            return lax.ppermute(block, ("row", "col"), swap if t == 0 else [])

    near = along_chips(features, 1)
    mine_first = {0: features, 1: near}
    step = half // 2
    while step > 1:
        evens = [d for d in mine_first if d % 2 == 0]
        mine_first.update({d + step: along_chips(mine_first[d], step) for d in evens})
        step //= 2
    theirs_first = {0: other_core(features), 1: other_core(near)}
    own_feats = {0: send_own(features, 0)}
    tile, turned = densify(
        block_rows.reshape(-1),
        block_cols.reshape(-1),
        block_count.reshape(-1),
        block_vals[0, 0],
        nd,
        rs,
        cs,
        [],
    )
    mine_last = {d + 1: along_chips(x, 1) for d, x in mine_first.items() if d > 1}
    theirs_first.update({d: other_core(x) for d, x in mine_first.items() if d > 1})
    theirs_last = {d: other_core(x) for d, x in mine_last.items()}
    own_feats[1] = send_own(near, 1)

    def placed(mine, theirs):
        places = list(mine) + [half + d for d in theirs]
        return places, [*mine.values(), *theirs.values()]

    begun = forward_first(
        tile, *placed(mine_first, theirs_first), nd, [own_feats[0], own_feats[1]]
    )
    degree = row_sums(tile, nd, cs)
    step = 1
    while step < cs:
        masses = [degree, along_col(degree, step)]
        degree = masses[0] + masses[1]
        step *= 2
    evens = {d: send_own(follow(x, [begun, masses[0]]), d) for d, x in mine_first.items() if d > 1}
    own_feats.update(evens)
    own_feats.update({d: send_own(x, d) for d, x in mine_last.items()})
    parts = forward_parts(begun, tile, *placed(mine_last, theirs_last), nd, cs, list(evens.values()))
    own_feat = sum(list(own_feats.values())[1:], own_feats[0])
    inverse = 1.0 / (degree[0] + 1.0)
    inverse = jnp.broadcast_to(inverse[:, None], (rt, LANES))
    own = jnp.dot(own_feat, w_self, preferred_element_type=F32).astype(BF16)

    turned_neigh, turned_self = turn([w_neigh, w_self], [parts[0]])
    parts = [parts[0]] + [along_col(parts[k], k) for k in range(1, cs)]
    output, sums, *packs = activation(
        parts, masses, own, own_feat, w_neigh, bias[None, :], cotangent, [turned_neigh]
    )
    packs = [packs[0]] + [along_col(packs[k], k) for k in range(1, cs)]

    mid = cs // 2
    scaled_args = (inverse, turned_neigh, turned_self, cs, rs)
    early = scaled_parts(packs[:mid], 0, *scaled_args)
    keep, send = weight_parts(packs, sums, rs, xr, nc, early[:1])
    came = other_core(send)
    late = scaled_parts(packs[mid:], mid, *scaled_args, [keep])
    scaled, self_parts = zip(early, late)
    chunks = pair_sum(keep, came)
    chunks = [chunks[0]] + [along_chips(chunks[k], k) for k in range(1, half)]
    line = gather_chips(last_sum(chunks))

    keep, send = back_parts(turned, scaled, self_parts, nd, cs, rs, [keep])
    keep, send = fold(keep, other_core(follow(send, chunks[1:])), line[1:])
    line = stack(line, after=[send])
    step = 1
    while step < half:
        folded = fold(keep, along_chips(send, step))
        keep, send = folded if 2 * step < half else (folded, None)
        step *= 2
    grad_input = keep

    def piece(array, first, column, mine):
        return array, [(first + t, column) for t in range(array.shape[0])], mine

    mid = half // 2
    if cs == 4 and mid:
        first, second = along_col(line, 1), along_col(line, 2)
        near = [(line, 0, 0), (first, 0, 1), (second, 0, 2)]
        rest = [(along_col(first[:mid], 2), 0, 3), (along_col(second[mid:], 1), mid, 3)]
    else:
        near = [(line, 0, 0)] + [(along_col(line, k), 0, k) for k in range(1, cs - 1)]
        rest = [(along_col(line, cs - 1), 0, cs - 1)]
    factor = 1.0 / math.sqrt(nd * rs * cs)
    sizes = (depth, hid, xr, nc, cs, (factor, 32.0 * factor))
    begun = assemble([piece(*x, True) for x in near + rest], (), *sizes, ())
    pieces = [piece(other_core(x), *where, False) for x, *where in near + rest]
    total_self, total_neigh, total_bias = assemble(pieces, begun, *sizes, [grad_input])
    return output, grad_input, total_self, total_neigh, total_bias.reshape(-1)


def solution(mesh):
    in_specs = (
        P(("col", "row"), None),
        P(),
        P(),
        P(),
        P(("row", "col"), None),
        P("row", "col", None),
        P("row", "col", None),
        P("row", "col", None, None, None),
        P("row", "col"),
    )
    out_specs = (P(("row", "col"), None), P(("col", "row"), None), P(), P(), P())
    return jax.shard_map(local, mesh=mesh, in_specs=in_specs, out_specs=out_specs, check_vma=False)
```

```python
import math

import jax
import jax.numpy as jnp
from jax import lax
from jax.experimental import pallas as pl
from jax.experimental.pallas import tpu as pltpu
from jax.sharding import PartitionSpec as P

F32 = jnp.float32
BF16 = jnp.bfloat16
LANES = 128
EXTRA = 16
VMEM = pl.BlockSpec(memory_space=pltpu.VMEM)
SMEM = pl.BlockSpec(memory_space=pltpu.SMEM)
MIB = 1024 * 1024


def limits(arrays, scratch=0):
    held = sum(math.prod(a.shape) * a.dtype.itemsize for a in arrays) + scratch
    return pltpu.CompilerParams(vmem_limit_bytes=min(56 * MIB, 2 * held + 12 * MIB))


def call(body, outs, args, scratch=(), smem=0, flops=0, after=()):
    count = len(args)
    moved = sum(math.prod(a.shape) * a.dtype.itemsize for a in (*outs, *args))
    held = sum(math.prod(x.shape) * x.dtype.itemsize for x in scratch)

    def run(*refs):
        body(*refs[:count], *refs[count + len(after) :])

    return pl.pallas_call(
        run,
        out_shape=outs,
        in_specs=[SMEM] * smem
        + [VMEM] * (count - smem)
        + [pl.BlockSpec(memory_space=pl.ANY)] * len(after),
        out_specs=[VMEM] * len(outs),
        scratch_shapes=list(scratch),
        compiler_params=limits([*outs, *args], held),
        cost_estimate=pl.CostEstimate(flops=flops, bytes_accessed=moved, transcendentals=0),
    )(*args, *after)


def shape(dims, dtype):
    return jax.ShapeDtypeStruct(tuple(dims), dtype)


def mm(a, b, ca=1, cb=0):
    return lax.dot_general(a, b, (((ca,), (cb,)), ((), ())), preferred_element_type=F32)


def follow(x, after):
    def body(x_ref, out_ref):
        out_ref[...] = x_ref[...]

    return call(body, [shape(x.shape, x.dtype)], [x], after=after)[0]


def turn(weights, after):
    def body(*refs):
        for ref, out_ref in zip(refs, refs[len(weights) :]):
            out_ref[...] = ref[...].T

    return call(body, [shape(w.shape[::-1], w.dtype) for w in weights], weights, after=after)


def stack(parts, joined=False, after=()):
    count = parts[0].shape[0] if joined else 1

    def body(*refs):
        for k, ref in enumerate(refs[:-1]):
            if joined:
                refs[-1][k * count : (k + 1) * count] = ref[...]
            else:
                refs[-1][k] = ref[...]

    dims = parts[0].shape[1:] if joined else parts[0].shape
    out = shape((len(parts) * count, *dims), parts[0].dtype)
    return call(body, [out], parts, after=after)[0]


def densify(rows, cols, count, values, nd, rs, cs, after):
    rt, ct, half = nd * cs, nd * rs, rs // 2

    def body(rows_ref, cols_ref, count_ref, values_ref, tile_ref, turned_ref, acc):
        i, j = lax.axis_index("row"), lax.axis_index("col")
        z, c = i // 2, lax.rem(i, 2)
        acc[...] = jnp.zeros_like(acc)

        def add(s, carry):
            col = cols_ref[s]
            row = rows_ref[s] ^ j
            col = (z ^ (col // 2)) + half * (lax.rem(col, 2) ^ c)
            r = pl.multiple_of(row * nd, nd)
            c0 = pl.multiple_of(col * nd, nd)
            acc[pl.ds(r, nd), pl.ds(c0, nd)] += values_ref[s].astype(F32)
            return carry

        lax.fori_loop(0, count_ref[0], add, 0)
        tile_ref[...] = acc[...].astype(BF16)
        for k in range(rs):
            cut = acc[:, k * nd : (k + 1) * nd]
            turned_ref[k * nd : (k + 1) * nd, :] = cut.T.astype(BF16)

    return call(
        body,
        [shape((rt, ct), BF16), shape((ct, rt), BF16)],
        [rows, cols, count, values],
        [pltpu.VMEM((rt, ct), F32)],
        smem=3,
        flops=rt * ct,
        after=after,
    )


def tile_columns(tile_ref, places, nd):
    return jnp.concatenate([tile_ref[:, p * nd : (p + 1) * nd] for p in places], axis=1)


def row_sums(tile, nd, cs):
    rt, ct = tile.shape

    def body(tile_ref, mass_ref):
        j = lax.axis_index("col")
        ones = jnp.ones((8, ct), BF16)
        for k in range(cs):
            place = pl.multiple_of((j ^ k) * nd, nd)
            mass_ref[:, pl.ds(place, nd)] = mm(ones, tile_ref[k * nd : (k + 1) * nd, :], 1, 1)

    return call(body, [shape((8, rt), F32)], [tile], flops=16 * tile.size)[0]


def forward_first(tile, places, blocks, nd, after):
    rt = tile.shape[0]
    width = blocks[0].shape[1]

    def body(*refs):
        tile_ref, feat_refs = refs[0], refs[1 : 1 + len(blocks)]
        sum_ref = refs[1 + len(blocks)]
        feats = jnp.concatenate([r[...] for r in feat_refs], axis=0)
        sum_ref[...] = mm(tile_columns(tile_ref, places, nd), feats)

    return call(
        body,
        [shape((rt, width), F32)],
        [tile, *blocks],
        flops=2 * rt * len(places) * nd * width,
        after=after,
    )[0]


def forward_parts(begun, tile, places, blocks, nd, cs, after):
    width = blocks[0].shape[1]

    def body(*refs):
        sum_ref, tile_ref, feat_refs = refs[0], refs[1], refs[2 : 2 + len(blocks)]
        outs = refs[2 + len(blocks) :]
        feats = jnp.concatenate([r[...] for r in feat_refs], axis=0)
        parts = sum_ref[...] + mm(tile_columns(tile_ref, places, nd), feats)
        for k in range(cs):
            outs[k][...] = parts[k * nd : (k + 1) * nd].astype(outs[k].dtype)

    return call(
        body,
        [shape((nd, width), BF16 if k else F32) for k in range(cs)],
        [begun, tile, *blocks],
        flops=2 * tile.shape[0] * len(places) * nd * width,
        after=after,
    )


def activation(parts, masses, own, own_feat, w_neigh, bias, cotangent, after):
    cs = len(parts)
    nd, hid = own.shape
    depth = own_feat.shape[1]
    xw = 2 * depth // cs

    def body(*refs):
        part_refs = refs[:cs]
        mass_refs = refs[cs : cs + 2]
        own_ref, feat_ref, w_ref, bias_ref, cot_ref = refs[cs + 2 : cs + 7]
        out_ref, sum_ref, *packs = refs[cs + 7 : -1]
        both = refs[-1]
        j = lax.axis_index("col")
        here = pl.ds(pl.multiple_of(j * nd, nd), nd)
        inv = 1.0 / (mass_refs[0][:, here] + mass_refs[1][:, here] + 1.0)
        inv = jnp.broadcast_to(inv.T[:, :1], (nd, LANES))
        total = sum(r[...].astype(F32) for r in part_refs)
        mean = (total * jnp.concatenate([inv] * (depth // LANES), axis=1)).astype(BF16)
        both[:, :depth] = feat_ref[...]
        both[:, depth:] = mean
        pre = own_ref[...].astype(F32) + mm(mean, w_ref[...]) + bias_ref[...]
        slope = jnp.where(pre > 0, 1.0, jnp.exp(jnp.minimum(pre, 0.0)))
        out_ref[...] = jnp.where(pre > 0, pre, slope - 1.0).astype(BF16)
        grad = cot_ref[...].astype(F32) * slope
        sum_ref[...] = jnp.broadcast_to(jnp.sum(grad, axis=0, keepdims=True), (8, hid))
        grad = grad.astype(BF16)
        for k in range(cs):
            packs[k][:, :hid] = grad
            target = j ^ k
            if xw % LANES == 0:
                start = pl.multiple_of(target * xw, LANES)
                packs[k][:, hid:] = both[:, pl.ds(start, xw)]
            else:
                for d in range(cs):

                    @pl.when(target == d)
                    def _():
                        packs[k][:, hid:] = both[:, d * xw : (d + 1) * xw]

    return call(
        body,
        [shape((nd, hid), BF16), shape((8, hid), F32)] + [shape((nd, hid + xw), BF16)] * cs,
        [*parts, *masses, own, own_feat, w_neigh, bias, cotangent],
        [pltpu.VMEM((nd, 2 * depth), BF16)],
        flops=2 * own_feat.size * hid,
        after=after,
    )


def split_pair(total):
    high = total.astype(BF16).astype(F32)
    return jnp.concatenate([high, total - high], axis=0)


def weight_parts(packs, sums, rs, xr, nc, after):
    cs = len(packs)
    hid = sums.shape[1]
    nd, xw = packs[0].shape[0], packs[0].shape[1] - hid
    half = rs // 2

    def body(*refs):
        pack_refs = refs[:cs]
        sum_ref, keep_ref, send_ref, acc = refs[cs:]
        x_all = jnp.concatenate([r[:, hid:] for r in pack_refs], axis=0)
        g_all = jnp.concatenate([r[:, :hid] for r in pack_refs], axis=0)
        acc[...] = mm(x_all, g_all, 0, 0)
        i = lax.axis_index("row")
        z, c = i // 2, lax.rem(i, 2)
        for k in range(half):
            for core, ref in ((c, keep_ref), (1 - c, send_ref)):
                q = 2 * (z ^ k) + core
                row = pl.multiple_of((q // nc) * xr, xr)
                col = pl.multiple_of(lax.rem(q, nc) * LANES, LANES)
                ref[k, :xr, :] = acc[pl.ds(row, xr), pl.ds(col, LANES)].astype(ref.dtype)
                ref[k, xr:, :] = split_pair(sum_ref[:, pl.ds(col, LANES)]).astype(ref.dtype)

    dims = (half, xr + EXTRA, LANES)
    return call(
        body,
        [shape(dims, F32), shape(dims, BF16)],
        [*packs, sums],
        [pltpu.VMEM((xw, hid), F32)],
        flops=2 * cs * nd * xw * hid,
        after=after,
    )


def scaled_parts(packs, first, inverse, turned_neigh, turned_self, cs, rs, after=()):
    count = len(packs)
    nd = packs[0].shape[0]
    hid, depth = turned_neigh.shape

    def body(neigh_ref, own_ref, inv_ref, *refs):
        pack_refs, scaled_ref, self_ref = refs[:count], refs[count], refs[count + 1]
        i, j = lax.axis_index("row"), lax.axis_index("col")
        grads = jnp.concatenate([r[:, :hid] for r in pack_refs], axis=0)
        product = mm(grads, neigh_ref[...])
        for r in range(count):
            start = pl.multiple_of((j ^ (first + r)) * nd, nd)
            inv = inv_ref[pl.ds(start, nd), :]
            inv = jnp.concatenate([inv] * (depth // LANES), axis=1)
            rows = slice(r * nd, (r + 1) * nd)
            scaled_ref[rows, :] = (product[rows] * inv).astype(BF16)

        @pl.when(i * cs // rs == j)
        def _():
            self_ref[...] = mm(grads, own_ref[...])

    return call(
        body,
        [shape((count * nd, depth), BF16), shape((count * nd, depth), F32)],
        [turned_neigh, turned_self, inverse, *packs],
        flops=4 * count * nd * hid * depth,
        after=after,
    )


def halving_order(count):
    order = [0]
    step = count // 2
    while step:
        order = order + [d + step for d in order]
        step //= 2
    return order


def back_parts(turned, scaled, self_parts, nd, cs, rs, after):
    depth = scaled[0].shape[1]
    half = rs // 2
    count = len(scaled)
    each = cs // count

    def body(tile_ref, *refs):
        scaled_refs, self_refs = refs[:count], refs[count : 2 * count]
        keep_ref, send_ref, acc = refs[2 * count :]
        i, j = lax.axis_index("row"), lax.axis_index("col")
        z, c = i // 2, lax.rem(i, 2)
        acc[...] = mm(tile_ref[...], jnp.concatenate([r[...] for r in scaled_refs], axis=0))

        @pl.when(i * cs // rs == j)
        def _():
            for r in range(cs):
                q = i * cs - j * rs + (j ^ r)
                place = ((z ^ (q // 2)) + half * (lax.rem(q, 2) ^ c)) * nd
                rows = slice(r % each * nd, (r % each + 1) * nd)
                acc[pl.ds(pl.multiple_of(place, nd), nd), :] += self_refs[r // each][rows]

        for ref, base in ((send_ref, half), (keep_ref, 0)):
            for k, distance in enumerate(halving_order(half)):
                place = (base + distance) * nd
                ref[k] = acc[place : place + nd, :].astype(ref.dtype)

    dims = (half, nd, depth)
    return call(
        body,
        [shape(dims, F32), shape(dims, BF16)],
        [turned, *scaled, *self_parts],
        [pltpu.VMEM((rs * nd, depth), F32)],
        flops=2 * turned.size * depth,
        after=after,
    )


def fold(keep, came, after=()):
    count, rows, width = keep.shape
    half = count // 2

    def body(keep_ref, came_ref, *outs):
        total = keep_ref[...] + came_ref[...].astype(F32)
        if count == 1:
            outs[0][...] = total[0].astype(BF16)
        else:
            outs[0][...] = total[:half]
            outs[1][...] = total[half:].astype(BF16)

    if count == 1:
        return call(body, [shape((rows, width), BF16)], [keep, came], after=after)[0]
    dims = (half, rows, width)
    return call(body, [shape(dims, F32), shape(dims, BF16)], [keep, came], after=after)


def pair_sum(keep, came):
    half, rows, width = keep.shape
    main = rows - EXTRA

    def body(keep_ref, came_ref, *outs):
        for k in range(half):
            total = keep_ref[k] + came_ref[k].astype(F32)
            dtype = outs[k].dtype
            outs[k][:main, :] = total[:main].astype(dtype)
            merged = total[main : main + 8] + total[main + 8 :]
            outs[k][main:, :] = split_pair(merged).astype(dtype)

    return call(
        body,
        [shape((rows, width), BF16 if k else F32) for k in range(half)],
        [keep, came],
    )


def last_sum(parts):
    rows, width = parts[0].shape
    main = rows - EXTRA

    def body(*refs):
        out_ref = refs[-1]
        total = refs[0][...]
        for ref in refs[1:-1]:
            total = total + ref[...].astype(F32)
        out_ref[:main, :] = total[:main].astype(BF16)
        merged = total[main : main + 8] + total[main + 8 :]
        out_ref[main:, :] = split_pair(merged).astype(BF16)

    return call(body, [shape((rows, width), BF16)], parts)[0]


def assemble(pieces, begun, depth, hid, xr, nc, cs, factors, after):
    xw = 2 * depth // cs
    side = cs // 2
    copies = sum(len(where) for _, where, _ in pieces)
    arrays = [array for array, _, _ in pieces]
    inputs = arrays + list(begun)
    weight = shape((depth, hid), F32)

    def body(*refs):
        piece_refs = refs[: len(pieces)]
        self_ref, neigh_ref, bias_ref, staged, sems = refs[-5:]
        i, j = lax.axis_index("row"), lax.axis_index("col")
        z, c = i // 2, lax.rem(i, 2)
        if begun:
            bias_ref[...] = refs[len(inputs) - 1][...]
        else:
            bias_ref[...] = jnp.zeros_like(bias_ref)
        waits = []
        at = 0
        for ref, (_, where, mine) in zip(piece_refs, pieces):
            for t, (distance, column) in enumerate(where):
                owner = j ^ column
                first = owner < side
                q = 2 * (z ^ distance) + (c if mine else 1 - c)
                col = pl.multiple_of(lax.rem(q, nc) * LANES, LANES)
                turn = q // nc
                row = pl.multiple_of(lax.rem(owner, side) * xw + turn * xr, xr)
                scale = jnp.where(first, factors[0], factors[1])
                staged[at] = ref[t, :xr, :].astype(F32) * scale
                for target, here in ((self_ref, first), (neigh_ref, jnp.logical_not(first))):
                    copy = pltpu.make_async_copy(
                        staged.at[at],
                        target.at[pl.ds(row, xr), pl.ds(col, LANES)],
                        sems.at[at],
                    )
                    pl.when(here)(copy.start)
                    waits.append((here, copy))

                @pl.when(turn == 0)
                def _():
                    total = ref[t, xr:, :].astype(F32)
                    total = (total[:1] + total[8:9]) * factors[0]
                    bias_ref[:, pl.ds(col, LANES)] += total

                at += 1
        for here, copy in waits:
            pl.when(here)(copy.wait)

    def run(*refs):
        body(*refs[: len(inputs)], *refs[len(inputs) + len(after) :])

    somewhere = pl.BlockSpec(memory_space=pl.ANY)
    moved = 2 * copies * xr * LANES * 6
    return pl.pallas_call(
        run,
        out_shape=[weight, weight, shape((1, hid), F32)],
        in_specs=[VMEM] * len(arrays)
        + ([somewhere, somewhere, VMEM] if begun else [])
        + [somewhere] * len(after),
        out_specs=[somewhere, somewhere, VMEM],
        scratch_shapes=[
            pltpu.VMEM((copies, xr, LANES), F32),
            pltpu.SemaphoreType.DMA((copies,)),
        ],
        input_output_aliases={len(arrays): 0, len(arrays) + 1: 1} if begun else {},
        compiler_params=limits(arrays, copies * xr * LANES * 4),
        cost_estimate=pl.CostEstimate(flops=0, bytes_accessed=moved, transcendentals=0),
    )(*inputs, *after)


def local(
    features, w_neigh, w_self, bias, cotangent, block_rows, block_cols, block_vals, block_count
):
    rs = lax.axis_size("row")
    cs = lax.axis_size("col")
    nd, depth = features.shape
    hid = w_self.shape[1]
    rt = nd * cs
    half = rs // 2
    xw = 2 * depth // cs
    nc = min(rs, hid // LANES)
    nr = rs // nc
    xr = xw // nr

    def along_col(x, k):
        return lax.ppermute(x, "col", [(s, s ^ k) for s in range(cs)])

    def along_chips(x, k):
        return lax.ppermute(x, "row", [(s, s ^ (2 * k)) for s in range(rs)])

    def other_core(x):
        return lax.ppermute(x, "row", [(s, s ^ 1) for s in range(rs)])

    def gather_chips(x):
        found = {0: x}
        step = half // 2
        while step:
            found.update({d + step: along_chips(found[d], step) for d in list(found)})
            step //= 2
        return [found[d] for d in range(half)]

    if rs == 2 * cs:

        def send_own(block, t):
            pairs = []
            for z in range(half):
                for core in range(2):
                    q = 2 * (z ^ t) + core
                    source = (2 * z + core) * cs + z
                    pairs.append((source, (2 * z + q // cs) * cs + q % cs))
            return lax.ppermute(block, ("row", "col"), pairs)

    else:
        swap = [((b % rs) * cs + b // rs, b) for b in range(rs * cs)]

        def send_own(block, t):
            return lax.ppermute(block, ("row", "col"), swap if t == 0 else [])

    near = along_chips(features, 1)
    mine_first = {0: features, 1: near}
    step = half // 2
    while step > 1:
        evens = [d for d in mine_first if d % 2 == 0]
        mine_first.update({d + step: along_chips(mine_first[d], step) for d in evens})
        step //= 2
    theirs_first = {0: other_core(features), 1: other_core(near)}
    own_feats = {0: send_own(features, 0)}
    tile, turned = densify(
        block_rows.reshape(-1),
        block_cols.reshape(-1),
        block_count.reshape(-1),
        block_vals[0, 0],
        nd,
        rs,
        cs,
        [],
    )
    mine_last = {d + 1: along_chips(x, 1) for d, x in mine_first.items() if d > 1}
    theirs_first.update({d: other_core(x) for d, x in mine_first.items() if d > 1})
    own_feats[1] = send_own(near, 1)

    def placed(mine, theirs):
        places = list(mine) + [half + d for d in theirs]
        return places, [*mine.values(), *theirs.values()]

    begun = forward_first(
        tile, *placed(mine_first, theirs_first), nd, [own_feats[0], own_feats[1]]
    )
    degree = row_sums(tile, nd, cs)
    step = 1
    while step < cs:
        masses = [degree, along_col(degree, step)]
        degree = masses[0] + masses[1]
        step *= 2
    theirs_last = {d: other_core(follow(x, [begun])) for d, x in mine_last.items()}
    evens = {d: send_own(follow(x, [begun, masses[0]]), d) for d, x in mine_first.items() if d > 1}
    own_feats.update(evens)
    own_feats.update({d: send_own(x, d) for d, x in mine_last.items()})
    parts = forward_parts(begun, tile, *placed(mine_last, theirs_last), nd, cs, list(evens.values()))
    own_feat = sum(list(own_feats.values())[1:], own_feats[0])
    inverse = 1.0 / (degree[0] + 1.0)
    inverse = jnp.broadcast_to(inverse[:, None], (rt, LANES))
    own = jnp.dot(own_feat, w_self, preferred_element_type=F32).astype(BF16)

    turned_neigh, turned_self = turn([w_neigh, w_self], [parts[0]])
    parts = [parts[0]] + [along_col(parts[k], k) for k in range(1, cs)]
    output, sums, *packs = activation(
        parts, masses, own, own_feat, w_neigh, bias[None, :], cotangent, [turned_neigh]
    )
    packs = [packs[0]] + [along_col(packs[k], k) for k in range(1, cs)]

    mid = cs // 2
    scaled_args = (inverse, turned_neigh, turned_self, cs, rs)
    early = scaled_parts(packs[:mid], 0, *scaled_args)
    keep, send = weight_parts(packs, sums, rs, xr, nc, early[:1])
    came = other_core(send)
    late = scaled_parts(packs[mid:], mid, *scaled_args, [keep])
    scaled, self_parts = zip(early, late)
    chunks = pair_sum(keep, came)
    chunks = [chunks[0]] + [along_chips(chunks[k], k) for k in range(1, half)]
    line = gather_chips(last_sum(chunks))

    keep, send = back_parts(turned, scaled, self_parts, nd, cs, rs, [keep])
    keep, send = fold(keep, other_core(follow(send, chunks[1:])), line[1:])
    line = stack(line, after=[send])
    step = 1
    while step < half:
        folded = fold(keep, along_chips(send, step))
        keep, send = folded if 2 * step < half else (folded, None)
        step *= 2
    grad_input = keep

    def piece(array, first, column, mine):
        return array, [(first + t, column) for t in range(array.shape[0])], mine

    mid = half // 2
    if cs == 4 and mid:
        first, second = along_col(line, 1), along_col(line, 2)
        near = [(line, 0, 0), (first, 0, 1), (second, 0, 2)]
        rest = [(along_col(first[:mid], 2), 0, 3), (along_col(second[mid:], 1), mid, 3)]
    else:
        near = [(line, 0, 0)] + [(along_col(line, k), 0, k) for k in range(1, cs - 1)]
        rest = [(along_col(line, cs - 1), 0, cs - 1)]
    factor = 1.0 / math.sqrt(nd * rs * cs)
    sizes = (depth, hid, xr, nc, cs, (factor, 32.0 * factor))
    begun = assemble([piece(*x, True) for x in near], (), *sizes, ())
    pieces = [piece(*x, True) for x in rest]
    sent = [(follow(x, begun[2:]) if n == 1 else x, *where) for n, (x, *where) in enumerate(near)]
    pieces += [piece(other_core(x), *where, False) for x, *where in sent + rest]
    total_self, total_neigh, total_bias = assemble(pieces, begun, *sizes, [grad_input])
    return output, grad_input, total_self, total_neigh, total_bias.reshape(-1)


def solution(mesh):
    in_specs = (
        P(("col", "row"), None),
        P(),
        P(),
        P(),
        P(("row", "col"), None),
        P("row", "col", None),
        P("row", "col", None),
        P("row", "col", None, None, None),
        P("row", "col"),
    )
    out_specs = (P(("row", "col"), None), P(("col", "row"), None), P(), P(), P())
    return jax.shard_map(local, mesh=mesh, in_specs=in_specs, out_specs=out_specs, check_vma=False)
```

```python
import math

import jax
import jax.numpy as jnp
from jax import lax
from jax.experimental import pallas as pl
from jax.experimental.pallas import tpu as pltpu
from jax.sharding import PartitionSpec as P

F32 = jnp.float32
BF16 = jnp.bfloat16
LANES = 128
EXTRA = 16
VMEM = pl.BlockSpec(memory_space=pltpu.VMEM)
SMEM = pl.BlockSpec(memory_space=pltpu.SMEM)
MIB = 1024 * 1024


def limits(arrays, scratch=0):
    held = sum(math.prod(a.shape) * a.dtype.itemsize for a in arrays) + scratch
    return pltpu.CompilerParams(vmem_limit_bytes=min(56 * MIB, 2 * held + 12 * MIB))


def call(body, outs, args, scratch=(), smem=0, flops=0, after=()):
    count = len(args)
    moved = sum(math.prod(a.shape) * a.dtype.itemsize for a in (*outs, *args))
    held = sum(math.prod(x.shape) * x.dtype.itemsize for x in scratch)

    def run(*refs):
        body(*refs[:count], *refs[count + len(after) :])

    return pl.pallas_call(
        run,
        out_shape=outs,
        in_specs=[SMEM] * smem
        + [VMEM] * (count - smem)
        + [pl.BlockSpec(memory_space=pl.ANY)] * len(after),
        out_specs=[VMEM] * len(outs),
        scratch_shapes=list(scratch),
        compiler_params=limits([*outs, *args], held),
        cost_estimate=pl.CostEstimate(flops=flops, bytes_accessed=moved, transcendentals=0),
    )(*args, *after)


def shape(dims, dtype):
    return jax.ShapeDtypeStruct(tuple(dims), dtype)


def mm(a, b, ca=1, cb=0):
    return lax.dot_general(a, b, (((ca,), (cb,)), ((), ())), preferred_element_type=F32)


def follow(x, after):
    def body(x_ref, out_ref):
        out_ref[...] = x_ref[...]

    return call(body, [shape(x.shape, x.dtype)], [x], after=after)[0]


def turn(weights, after):
    def body(*refs):
        for ref, out_ref in zip(refs, refs[len(weights) :]):
            out_ref[...] = ref[...].T

    return call(body, [shape(w.shape[::-1], w.dtype) for w in weights], weights, after=after)


def stack(parts, joined=False, after=()):
    count = parts[0].shape[0] if joined else 1

    def body(*refs):
        for k, ref in enumerate(refs[:-1]):
            if joined:
                refs[-1][k * count : (k + 1) * count] = ref[...]
            else:
                refs[-1][k] = ref[...]

    dims = parts[0].shape[1:] if joined else parts[0].shape
    out = shape((len(parts) * count, *dims), parts[0].dtype)
    return call(body, [out], parts, after=after)[0]


def densify(rows, cols, count, values, nd, rs, cs, after):
    rt, ct, half = nd * cs, nd * rs, rs // 2

    def body(rows_ref, cols_ref, count_ref, values_ref, tile_ref, turned_ref, acc):
        i, j = lax.axis_index("row"), lax.axis_index("col")
        z, c = i // 2, lax.rem(i, 2)
        acc[...] = jnp.zeros_like(acc)

        def add(s, carry):
            col = cols_ref[s]
            row = rows_ref[s] ^ j
            col = (z ^ (col // 2)) + half * (lax.rem(col, 2) ^ c)
            r = pl.multiple_of(row * nd, nd)
            c0 = pl.multiple_of(col * nd, nd)
            acc[pl.ds(r, nd), pl.ds(c0, nd)] += values_ref[s].astype(F32)
            return carry

        lax.fori_loop(0, count_ref[0], add, 0)
        tile_ref[...] = acc[...].astype(BF16)
        for k in range(rs):
            cut = acc[:, k * nd : (k + 1) * nd]
            turned_ref[k * nd : (k + 1) * nd, :] = cut.T.astype(BF16)

    return call(
        body,
        [shape((rt, ct), BF16), shape((ct, rt), BF16)],
        [rows, cols, count, values],
        [pltpu.VMEM((rt, ct), F32)],
        smem=3,
        flops=rt * ct,
        after=after,
    )


def tile_columns(tile_ref, places, nd):
    return jnp.concatenate([tile_ref[:, p * nd : (p + 1) * nd] for p in places], axis=1)


def row_sums(tile, nd, cs):
    rt, ct = tile.shape

    def body(tile_ref, mass_ref):
        j = lax.axis_index("col")
        ones = jnp.ones((8, ct), BF16)
        for k in range(cs):
            place = pl.multiple_of((j ^ k) * nd, nd)
            mass_ref[:, pl.ds(place, nd)] = mm(ones, tile_ref[k * nd : (k + 1) * nd, :], 1, 1)

    return call(body, [shape((8, rt), F32)], [tile], flops=16 * tile.size)[0]


def forward_first(tile, places, blocks, nd, after):
    rt = tile.shape[0]
    width = blocks[0].shape[1]

    def body(*refs):
        tile_ref, feat_refs = refs[0], refs[1 : 1 + len(blocks)]
        sum_ref = refs[1 + len(blocks)]
        feats = jnp.concatenate([r[...] for r in feat_refs], axis=0)
        sum_ref[...] = mm(tile_columns(tile_ref, places, nd), feats)

    return call(
        body,
        [shape((rt, width), F32)],
        [tile, *blocks],
        flops=2 * rt * len(places) * nd * width,
        after=after,
    )[0]


def forward_parts(begun, tile, places, blocks, nd, cs, after):
    width = blocks[0].shape[1]

    def body(*refs):
        sum_ref, tile_ref, feat_refs = refs[0], refs[1], refs[2 : 2 + len(blocks)]
        outs = refs[2 + len(blocks) :]
        feats = jnp.concatenate([r[...] for r in feat_refs], axis=0)
        parts = sum_ref[...] + mm(tile_columns(tile_ref, places, nd), feats)
        for k in range(cs):
            outs[k][...] = parts[k * nd : (k + 1) * nd].astype(outs[k].dtype)

    return call(
        body,
        [shape((nd, width), BF16 if k else F32) for k in range(cs)],
        [begun, tile, *blocks],
        flops=2 * tile.shape[0] * len(places) * nd * width,
        after=after,
    )


def activation(parts, masses, own, own_feat, w_neigh, bias, cotangent, after):
    cs = len(parts)
    nd, hid = own.shape
    depth = own_feat.shape[1]
    xw = 2 * depth // cs

    def body(*refs):
        part_refs = refs[:cs]
        mass_refs = refs[cs : cs + 2]
        own_ref, feat_ref, w_ref, bias_ref, cot_ref = refs[cs + 2 : cs + 7]
        out_ref, sum_ref, *packs = refs[cs + 7 : -1]
        both = refs[-1]
        j = lax.axis_index("col")
        here = pl.ds(pl.multiple_of(j * nd, nd), nd)
        inv = 1.0 / (mass_refs[0][:, here] + mass_refs[1][:, here] + 1.0)
        inv = jnp.broadcast_to(inv.T[:, :1], (nd, LANES))
        total = sum(r[...].astype(F32) for r in part_refs)
        mean = (total * jnp.concatenate([inv] * (depth // LANES), axis=1)).astype(BF16)
        both[:, :depth] = feat_ref[...]
        both[:, depth:] = mean
        pre = own_ref[...].astype(F32) + mm(mean, w_ref[...]) + bias_ref[...]
        slope = jnp.where(pre > 0, 1.0, jnp.exp(jnp.minimum(pre, 0.0)))
        out_ref[...] = jnp.where(pre > 0, pre, slope - 1.0).astype(BF16)
        grad = cot_ref[...].astype(F32) * slope
        sum_ref[...] = jnp.broadcast_to(jnp.sum(grad, axis=0, keepdims=True), (8, hid))
        grad = grad.astype(BF16)
        for k in range(cs):
            packs[k][:, :hid] = grad
            target = j ^ k
            if xw % LANES == 0:
                start = pl.multiple_of(target * xw, LANES)
                packs[k][:, hid:] = both[:, pl.ds(start, xw)]
            else:
                for d in range(cs):

                    @pl.when(target == d)
                    def _():
                        packs[k][:, hid:] = both[:, d * xw : (d + 1) * xw]

    return call(
        body,
        [shape((nd, hid), BF16), shape((8, hid), F32)] + [shape((nd, hid + xw), BF16)] * cs,
        [*parts, *masses, own, own_feat, w_neigh, bias, cotangent],
        [pltpu.VMEM((nd, 2 * depth), BF16)],
        flops=2 * own_feat.size * hid,
        after=after,
    )


def split_pair(total):
    high = total.astype(BF16).astype(F32)
    return jnp.concatenate([high, total - high], axis=0)


def weight_parts(packs, sums, rs, xr, nc):
    cs = len(packs)
    hid = sums.shape[1]
    nd, xw = packs[0].shape[0], packs[0].shape[1] - hid
    half = rs // 2

    def body(*refs):
        pack_refs = refs[:cs]
        sum_ref, keep_ref, send_ref, acc = refs[cs:]
        x_all = jnp.concatenate([r[:, hid:] for r in pack_refs], axis=0)
        g_all = jnp.concatenate([r[:, :hid] for r in pack_refs], axis=0)
        acc[...] = mm(x_all, g_all, 0, 0)
        i = lax.axis_index("row")
        z, c = i // 2, lax.rem(i, 2)
        for k in range(half):
            for core, ref in ((c, keep_ref), (1 - c, send_ref)):
                q = 2 * (z ^ k) + core
                row = pl.multiple_of((q // nc) * xr, xr)
                col = pl.multiple_of(lax.rem(q, nc) * LANES, LANES)
                ref[k, :xr, :] = acc[pl.ds(row, xr), pl.ds(col, LANES)].astype(ref.dtype)
                ref[k, xr:, :] = split_pair(sum_ref[:, pl.ds(col, LANES)]).astype(ref.dtype)

    dims = (half, xr + EXTRA, LANES)
    return call(
        body,
        [shape(dims, F32), shape(dims, BF16)],
        [*packs, sums],
        [pltpu.VMEM((xw, hid), F32)],
        flops=2 * cs * nd * xw * hid,
    )


def scaled_parts(packs, inverse, turned_neigh, turned_self, rs, after):
    cs = len(packs)
    nd = packs[0].shape[0]
    hid, depth = turned_neigh.shape

    def body(neigh_ref, own_ref, inv_ref, *refs):
        pack_refs, scaled_ref, self_ref = refs[:cs], refs[cs], refs[cs + 1]
        i, j = lax.axis_index("row"), lax.axis_index("col")
        grads = jnp.concatenate([r[:, :hid] for r in pack_refs], axis=0)
        product = mm(grads, neigh_ref[...])
        for r in range(cs):
            inv = inv_ref[pl.ds(pl.multiple_of((j ^ r) * nd, nd), nd), :]
            inv = jnp.concatenate([inv] * (depth // LANES), axis=1)
            rows = slice(r * nd, (r + 1) * nd)
            scaled_ref[rows, :] = (product[rows] * inv).astype(BF16)

        @pl.when(i * cs // rs == j)
        def _():
            self_ref[...] = mm(grads, own_ref[...])

    return call(
        body,
        [shape((cs * nd, depth), BF16), shape((cs * nd, depth), F32)],
        [turned_neigh, turned_self, inverse, *packs],
        flops=4 * cs * nd * hid * depth,
        after=after,
    )


def halving_order(count):
    order = [0]
    step = count // 2
    while step:
        order = order + [d + step for d in order]
        step //= 2
    return order


def back_parts(turned, scaled, self_part, nd, cs, rs, after):
    depth = scaled.shape[1]
    half = rs // 2

    def body(tile_ref, scaled_ref, self_ref, keep_ref, send_ref, acc):
        i, j = lax.axis_index("row"), lax.axis_index("col")
        z, c = i // 2, lax.rem(i, 2)
        acc[...] = mm(tile_ref[...], scaled_ref[...])

        @pl.when(i * cs // rs == j)
        def _():
            for r in range(cs):
                q = i * cs - j * rs + (j ^ r)
                place = ((z ^ (q // 2)) + half * (lax.rem(q, 2) ^ c)) * nd
                acc[pl.ds(pl.multiple_of(place, nd), nd), :] += self_ref[r * nd : (r + 1) * nd]

        for ref, base in ((send_ref, half), (keep_ref, 0)):
            for k, distance in enumerate(halving_order(half)):
                place = (base + distance) * nd
                ref[k] = acc[place : place + nd, :].astype(ref.dtype)

    dims = (half, nd, depth)
    return call(
        body,
        [shape(dims, F32), shape(dims, BF16)],
        [turned, scaled, self_part],
        [pltpu.VMEM((rs * nd, depth), F32)],
        flops=2 * turned.size * depth,
        after=after,
    )


def fold(keep, came, after=()):
    count, rows, width = keep.shape
    half = count // 2

    def body(keep_ref, came_ref, *outs):
        total = keep_ref[...] + came_ref[...].astype(F32)
        if count == 1:
            outs[0][...] = total[0].astype(BF16)
        else:
            outs[0][...] = total[:half]
            outs[1][...] = total[half:].astype(BF16)

    if count == 1:
        return call(body, [shape((rows, width), BF16)], [keep, came], after=after)[0]
    dims = (half, rows, width)
    return call(body, [shape(dims, F32), shape(dims, BF16)], [keep, came], after=after)


def pair_sum(keep, came):
    half, rows, width = keep.shape
    main = rows - EXTRA

    def body(keep_ref, came_ref, *outs):
        for k in range(half):
            total = keep_ref[k] + came_ref[k].astype(F32)
            dtype = outs[k].dtype
            outs[k][:main, :] = total[:main].astype(dtype)
            merged = total[main : main + 8] + total[main + 8 :]
            outs[k][main:, :] = split_pair(merged).astype(dtype)

    return call(
        body,
        [shape((rows, width), BF16 if k else F32) for k in range(half)],
        [keep, came],
    )


def last_sum(parts):
    rows, width = parts[0].shape
    main = rows - EXTRA

    def body(*refs):
        out_ref = refs[-1]
        total = refs[0][...]
        for ref in refs[1:-1]:
            total = total + ref[...].astype(F32)
        out_ref[:main, :] = total[:main].astype(BF16)
        merged = total[main : main + 8] + total[main + 8 :]
        out_ref[main:, :] = split_pair(merged).astype(BF16)

    return call(body, [shape((rows, width), BF16)], parts)[0]


def assemble(pieces, begun, depth, hid, xr, nc, cs, factors, after):
    xw = 2 * depth // cs
    side = cs // 2
    copies = sum(len(where) for _, where, _ in pieces)
    arrays = [array for array, _, _ in pieces]
    inputs = arrays + list(begun)
    weight = shape((depth, hid), F32)

    def body(*refs):
        piece_refs = refs[: len(pieces)]
        self_ref, neigh_ref, bias_ref, staged, sems = refs[-5:]
        i, j = lax.axis_index("row"), lax.axis_index("col")
        z, c = i // 2, lax.rem(i, 2)
        if begun:
            bias_ref[...] = refs[len(inputs) - 1][...]
        else:
            bias_ref[...] = jnp.zeros_like(bias_ref)
        waits = []
        at = 0
        for ref, (_, where, mine) in zip(piece_refs, pieces):
            for t, (distance, column) in enumerate(where):
                owner = j ^ column
                first = owner < side
                q = 2 * (z ^ distance) + (c if mine else 1 - c)
                col = pl.multiple_of(lax.rem(q, nc) * LANES, LANES)
                turn = q // nc
                row = pl.multiple_of(lax.rem(owner, side) * xw + turn * xr, xr)
                scale = jnp.where(first, factors[0], factors[1])
                staged[at] = ref[t, :xr, :].astype(F32) * scale
                for target, here in ((self_ref, first), (neigh_ref, jnp.logical_not(first))):
                    copy = pltpu.make_async_copy(
                        staged.at[at],
                        target.at[pl.ds(row, xr), pl.ds(col, LANES)],
                        sems.at[at],
                    )
                    pl.when(here)(copy.start)
                    waits.append((here, copy))

                @pl.when(turn == 0)
                def _():
                    total = ref[t, xr:, :].astype(F32)
                    total = (total[:1] + total[8:9]) * factors[0]
                    bias_ref[:, pl.ds(col, LANES)] += total

                at += 1
        for here, copy in waits:
            pl.when(here)(copy.wait)

    def run(*refs):
        body(*refs[: len(inputs)], *refs[len(inputs) + len(after) :])

    somewhere = pl.BlockSpec(memory_space=pl.ANY)
    moved = 2 * copies * xr * LANES * 6
    return pl.pallas_call(
        run,
        out_shape=[weight, weight, shape((1, hid), F32)],
        in_specs=[VMEM] * len(arrays)
        + ([somewhere, somewhere, VMEM] if begun else [])
        + [somewhere] * len(after),
        out_specs=[somewhere, somewhere, VMEM],
        scratch_shapes=[
            pltpu.VMEM((copies, xr, LANES), F32),
            pltpu.SemaphoreType.DMA((copies,)),
        ],
        input_output_aliases={len(arrays): 0, len(arrays) + 1: 1} if begun else {},
        compiler_params=limits(arrays, copies * xr * LANES * 4),
        cost_estimate=pl.CostEstimate(flops=0, bytes_accessed=moved, transcendentals=0),
    )(*inputs, *after)


def local(
    features, w_neigh, w_self, bias, cotangent, block_rows, block_cols, block_vals, block_count
):
    rs = lax.axis_size("row")
    cs = lax.axis_size("col")
    nd, depth = features.shape
    hid = w_self.shape[1]
    rt = nd * cs
    half = rs // 2
    xw = 2 * depth // cs
    nc = min(rs, hid // LANES)
    nr = rs // nc
    xr = xw // nr

    def along_col(x, k):
        return lax.ppermute(x, "col", [(s, s ^ k) for s in range(cs)])

    def along_chips(x, k):
        return lax.ppermute(x, "row", [(s, s ^ (2 * k)) for s in range(rs)])

    def other_core(x):
        return lax.ppermute(x, "row", [(s, s ^ 1) for s in range(rs)])

    def gather_chips(x):
        found = {0: x}
        step = half // 2
        while step:
            found.update({d + step: along_chips(found[d], step) for d in list(found)})
            step //= 2
        return [found[d] for d in range(half)]

    if rs == 2 * cs:

        def send_own(block, t):
            pairs = []
            for z in range(half):
                for core in range(2):
                    q = 2 * (z ^ t) + core
                    source = (2 * z + core) * cs + z
                    pairs.append((source, (2 * z + q // cs) * cs + q % cs))
            return lax.ppermute(block, ("row", "col"), pairs)

    else:
        swap = [((b % rs) * cs + b // rs, b) for b in range(rs * cs)]

        def send_own(block, t):
            return lax.ppermute(block, ("row", "col"), swap if t == 0 else [])

    near = along_chips(features, 1)
    mine_first = {0: features, 1: near}
    step = half // 2
    while step > 1:
        evens = [d for d in mine_first if d % 2 == 0]
        mine_first.update({d + step: along_chips(mine_first[d], step) for d in evens})
        step //= 2
    theirs_first = {0: other_core(features), 1: other_core(near)}
    own_feats = {0: send_own(features, 0)}
    tile, turned = densify(
        block_rows.reshape(-1),
        block_cols.reshape(-1),
        block_count.reshape(-1),
        block_vals[0, 0],
        nd,
        rs,
        cs,
        [],
    )
    mine_last = {d + 1: along_chips(x, 1) for d, x in mine_first.items() if d > 1}
    theirs_first.update({d: other_core(x) for d, x in mine_first.items() if d > 1})
    theirs_last = {d: other_core(x) for d, x in mine_last.items()}
    own_feats[1] = send_own(near, 1)

    def placed(mine, theirs):
        places = list(mine) + [half + d for d in theirs]
        return places, [*mine.values(), *theirs.values()]

    begun = forward_first(
        tile, *placed(mine_first, theirs_first), nd, [own_feats[0], own_feats[1]]
    )
    degree = row_sums(tile, nd, cs)
    step = 1
    while step < cs:
        masses = [degree, along_col(degree, step)]
        degree = masses[0] + masses[1]
        step *= 2
    evens = {d: send_own(follow(x, [begun, masses[0]]), d) for d, x in mine_first.items() if d > 1}
    own_feats.update(evens)
    own_feats.update({d: send_own(x, d) for d, x in mine_last.items()})
    parts = forward_parts(begun, tile, *placed(mine_last, theirs_last), nd, cs, list(evens.values()))
    own_feat = sum(list(own_feats.values())[1:], own_feats[0])
    inverse = 1.0 / (degree[0] + 1.0)
    inverse = jnp.broadcast_to(inverse[:, None], (rt, LANES))
    own = jnp.dot(own_feat, w_self, preferred_element_type=F32).astype(BF16)

    turned_neigh, turned_self = turn([w_neigh, w_self], [parts[0]])
    parts = [parts[0]] + [along_col(parts[k], k) for k in range(cs - 1, 0, -1)]
    output, sums, *packs = activation(
        parts, masses, own, own_feat, w_neigh, bias[None, :], cotangent, [turned_neigh]
    )
    packs = [packs[0]] + [along_col(packs[k], k) for k in range(cs - 1, 0, -1)]

    keep, send = weight_parts(packs, sums, rs, xr, nc)
    packs = [packs[0]] + packs[:0:-1]
    came = other_core(send)
    scaled, self_part = scaled_parts(packs, inverse, turned_neigh, turned_self, rs, [keep])
    chunks = pair_sum(keep, came)
    chunks = [chunks[0]] + [along_chips(chunks[k], k) for k in range(half - 1, 0, -1)]
    line = gather_chips(last_sum(chunks))

    keep, send = back_parts(turned, scaled, self_part, nd, cs, rs, [keep])
    keep, send = fold(keep, other_core(follow(send, chunks[1:])), line[1:])
    line = stack(line, after=[send])
    step = 1
    while step < half:
        folded = fold(keep, along_chips(send, step))
        keep, send = folded if 2 * step < half else (folded, None)
        step *= 2
    grad_input = keep

    def piece(array, first, column, mine):
        return array, [(first + t, column) for t in range(array.shape[0])], mine

    mid = half // 2
    if cs == 4 and mid:
        first, second = along_col(line, 1), along_col(line, 2)
        near = [(line, 0, 0), (first, 0, 1), (second, 0, 2)]
        rest = [(along_col(first[:mid], 2), 0, 3), (along_col(second[mid:], 1), mid, 3)]
    else:
        near = [(line, 0, 0)] + [(along_col(line, k), 0, k) for k in range(1, cs - 1)]
        rest = [(along_col(line, cs - 1), 0, cs - 1)]
    factor = 1.0 / math.sqrt(nd * rs * cs)
    sizes = (depth, hid, xr, nc, cs, (factor, 32.0 * factor))
    begun = assemble([piece(*x, True) for x in near + rest], (), *sizes, ())
    pieces = [piece(other_core(x), *where, False) for x, *where in near + rest]
    total_self, total_neigh, total_bias = assemble(pieces, begun, *sizes, [grad_input])
    return output, grad_input, total_self, total_neigh, total_bias.reshape(-1)


def solution(mesh):
    in_specs = (
        P(("col", "row"), None),
        P(),
        P(),
        P(),
        P(("row", "col"), None),
        P("row", "col", None),
        P("row", "col", None),
        P("row", "col", None, None, None),
        P("row", "col"),
    )
    out_specs = (P(("row", "col"), None), P(("col", "row"), None), P(), P(), P())
    return jax.shard_map(local, mesh=mesh, in_specs=in_specs, out_specs=out_specs, check_vma=False)
```

```python
import math

import jax
import jax.numpy as jnp
from jax import lax
from jax.experimental import pallas as pl
from jax.experimental.pallas import tpu as pltpu
from jax.sharding import PartitionSpec as P

F32 = jnp.float32
BF16 = jnp.bfloat16
LANES = 128
EXTRA = 16
VMEM = pl.BlockSpec(memory_space=pltpu.VMEM)
SMEM = pl.BlockSpec(memory_space=pltpu.SMEM)
MIB = 1024 * 1024


def limits(arrays, scratch=0):
    held = sum(math.prod(a.shape) * a.dtype.itemsize for a in arrays) + scratch
    return pltpu.CompilerParams(vmem_limit_bytes=min(56 * MIB, 2 * held + 12 * MIB))


def call(body, outs, args, scratch=(), smem=0, flops=0, after=()):
    count = len(args)
    moved = sum(math.prod(a.shape) * a.dtype.itemsize for a in (*outs, *args))
    held = sum(math.prod(x.shape) * x.dtype.itemsize for x in scratch)

    def run(*refs):
        body(*refs[:count], *refs[count + len(after) :])

    return pl.pallas_call(
        run,
        out_shape=outs,
        in_specs=[SMEM] * smem
        + [VMEM] * (count - smem)
        + [pl.BlockSpec(memory_space=pl.ANY)] * len(after),
        out_specs=[VMEM] * len(outs),
        scratch_shapes=list(scratch),
        compiler_params=limits([*outs, *args], held),
        cost_estimate=pl.CostEstimate(flops=flops, bytes_accessed=moved, transcendentals=0),
    )(*args, *after)


def shape(dims, dtype):
    return jax.ShapeDtypeStruct(tuple(dims), dtype)


def mm(a, b, ca=1, cb=0):
    return lax.dot_general(a, b, (((ca,), (cb,)), ((), ())), preferred_element_type=F32)


def follow(x, after):
    def body(x_ref, out_ref):
        out_ref[...] = x_ref[...]

    return call(body, [shape(x.shape, x.dtype)], [x], after=after)[0]


def turn(weights, after):
    def body(*refs):
        for ref, out_ref in zip(refs, refs[len(weights) :]):
            out_ref[...] = ref[...].T

    return call(body, [shape(w.shape[::-1], w.dtype) for w in weights], weights, after=after)


def stack(parts, joined=False, after=()):
    count = parts[0].shape[0] if joined else 1

    def body(*refs):
        for k, ref in enumerate(refs[:-1]):
            if joined:
                refs[-1][k * count : (k + 1) * count] = ref[...]
            else:
                refs[-1][k] = ref[...]

    dims = parts[0].shape[1:] if joined else parts[0].shape
    out = shape((len(parts) * count, *dims), parts[0].dtype)
    return call(body, [out], parts, after=after)[0]


def densify(rows, cols, count, values, nd, rs, cs, after):
    rt, ct, half = nd * cs, nd * rs, rs // 2

    def body(rows_ref, cols_ref, count_ref, values_ref, tile_ref, turned_ref, acc):
        i, j = lax.axis_index("row"), lax.axis_index("col")
        z, c = i // 2, lax.rem(i, 2)
        acc[...] = jnp.zeros_like(acc)

        def add(s, carry):
            col = cols_ref[s]
            row = rows_ref[s] ^ j
            col = (z ^ (col // 2)) + half * (lax.rem(col, 2) ^ c)
            r = pl.multiple_of(row * nd, nd)
            c0 = pl.multiple_of(col * nd, nd)
            acc[pl.ds(r, nd), pl.ds(c0, nd)] += values_ref[s].astype(F32)
            return carry

        lax.fori_loop(0, count_ref[0], add, 0)
        tile_ref[...] = acc[...].astype(BF16)
        for k in range(rs):
            cut = acc[:, k * nd : (k + 1) * nd]
            turned_ref[k * nd : (k + 1) * nd, :] = cut.T.astype(BF16)

    return call(
        body,
        [shape((rt, ct), BF16), shape((ct, rt), BF16)],
        [rows, cols, count, values],
        [pltpu.VMEM((rt, ct), F32)],
        smem=3,
        flops=rt * ct,
        after=after,
    )


def tile_columns(tile_ref, places, nd):
    return jnp.concatenate([tile_ref[:, p * nd : (p + 1) * nd] for p in places], axis=1)


def row_sums(tile, nd, cs):
    rt, ct = tile.shape

    def body(tile_ref, mass_ref):
        j = lax.axis_index("col")
        ones = jnp.ones((8, ct), BF16)
        for k in range(cs):
            place = pl.multiple_of((j ^ k) * nd, nd)
            mass_ref[:, pl.ds(place, nd)] = mm(ones, tile_ref[k * nd : (k + 1) * nd, :], 1, 1)

    return call(body, [shape((8, rt), F32)], [tile], flops=16 * tile.size)[0]


def forward_first(tile, places, blocks, nd, after):
    rt = tile.shape[0]
    width = blocks[0].shape[1]

    def body(*refs):
        tile_ref, feat_refs = refs[0], refs[1 : 1 + len(blocks)]
        sum_ref = refs[1 + len(blocks)]
        feats = jnp.concatenate([r[...] for r in feat_refs], axis=0)
        sum_ref[...] = mm(tile_columns(tile_ref, places, nd), feats)

    return call(
        body,
        [shape((rt, width), F32)],
        [tile, *blocks],
        flops=2 * rt * len(places) * nd * width,
        after=after,
    )[0]


def forward_parts(begun, tile, places, blocks, nd, cs, after):
    width = blocks[0].shape[1]

    def body(*refs):
        sum_ref, tile_ref, feat_refs = refs[0], refs[1], refs[2 : 2 + len(blocks)]
        outs = refs[2 + len(blocks) :]
        feats = jnp.concatenate([r[...] for r in feat_refs], axis=0)
        parts = sum_ref[...] + mm(tile_columns(tile_ref, places, nd), feats)
        for k in range(cs):
            outs[k][...] = parts[k * nd : (k + 1) * nd].astype(outs[k].dtype)

    return call(
        body,
        [shape((nd, width), BF16 if k else F32) for k in range(cs)],
        [begun, tile, *blocks],
        flops=2 * tile.shape[0] * len(places) * nd * width,
        after=after,
    )


def activation(parts, masses, own, own_feat, w_neigh, bias, cotangent, after):
    cs = len(parts)
    nd, hid = own.shape
    depth = own_feat.shape[1]
    xw = 2 * depth // cs

    def body(*refs):
        part_refs = refs[:cs]
        mass_refs = refs[cs : cs + 2]
        own_ref, feat_ref, w_ref, bias_ref, cot_ref = refs[cs + 2 : cs + 7]
        out_ref, sum_ref, *packs = refs[cs + 7 : -1]
        both = refs[-1]
        j = lax.axis_index("col")
        here = pl.ds(pl.multiple_of(j * nd, nd), nd)
        inv = 1.0 / (mass_refs[0][:, here] + mass_refs[1][:, here] + 1.0)
        inv = jnp.broadcast_to(inv.T[:, :1], (nd, LANES))
        total = sum(r[...].astype(F32) for r in part_refs)
        mean = (total * jnp.concatenate([inv] * (depth // LANES), axis=1)).astype(BF16)
        both[:, :depth] = feat_ref[...]
        both[:, depth:] = mean
        pre = own_ref[...].astype(F32) + mm(mean, w_ref[...]) + bias_ref[...]
        slope = jnp.where(pre > 0, 1.0, jnp.exp(jnp.minimum(pre, 0.0)))
        out_ref[...] = jnp.where(pre > 0, pre, slope - 1.0).astype(BF16)
        grad = cot_ref[...].astype(F32) * slope
        sum_ref[...] = jnp.broadcast_to(jnp.sum(grad, axis=0, keepdims=True), (8, hid))
        grad = grad.astype(BF16)
        for k in range(cs):
            packs[k][:, :hid] = grad
            target = j ^ k
            if xw % LANES == 0:
                start = pl.multiple_of(target * xw, LANES)
                packs[k][:, hid:] = both[:, pl.ds(start, xw)]
            else:
                for d in range(cs):

                    @pl.when(target == d)
                    def _():
                        packs[k][:, hid:] = both[:, d * xw : (d + 1) * xw]

    return call(
        body,
        [shape((nd, hid), BF16), shape((8, hid), F32)] + [shape((nd, hid + xw), BF16)] * cs,
        [*parts, *masses, own, own_feat, w_neigh, bias, cotangent],
        [pltpu.VMEM((nd, 2 * depth), BF16)],
        flops=2 * own_feat.size * hid,
        after=after,
    )


def split_pair(total):
    high = total.astype(BF16).astype(F32)
    return jnp.concatenate([high, total - high], axis=0)


def weight_parts(packs, sums, rs, xr, nc, after):
    cs = len(packs)
    hid = sums.shape[1]
    nd, xw = packs[0].shape[0], packs[0].shape[1] - hid
    half = rs // 2

    def body(*refs):
        pack_refs = refs[:cs]
        sum_ref, keep_ref, send_ref, acc = refs[cs:]
        x_all = jnp.concatenate([r[:, hid:] for r in pack_refs], axis=0)
        g_all = jnp.concatenate([r[:, :hid] for r in pack_refs], axis=0)
        acc[...] = mm(x_all, g_all, 0, 0)
        i = lax.axis_index("row")
        z, c = i // 2, lax.rem(i, 2)
        for k in range(half):
            for core, ref in ((c, keep_ref), (1 - c, send_ref)):
                q = 2 * (z ^ k) + core
                row = pl.multiple_of((q // nc) * xr, xr)
                col = pl.multiple_of(lax.rem(q, nc) * LANES, LANES)
                ref[k, :xr, :] = acc[pl.ds(row, xr), pl.ds(col, LANES)].astype(ref.dtype)
                ref[k, xr:, :] = split_pair(sum_ref[:, pl.ds(col, LANES)]).astype(ref.dtype)

    dims = (half, xr + EXTRA, LANES)
    return call(
        body,
        [shape(dims, F32), shape(dims, BF16)],
        [*packs, sums],
        [pltpu.VMEM((xw, hid), F32)],
        flops=2 * cs * nd * xw * hid,
        after=after,
    )


def scaled_parts(packs, first, inverse, turned_neigh, turned_self, cs, rs, after=()):
    count = len(packs)
    nd = packs[0].shape[0]
    hid, depth = turned_neigh.shape

    def body(neigh_ref, own_ref, inv_ref, *refs):
        pack_refs, scaled_ref, self_ref = refs[:count], refs[count], refs[count + 1]
        i, j = lax.axis_index("row"), lax.axis_index("col")
        grads = jnp.concatenate([r[:, :hid] for r in pack_refs], axis=0)
        product = mm(grads, neigh_ref[...])
        for r in range(count):
            start = pl.multiple_of((j ^ (first + r)) * nd, nd)
            inv = inv_ref[pl.ds(start, nd), :]
            inv = jnp.concatenate([inv] * (depth // LANES), axis=1)
            rows = slice(r * nd, (r + 1) * nd)
            scaled_ref[rows, :] = (product[rows] * inv).astype(BF16)

        @pl.when(i * cs // rs == j)
        def _():
            self_ref[...] = mm(grads, own_ref[...])

    return call(
        body,
        [shape((count * nd, depth), BF16), shape((count * nd, depth), F32)],
        [turned_neigh, turned_self, inverse, *packs],
        flops=4 * count * nd * hid * depth,
        after=after,
    )


def halving_order(count):
    order = [0]
    step = count // 2
    while step:
        order = order + [d + step for d in order]
        step //= 2
    return order


def back_parts(turned, scaled, self_parts, nd, cs, rs, after):
    depth = scaled[0].shape[1]
    half = rs // 2
    count = len(scaled)
    each = cs // count

    def body(tile_ref, *refs):
        scaled_refs, self_refs = refs[:count], refs[count : 2 * count]
        keep_ref, send_ref, acc = refs[2 * count :]
        i, j = lax.axis_index("row"), lax.axis_index("col")
        z, c = i // 2, lax.rem(i, 2)
        acc[...] = mm(tile_ref[...], jnp.concatenate([r[...] for r in scaled_refs], axis=0))

        @pl.when(i * cs // rs == j)
        def _():
            for r in range(cs):
                q = i * cs - j * rs + (j ^ r)
                place = ((z ^ (q // 2)) + half * (lax.rem(q, 2) ^ c)) * nd
                rows = slice(r % each * nd, (r % each + 1) * nd)
                acc[pl.ds(pl.multiple_of(place, nd), nd), :] += self_refs[r // each][rows]

        for ref, base in ((send_ref, half), (keep_ref, 0)):
            for k, distance in enumerate(halving_order(half)):
                place = (base + distance) * nd
                ref[k] = acc[place : place + nd, :].astype(ref.dtype)

    dims = (half, nd, depth)
    return call(
        body,
        [shape(dims, F32), shape(dims, BF16)],
        [turned, *scaled, *self_parts],
        [pltpu.VMEM((rs * nd, depth), F32)],
        flops=2 * turned.size * depth,
        after=after,
    )


def fold(keep, came, after=()):
    count, rows, width = keep.shape
    half = count // 2

    def body(keep_ref, came_ref, *outs):
        total = keep_ref[...] + came_ref[...].astype(F32)
        outs[0][...] = total[:half]
        outs[1][...] = total[half:].astype(BF16)

    dims = (half, rows, width)
    return call(body, [shape(dims, F32), shape(dims, BF16)], [keep, came], after=after)


def pair_sum(keep, came):
    half, rows, width = keep.shape
    main = rows - EXTRA

    def body(keep_ref, came_ref, *outs):
        for k in range(half):
            total = keep_ref[k] + came_ref[k].astype(F32)
            dtype = outs[k].dtype
            outs[k][:main, :] = total[:main].astype(dtype)
            merged = total[main : main + 8] + total[main + 8 :]
            outs[k][main:, :] = split_pair(merged).astype(dtype)

    return call(
        body,
        [shape((rows, width), BF16 if k else F32) for k in range(half)],
        [keep, came],
    )


def last_sum(parts):
    rows, width = parts[0].shape
    main = rows - EXTRA

    def body(*refs):
        out_ref = refs[-1]
        total = refs[0][...]
        for ref in refs[1:-1]:
            total = total + ref[...].astype(F32)
        out_ref[:main, :] = total[:main].astype(BF16)
        merged = total[main : main + 8] + total[main + 8 :]
        out_ref[main:, :] = split_pair(merged).astype(BF16)

    return call(body, [shape((rows, width), BF16)], parts)[0]


def assemble(pieces, begun, depth, hid, xr, nc, cs, factors, after, adds=()):
    xw = 2 * depth // cs
    side = cs // 2
    copies = sum(len(where) for _, where, _ in pieces)
    arrays = [array for array, _, _ in pieces]
    inputs = arrays + list(begun) + list(adds)
    weight = shape((depth, hid), F32)

    def body(*refs):
        piece_refs = refs[: len(pieces)]
        self_ref, neigh_ref, bias_ref, *sum_ref, staged, sems = refs[len(inputs) :]
        i, j = lax.axis_index("row"), lax.axis_index("col")
        z, c = i // 2, lax.rem(i, 2)
        if begun:
            bias_ref[...] = refs[len(arrays) + 2][...]
        else:
            bias_ref[...] = jnp.zeros_like(bias_ref)
        waits = []
        at = 0
        for ref, (_, where, mine) in zip(piece_refs, pieces):
            for t, (distance, column) in enumerate(where):
                owner = j ^ column
                first = owner < side
                q = 2 * (z ^ distance) + (c if mine else 1 - c)
                col = pl.multiple_of(lax.rem(q, nc) * LANES, LANES)
                turn = q // nc
                row = pl.multiple_of(lax.rem(owner, side) * xw + turn * xr, xr)
                scale = jnp.where(first, factors[0], factors[1])
                staged[at] = ref[t, :xr, :].astype(F32) * scale
                for target, here in ((self_ref, first), (neigh_ref, jnp.logical_not(first))):
                    copy = pltpu.make_async_copy(
                        staged.at[at],
                        target.at[pl.ds(row, xr), pl.ds(col, LANES)],
                        sems.at[at],
                    )
                    pl.when(here)(copy.start)
                    waits.append((here, copy))

                @pl.when(turn == 0)
                def _():
                    total = ref[t, xr:, :].astype(F32)
                    total = (total[:1] + total[8:9]) * factors[0]
                    bias_ref[:, pl.ds(col, LANES)] += total

                at += 1
        if adds:
            keep_ref, came_ref = refs[len(inputs) - 2 : len(inputs)]
            sum_ref[0][...] = (keep_ref[0] + came_ref[0].astype(F32)).astype(BF16)
        for here, copy in waits:
            pl.when(here)(copy.wait)

    def run(*refs):
        body(*refs[: len(inputs)], *refs[len(inputs) + len(after) :])

    somewhere = pl.BlockSpec(memory_space=pl.ANY)
    sums = [shape(adds[0].shape[1:], BF16)] if adds else []
    moved = 2 * copies * xr * LANES * 6
    return pl.pallas_call(
        run,
        out_shape=[weight, weight, shape((1, hid), F32), *sums],
        in_specs=[VMEM] * len(arrays)
        + ([somewhere, somewhere, VMEM] if begun else [])
        + [VMEM] * len(adds)
        + [somewhere] * len(after),
        out_specs=[somewhere, somewhere, VMEM] + [VMEM] * len(sums),
        scratch_shapes=[
            pltpu.VMEM((copies, xr, LANES), F32),
            pltpu.SemaphoreType.DMA((copies,)),
        ],
        input_output_aliases={len(arrays): 0, len(arrays) + 1: 1} if begun else {},
        compiler_params=limits(arrays, copies * xr * LANES * 4),
        cost_estimate=pl.CostEstimate(flops=0, bytes_accessed=moved, transcendentals=0),
    )(*inputs, *after)


def local(
    features, w_neigh, w_self, bias, cotangent, block_rows, block_cols, block_vals, block_count
):
    rs = lax.axis_size("row")
    cs = lax.axis_size("col")
    nd, depth = features.shape
    hid = w_self.shape[1]
    rt = nd * cs
    half = rs // 2
    xw = 2 * depth // cs
    nc = min(rs, hid // LANES)
    nr = rs // nc
    xr = xw // nr

    def along_col(x, k):
        return lax.ppermute(x, "col", [(s, s ^ k) for s in range(cs)])

    def along_chips(x, k):
        return lax.ppermute(x, "row", [(s, s ^ (2 * k)) for s in range(rs)])

    def other_core(x):
        return lax.ppermute(x, "row", [(s, s ^ 1) for s in range(rs)])

    def gather_chips(x):
        found = {0: x}
        step = half // 2
        while step:
            found.update({d + step: along_chips(found[d], step) for d in list(found)})
            step //= 2
        return [found[d] for d in range(half)]

    if rs == 2 * cs:

        def send_own(block, t):
            pairs = []
            for z in range(half):
                for core in range(2):
                    q = 2 * (z ^ t) + core
                    source = (2 * z + core) * cs + z
                    pairs.append((source, (2 * z + q // cs) * cs + q % cs))
            return lax.ppermute(block, ("row", "col"), pairs)

    else:
        swap = [((b % rs) * cs + b // rs, b) for b in range(rs * cs)]

        def send_own(block, t):
            return lax.ppermute(block, ("row", "col"), swap if t == 0 else [])

    near = along_chips(features, 1)
    mine_first = {0: features, 1: near}
    step = half // 2
    while step > 1:
        evens = [d for d in mine_first if d % 2 == 0]
        mine_first.update({d + step: along_chips(mine_first[d], step) for d in evens})
        step //= 2
    theirs_first = {0: other_core(features), 1: other_core(near)}
    own_feats = {0: send_own(features, 0)}
    tile, turned = densify(
        block_rows.reshape(-1),
        block_cols.reshape(-1),
        block_count.reshape(-1),
        block_vals[0, 0],
        nd,
        rs,
        cs,
        [],
    )
    mine_last = {d + 1: along_chips(x, 1) for d, x in mine_first.items() if d > 1}
    theirs_first.update({d: other_core(x) for d, x in mine_first.items() if d > 1})
    theirs_last = {d: other_core(x) for d, x in mine_last.items()}
    own_feats[1] = send_own(near, 1)

    def placed(mine, theirs):
        places = list(mine) + [half + d for d in theirs]
        return places, [*mine.values(), *theirs.values()]

    begun = forward_first(
        tile, *placed(mine_first, theirs_first), nd, [own_feats[0], own_feats[1]]
    )
    degree = row_sums(tile, nd, cs)
    step = 1
    while step < cs:
        masses = [degree, along_col(degree, step)]
        degree = masses[0] + masses[1]
        step *= 2
    evens = {d: send_own(follow(x, [begun, masses[0]]), d) for d, x in mine_first.items() if d > 1}
    own_feats.update(evens)
    own_feats.update({d: send_own(x, d) for d, x in mine_last.items()})
    parts = forward_parts(begun, tile, *placed(mine_last, theirs_last), nd, cs, list(evens.values()))
    own_feat = sum(list(own_feats.values())[1:], own_feats[0])
    inverse = 1.0 / (degree[0] + 1.0)
    inverse = jnp.broadcast_to(inverse[:, None], (rt, LANES))
    own = jnp.dot(own_feat, w_self, preferred_element_type=F32).astype(BF16)

    turned_neigh, turned_self = turn([w_neigh, w_self], [parts[0]])
    parts = [parts[0]] + [along_col(parts[k], k) for k in range(1, cs)]
    output, sums, *packs = activation(
        parts, masses, own, own_feat, w_neigh, bias[None, :], cotangent, [turned_neigh]
    )
    packs = [packs[0]] + [along_col(packs[k], k) for k in range(1, cs)]

    mid = cs // 2
    scaled_args = (inverse, turned_neigh, turned_self, cs, rs)
    early = scaled_parts(packs[:mid], 0, *scaled_args)
    keep, send = weight_parts(packs, sums, rs, xr, nc, early[:1])
    came = other_core(send)
    late = scaled_parts(packs[mid:], mid, *scaled_args, [keep])
    scaled, self_parts = zip(early, late)
    chunks = pair_sum(keep, came)
    chunks = [chunks[0]] + [along_chips(chunks[k], k) for k in range(half - 1, 0, -1)]
    line = gather_chips(last_sum(chunks))

    keep, send = back_parts(turned, scaled, self_parts, nd, cs, rs, [keep])
    keep, send = fold(keep, other_core(follow(send, chunks[1:])), line[1:])
    line = stack(line, after=[send])
    step = 1
    while 2 * step < half:
        keep, send = fold(keep, along_chips(send, step))
        step *= 2
    last = (keep, along_chips(send, step))

    def piece(array, first, column, mine):
        return array, [(first + t, column) for t in range(array.shape[0])], mine

    mid = half // 2
    if cs == 4 and mid:
        first, second = along_col(line, 1), along_col(line, 2)
        near = [(line, 0, 0), (first, 0, 1), (second, 0, 2)]
        rest = [(along_col(first[:mid], 2), 0, 3), (along_col(second[mid:], 1), mid, 3)]
    else:
        near = [(line, 0, 0)] + [(along_col(line, k), 0, k) for k in range(1, cs - 1)]
        rest = [(along_col(line, cs - 1), 0, cs - 1)]
    factor = 1.0 / math.sqrt(nd * rs * cs)
    sizes = (depth, hid, xr, nc, cs, (factor, 32.0 * factor))
    pieces = [piece(*x, True) for x in near + rest]
    *begun, grad_input = assemble(pieces, (), *sizes, (), last)
    pieces = [piece(other_core(x), *where, False) for x, *where in near + rest]
    total_self, total_neigh, total_bias = assemble(pieces, begun, *sizes, ())
    return output, grad_input, total_self, total_neigh, total_bias.reshape(-1)


def solution(mesh):
    in_specs = (
        P(("col", "row"), None),
        P(),
        P(),
        P(),
        P(("row", "col"), None),
        P("row", "col", None),
        P("row", "col", None),
        P("row", "col", None, None, None),
        P("row", "col"),
    )
    out_specs = (P(("row", "col"), None), P(("col", "row"), None), P(), P(), P())
    return jax.shard_map(local, mesh=mesh, in_specs=in_specs, out_specs=out_specs, check_vma=False)
```

```python
import math

import jax
import jax.numpy as jnp
from jax import lax
from jax.experimental import pallas as pl
from jax.experimental.pallas import tpu as pltpu
from jax.sharding import PartitionSpec as P

F32 = jnp.float32
BF16 = jnp.bfloat16
LANES = 128
EXTRA = 16
SPARE = 16
VMEM = pl.BlockSpec(memory_space=pltpu.VMEM)
SMEM = pl.BlockSpec(memory_space=pltpu.SMEM)
MIB = 1024 * 1024


def limits(arrays, scratch=0):
    held = sum(math.prod(a.shape) * a.dtype.itemsize for a in arrays) + scratch
    return pltpu.CompilerParams(vmem_limit_bytes=min(56 * MIB, 2 * held + 12 * MIB))


def call(body, outs, args, scratch=(), smem=0, flops=0, after=()):
    count = len(args)
    moved = sum(math.prod(a.shape) * a.dtype.itemsize for a in (*outs, *args))
    held = sum(math.prod(x.shape) * x.dtype.itemsize for x in scratch)

    def run(*refs):
        body(*refs[:count], *refs[count + len(after) :])

    return pl.pallas_call(
        run,
        out_shape=outs,
        in_specs=[SMEM] * smem
        + [VMEM] * (count - smem)
        + [pl.BlockSpec(memory_space=pl.ANY)] * len(after),
        out_specs=[VMEM] * len(outs),
        scratch_shapes=list(scratch),
        compiler_params=limits([*outs, *args], held),
        cost_estimate=pl.CostEstimate(flops=flops, bytes_accessed=moved, transcendentals=0),
    )(*args, *after)


def shape(dims, dtype):
    return jax.ShapeDtypeStruct(tuple(dims), dtype)


def mm(a, b, ca=1, cb=0):
    return lax.dot_general(a, b, (((ca,), (cb,)), ((), ())), preferred_element_type=F32)


def follow(x, after):
    def body(x_ref, out_ref):
        out_ref[...] = x_ref[...]

    return call(body, [shape(x.shape, x.dtype)], [x], after=after)[0]


def turn(weights, after):
    def body(*refs):
        for ref, out_ref in zip(refs, refs[len(weights) :]):
            out_ref[...] = ref[...].T

    return call(body, [shape(w.shape[::-1], w.dtype) for w in weights], weights, after=after)


def join(parts, after=()):
    counts = [x.shape[0] for x in parts]

    def body(*refs):
        at = 0
        for count, ref in zip(counts, refs):
            refs[-1][at : at + count] = ref[...]
            at += count

    out = shape((sum(counts), *parts[0].shape[1:]), parts[0].dtype)
    return call(body, [out], parts, after=after)[0]


def stack(parts, joined=False, after=()):
    count = parts[0].shape[0] if joined else 1

    def body(*refs):
        for k, ref in enumerate(refs[:-1]):
            if joined:
                refs[-1][k * count : (k + 1) * count] = ref[...]
            else:
                refs[-1][k] = ref[...]

    dims = parts[0].shape[1:] if joined else parts[0].shape
    out = shape((len(parts) * count, *dims), parts[0].dtype)
    return call(body, [out], parts, after=after)[0]


def densify(rows, cols, count, values, nd, rs, cs, after):
    rt, ct, half = nd * cs, nd * rs, rs // 2

    def body(rows_ref, cols_ref, count_ref, values_ref, tile_ref, turned_ref, acc):
        i, j = lax.axis_index("row"), lax.axis_index("col")
        z, c = i // 2, lax.rem(i, 2)
        acc[...] = jnp.zeros_like(acc)

        def add(s, carry):
            col = cols_ref[s]
            row = rows_ref[s] ^ j
            col = (z ^ (col // 2)) + half * (lax.rem(col, 2) ^ c)
            r = pl.multiple_of(row * nd, nd)
            c0 = pl.multiple_of(col * nd, nd)
            acc[pl.ds(r, nd), pl.ds(c0, nd)] += values_ref[s].astype(F32)
            return carry

        lax.fori_loop(0, count_ref[0], add, 0)
        tile_ref[...] = acc[...].astype(BF16)
        for k in range(rs):
            cut = acc[:, k * nd : (k + 1) * nd]
            turned_ref[k * nd : (k + 1) * nd, :] = cut.T.astype(BF16)

    return call(
        body,
        [shape((rt, ct), BF16), shape((ct, rt), BF16)],
        [rows, cols, count, values],
        [pltpu.VMEM((rt, ct), F32)],
        smem=3,
        flops=rt * ct,
        after=after,
    )


def tile_columns(tile_ref, places, nd):
    return jnp.concatenate([tile_ref[:, p * nd : (p + 1) * nd] for p in places], axis=1)


def row_sums(tile, nd, cs):
    rt, ct = tile.shape

    def body(tile_ref, mass_ref):
        j = lax.axis_index("col")
        ones = jnp.ones((8, ct), BF16)
        for k in range(cs):
            place = pl.multiple_of((j ^ k) * nd, nd)
            mass_ref[:, pl.ds(place, nd)] = mm(ones, tile_ref[k * nd : (k + 1) * nd, :], 1, 1)

    return call(body, [shape((8, rt), F32)], [tile], flops=16 * tile.size)[0]


def forward_first(tile, places, blocks, nd, after):
    rt = tile.shape[0]
    width = blocks[0].shape[1]

    def body(*refs):
        tile_ref, feat_refs = refs[0], refs[1 : 1 + len(blocks)]
        sum_ref = refs[1 + len(blocks)]
        feats = jnp.concatenate([r[...] for r in feat_refs], axis=0)
        sum_ref[...] = mm(tile_columns(tile_ref, places, nd), feats)

    return call(
        body,
        [shape((rt, width), F32)],
        [tile, *blocks],
        flops=2 * rt * len(places) * nd * width,
        after=after,
    )[0]


def forward_parts(begun, tile, places, blocks, nd, cs, after):
    width = blocks[0].shape[1]

    def body(*refs):
        sum_ref, tile_ref, feat_refs = refs[0], refs[1], refs[2 : 2 + len(blocks)]
        outs = refs[2 + len(blocks) :]
        feats = jnp.concatenate([r[...] for r in feat_refs], axis=0)
        parts = sum_ref[...] + mm(tile_columns(tile_ref, places, nd), feats)
        for k in range(cs):
            outs[k][...] = parts[k * nd : (k + 1) * nd].astype(outs[k].dtype)

    return call(
        body,
        [shape((nd, width), BF16 if k else F32) for k in range(cs)],
        [begun, tile, *blocks],
        flops=2 * tile.shape[0] * len(places) * nd * width,
        after=after,
    )


def activation(parts, masses, own, own_feat, w_neigh, bias, cotangent, after):
    cs = len(parts)
    nd, hid = own.shape
    depth = own_feat.shape[1]
    xw = 2 * depth // cs

    def body(*refs):
        part_refs = refs[:cs]
        mass_refs = refs[cs : cs + 2]
        own_ref, feat_ref, w_ref, bias_ref, cot_ref = refs[cs + 2 : cs + 7]
        out_ref, sum_ref, *packs = refs[cs + 7 : -1]
        both = refs[-1]
        j = lax.axis_index("col")
        here = pl.ds(pl.multiple_of(j * nd, nd), nd)
        inv = 1.0 / (mass_refs[0][:, here] + mass_refs[1][:, here] + 1.0)
        inv = jnp.broadcast_to(inv.T[:, :1], (nd, LANES))
        total = sum(r[...].astype(F32) for r in part_refs)
        mean = (total * jnp.concatenate([inv] * (depth // LANES), axis=1)).astype(BF16)
        both[:, :depth] = feat_ref[...]
        both[:, depth:] = mean
        pre = own_ref[...].astype(F32) + mm(mean, w_ref[...]) + bias_ref[...]
        slope = jnp.where(pre > 0, 1.0, jnp.exp(jnp.minimum(pre, 0.0)))
        out_ref[...] = jnp.where(pre > 0, pre, slope - 1.0).astype(BF16)
        grad = cot_ref[...].astype(F32) * slope
        sum_ref[...] = jnp.broadcast_to(jnp.sum(grad, axis=0, keepdims=True), (8, hid))
        grad = grad.astype(BF16)
        for k in range(cs):
            packs[k][:, :hid] = grad
            target = j ^ k
            if xw % LANES == 0:
                start = pl.multiple_of(target * xw, LANES)
                packs[k][:, hid:] = both[:, pl.ds(start, xw)]
            else:
                for d in range(cs):

                    @pl.when(target == d)
                    def _():
                        packs[k][:, hid:] = both[:, d * xw : (d + 1) * xw]

    return call(
        body,
        [shape((nd, hid), BF16), shape((8, hid), F32)] + [shape((nd, hid + xw), BF16)] * cs,
        [*parts, *masses, own, own_feat, w_neigh, bias, cotangent],
        [pltpu.VMEM((nd, 2 * depth), BF16)],
        flops=2 * own_feat.size * hid,
        after=after,
    )


def split_pair(total):
    high = total.astype(BF16).astype(F32)
    return jnp.concatenate([high, total - high], axis=0)


def weight_parts(packs, sums, rs, xr, nc, after):
    cs = len(packs)
    hid = sums.shape[1]
    nd, xw = packs[0].shape[0], packs[0].shape[1] - hid
    half = rs // 2

    def body(*refs):
        pack_refs = refs[:cs]
        sum_ref, keep_ref, send_ref, acc = refs[cs:]
        x_all = jnp.concatenate([r[:, hid:] for r in pack_refs], axis=0)
        g_all = jnp.concatenate([r[:, :hid] for r in pack_refs], axis=0)
        acc[...] = mm(x_all, g_all, 0, 0)
        i = lax.axis_index("row")
        z, c = i // 2, lax.rem(i, 2)
        for k in range(half):
            for core, ref in ((c, keep_ref), (1 - c, send_ref)):
                q = 2 * (z ^ k) + core
                row = pl.multiple_of((q // nc) * xr, xr)
                col = pl.multiple_of(lax.rem(q, nc) * LANES, LANES)
                ref[k, :xr, :] = acc[pl.ds(row, xr), pl.ds(col, LANES)].astype(ref.dtype)
                ref[k, xr:, :] = split_pair(sum_ref[:, pl.ds(col, LANES)]).astype(ref.dtype)

    dims = (half, xr + EXTRA, LANES)
    return call(
        body,
        [shape(dims, F32), shape(dims, BF16)],
        [*packs, sums],
        [pltpu.VMEM((xw, hid), F32)],
        flops=2 * cs * nd * xw * hid,
        after=after,
    )


def scaled_parts(packs, first, inverse, turned_neigh, turned_self, cs, rs, after=()):
    count = len(packs)
    nd = packs[0].shape[0]
    hid, depth = turned_neigh.shape

    def body(neigh_ref, own_ref, inv_ref, *refs):
        pack_refs, scaled_ref, self_ref = refs[:count], refs[count], refs[count + 1]
        i, j = lax.axis_index("row"), lax.axis_index("col")
        grads = jnp.concatenate([r[:, :hid] for r in pack_refs], axis=0)
        product = mm(grads, neigh_ref[...])
        for r in range(count):
            start = pl.multiple_of((j ^ (first + r)) * nd, nd)
            inv = inv_ref[pl.ds(start, nd), :]
            inv = jnp.concatenate([inv] * (depth // LANES), axis=1)
            rows = slice(r * nd, (r + 1) * nd)
            scaled_ref[rows, :] = (product[rows] * inv).astype(BF16)

        @pl.when(i * cs // rs == j)
        def _():
            self_ref[...] = mm(grads, own_ref[...])

    return call(
        body,
        [shape((count * nd, depth), BF16), shape((count * nd, depth), F32)],
        [turned_neigh, turned_self, inverse, *packs],
        flops=4 * count * nd * hid * depth,
        after=after,
    )


def halving_order(count):
    order = [0]
    step = count // 2
    while step:
        order = order + [d + step for d in order]
        step //= 2
    return order


def back_parts(turned, scaled, self_parts, nd, cs, rs, after):
    depth = scaled[0].shape[1]
    half = rs // 2
    count = len(scaled)
    each = cs // count

    def body(tile_ref, *refs):
        scaled_refs, self_refs = refs[:count], refs[count : 2 * count]
        keep_ref, send_ref, acc = refs[2 * count :]
        i, j = lax.axis_index("row"), lax.axis_index("col")
        z, c = i // 2, lax.rem(i, 2)
        acc[...] = mm(tile_ref[...], jnp.concatenate([r[...] for r in scaled_refs], axis=0))

        @pl.when(i * cs // rs == j)
        def _():
            for r in range(cs):
                q = i * cs - j * rs + (j ^ r)
                place = ((z ^ (q // 2)) + half * (lax.rem(q, 2) ^ c)) * nd
                rows = slice(r % each * nd, (r % each + 1) * nd)
                acc[pl.ds(pl.multiple_of(place, nd), nd), :] += self_refs[r // each][rows]

        for ref, base in ((send_ref, half), (keep_ref, 0)):
            for k, distance in enumerate(halving_order(half)):
                place = (base + distance) * nd
                ref[k] = acc[place : place + nd, :].astype(ref.dtype)

    dims = (half, nd, depth)
    return call(
        body,
        [shape(dims, F32), shape(dims, BF16)],
        [turned, *scaled, *self_parts],
        [pltpu.VMEM((rs * nd, depth), F32)],
        flops=2 * turned.size * depth,
        after=after,
    )


def fold(keep, came, after=(), spare=0):
    count, rows, width = keep.shape
    half = count // 2

    def body(keep_ref, came_ref, kept_ref, send_ref):
        total = keep_ref[...] + came_ref[...].astype(F32)
        kept_ref[...] = total[:half]
        send_ref[:, :rows, :] = total[half:].astype(BF16)
        if spare:
            send_ref[:, rows:, :] = jnp.zeros((half, spare, width), BF16)

    outs = [shape((half, rows, width), F32), shape((half, rows + spare, width), BF16)]
    return call(body, outs, [keep, came], after=after)


def pair_sum(keep, came):
    half, rows, width = keep.shape
    main = rows - EXTRA

    def body(keep_ref, came_ref, *outs):
        for k in range(half):
            total = keep_ref[k] + came_ref[k].astype(F32)
            dtype = outs[k].dtype
            outs[k][:main, :] = total[:main].astype(dtype)
            merged = total[main : main + 8] + total[main + 8 :]
            outs[k][main:, :] = split_pair(merged).astype(dtype)

    return call(
        body,
        [shape((rows, width), BF16 if k else F32) for k in range(half)],
        [keep, came],
    )


def last_sum(parts):
    rows, width = parts[0].shape
    main = rows - EXTRA

    def body(*refs):
        out_ref = refs[-1]
        total = refs[0][...]
        for ref in refs[1:-1]:
            total = total + ref[...].astype(F32)
        out_ref[:main, :] = total[:main].astype(BF16)
        merged = total[main : main + 8] + total[main + 8 :]
        out_ref[main:, :] = split_pair(merged).astype(BF16)

    return call(body, [shape((rows, width), BF16)], parts)[0]


def assemble(pieces, begun, depth, hid, xr, nc, cs, factors, after, adds=()):
    xw = 2 * depth // cs
    side = cs // 2
    copies = sum(len(where) for _, where, _ in pieces)
    arrays = [array for array, _, _ in pieces]
    inputs = arrays + list(begun) + list(adds)
    weight = shape((depth, hid), F32)

    def body(*refs):
        piece_refs = refs[: len(pieces)]
        self_ref, neigh_ref, bias_ref, *sum_ref, staged, sems = refs[len(inputs) :]
        i, j = lax.axis_index("row"), lax.axis_index("col")
        z, c = i // 2, lax.rem(i, 2)
        if begun:
            bias_ref[...] = refs[len(arrays) + 2][...]
        else:
            bias_ref[...] = jnp.zeros_like(bias_ref)
        waits = []
        at = 0
        for ref, (_, where, mine) in zip(piece_refs, pieces):
            for t, (distance, column) in enumerate(where):
                owner = j ^ column
                first = owner < side
                q = 2 * (z ^ distance) + (c if mine else 1 - c)
                col = pl.multiple_of(lax.rem(q, nc) * LANES, LANES)
                turn = q // nc
                row = pl.multiple_of(lax.rem(owner, side) * xw + turn * xr, xr)
                scale = jnp.where(first, factors[0], factors[1])
                staged[at] = ref[t, :xr, :].astype(F32) * scale
                for target, here in ((self_ref, first), (neigh_ref, jnp.logical_not(first))):
                    copy = pltpu.make_async_copy(
                        staged.at[at],
                        target.at[pl.ds(row, xr), pl.ds(col, LANES)],
                        sems.at[at],
                    )
                    pl.when(here)(copy.start)
                    waits.append((here, copy))

                @pl.when(turn == 0)
                def _():
                    total = ref[t, xr:, :].astype(F32)
                    total = (total[:1] + total[8:9]) * factors[0]
                    bias_ref[:, pl.ds(col, LANES)] += total

                at += 1
        if adds:
            keep_ref, came_ref = refs[len(inputs) - 2 : len(inputs)]
            came = came_ref[0, : keep_ref.shape[1], :].astype(F32)
            sum_ref[0][...] = (keep_ref[0] + came).astype(BF16)
        for here, copy in waits:
            pl.when(here)(copy.wait)

    def run(*refs):
        body(*refs[: len(inputs)], *refs[len(inputs) + len(after) :])

    somewhere = pl.BlockSpec(memory_space=pl.ANY)
    sums = [shape(adds[0].shape[1:], BF16)] if adds else []
    moved = 2 * copies * xr * LANES * 6
    return pl.pallas_call(
        run,
        out_shape=[weight, weight, shape((1, hid), F32), *sums],
        in_specs=[VMEM] * len(arrays)
        + ([somewhere, somewhere, VMEM] if begun else [])
        + [VMEM] * len(adds)
        + [somewhere] * len(after),
        out_specs=[somewhere, somewhere, VMEM] + [VMEM] * len(sums),
        scratch_shapes=[
            pltpu.VMEM((copies, xr, LANES), F32),
            pltpu.SemaphoreType.DMA((copies,)),
        ],
        input_output_aliases={len(arrays): 0, len(arrays) + 1: 1} if begun else {},
        compiler_params=limits(arrays, copies * xr * LANES * 4),
        cost_estimate=pl.CostEstimate(flops=0, bytes_accessed=moved, transcendentals=0),
    )(*inputs, *after)


def local(
    features, w_neigh, w_self, bias, cotangent, block_rows, block_cols, block_vals, block_count
):
    rs = lax.axis_size("row")
    cs = lax.axis_size("col")
    nd, depth = features.shape
    hid = w_self.shape[1]
    rt = nd * cs
    half = rs // 2
    xw = 2 * depth // cs
    nc = min(rs, hid // LANES)
    nr = rs // nc
    xr = xw // nr

    def along_col(x, k):
        return lax.ppermute(x, "col", [(s, s ^ k) for s in range(cs)])

    def along_chips(x, k):
        return lax.ppermute(x, "row", [(s, s ^ (2 * k)) for s in range(rs)])

    def other_core(x):
        return lax.ppermute(x, "row", [(s, s ^ 1) for s in range(rs)])

    def gather_chips(x):
        found = {0: x}
        step = half // 2
        while step:
            found.update({d + step: along_chips(found[d], step) for d in list(found)})
            step //= 2
        return [found[d] for d in range(half)]

    if rs == 2 * cs:

        def send_own(block, t):
            pairs = []
            for z in range(half):
                for core in range(2):
                    q = 2 * (z ^ t) + core
                    source = (2 * z + core) * cs + z
                    pairs.append((source, (2 * z + q // cs) * cs + q % cs))
            return lax.ppermute(block, ("row", "col"), pairs)

    else:
        swap = [((b % rs) * cs + b // rs, b) for b in range(rs * cs)]

        def send_own(block, t):
            return lax.ppermute(block, ("row", "col"), swap if t == 0 else [])

    near = along_chips(features, 1)
    mine_first = {0: features, 1: near}
    step = half // 2
    while step > 1:
        evens = [d for d in mine_first if d % 2 == 0]
        mine_first.update({d + step: along_chips(mine_first[d], step) for d in evens})
        step //= 2
    theirs_first = {0: other_core(features), 1: other_core(near)}
    own_feats = {0: send_own(features, 0)}
    tile, turned = densify(
        block_rows.reshape(-1),
        block_cols.reshape(-1),
        block_count.reshape(-1),
        block_vals[0, 0],
        nd,
        rs,
        cs,
        [],
    )
    mine_last = {d + 1: along_chips(x, 1) for d, x in mine_first.items() if d > 1}
    theirs_first.update({d: other_core(x) for d, x in mine_first.items() if d > 1})
    theirs_last = {d: other_core(x) for d, x in mine_last.items()}
    own_feats[1] = send_own(near, 1)

    def placed(mine, theirs):
        places = list(mine) + [half + d for d in theirs]
        return places, [*mine.values(), *theirs.values()]

    begun = forward_first(
        tile, *placed(mine_first, theirs_first), nd, [own_feats[0], own_feats[1]]
    )
    degree = row_sums(tile, nd, cs)
    step = 1
    while step < cs:
        masses = [degree, along_col(degree, step)]
        degree = masses[0] + masses[1]
        step *= 2
    evens = {d: send_own(follow(x, [begun, masses[0]]), d) for d, x in mine_first.items() if d > 1}
    own_feats.update(evens)
    own_feats.update({d: send_own(x, d) for d, x in mine_last.items()})
    parts = forward_parts(begun, tile, *placed(mine_last, theirs_last), nd, cs, list(evens.values()))
    own_feat = sum(list(own_feats.values())[1:], own_feats[0])
    inverse = 1.0 / (degree[0] + 1.0)
    inverse = jnp.broadcast_to(inverse[:, None], (rt, LANES))
    own = jnp.dot(own_feat, w_self, preferred_element_type=F32).astype(BF16)

    turned_neigh, turned_self = turn([w_neigh, w_self], [parts[0]])
    parts = [parts[0]] + [along_col(parts[k], k) for k in range(1, cs)]
    output, sums, *packs = activation(
        parts, masses, own, own_feat, w_neigh, bias[None, :], cotangent, [turned_neigh]
    )
    packs = [packs[0]] + [along_col(packs[k], k) for k in range(1, cs)]

    mid = cs // 2
    scaled_args = (inverse, turned_neigh, turned_self, cs, rs)
    early = scaled_parts(packs[:mid], 0, *scaled_args)
    keep, send = weight_parts(packs, sums, rs, xr, nc, early[:1])
    came = other_core(send)
    late = scaled_parts(packs[mid:], mid, *scaled_args, [keep])
    scaled, self_parts = zip(early, late)
    chunks = pair_sum(keep, came)
    chunks = [chunks[0]] + [along_chips(chunks[k], k) for k in range(half - 1, 0, -1)]
    line = gather_chips(last_sum(chunks))

    keep, send = back_parts(turned, scaled, self_parts, nd, cs, rs, [keep])
    keep, send = fold(keep, other_core(follow(send, chunks[1:])), line[1:])
    line = stack(line, after=[send])
    step = 1
    while 2 * step < half:
        spare = SPARE if 4 * step == half else 0
        keep, send = fold(keep, along_chips(send, step), (), spare)
        step *= 2
    last = (keep, along_chips(send, step))

    def piece(array, first, column, mine):
        return array, [(first + t, column) for t in range(array.shape[0])], mine

    mid = half // 2
    if cs == 4 and mid:
        first, second = along_col(line, 1), along_col(line, 2)
        near = [(line, 0, 0), (first, 0, 1), (second, 0, 2)]
        rest = [(along_col(first[:mid], 2), 0, 3), (along_col(second[mid:], 1), mid, 3)]
    else:
        near = [(line, 0, 0)] + [(along_col(line, k), 0, k) for k in range(1, cs - 1)]
        rest = [(along_col(line, cs - 1), 0, cs - 1)]
    factor = 1.0 / math.sqrt(nd * rs * cs)
    sizes = (depth, hid, xr, nc, cs, (factor, 32.0 * factor))
    where = [(d, k) for k in range(cs - 1) for d in range(half)]
    near = join([x for x, *_ in near], [keep])
    begun = assemble([(near, where, True), (other_core(near), where, False)], (), *sizes, ())
    rest[-1] = (follow(rest[-1][0], begun[2:]), *rest[-1][1:])
    pieces = [piece(*x, True) for x in rest]
    pieces += [piece(other_core(x), *where, False) for x, *where in rest]
    total_self, total_neigh, total_bias, grad_input = assemble(pieces, begun, *sizes, (), last)
    return output, grad_input, total_self, total_neigh, total_bias.reshape(-1)


def solution(mesh):
    in_specs = (
        P(("col", "row"), None),
        P(),
        P(),
        P(),
        P(("row", "col"), None),
        P("row", "col", None),
        P("row", "col", None),
        P("row", "col", None, None, None),
        P("row", "col"),
    )
    out_specs = (P(("row", "col"), None), P(("col", "row"), None), P(), P(), P())
    return jax.shard_map(local, mesh=mesh, in_specs=in_specs, out_specs=out_specs, check_vma=False)
```

```python
import math

import jax
import jax.numpy as jnp
from jax import lax
from jax.experimental import pallas as pl
from jax.experimental.pallas import tpu as pltpu
from jax.sharding import PartitionSpec as P

F32 = jnp.float32
BF16 = jnp.bfloat16
LANES = 128
EXTRA = 16
VMEM = pl.BlockSpec(memory_space=pltpu.VMEM)
SMEM = pl.BlockSpec(memory_space=pltpu.SMEM)
MIB = 1024 * 1024


def limits(arrays, scratch=0):
    held = sum(math.prod(a.shape) * a.dtype.itemsize for a in arrays) + scratch
    return pltpu.CompilerParams(vmem_limit_bytes=min(56 * MIB, 2 * held + 12 * MIB))


def call(body, outs, args, scratch=(), smem=0, flops=0, after=()):
    count = len(args)
    moved = sum(math.prod(a.shape) * a.dtype.itemsize for a in (*outs, *args))
    held = sum(math.prod(x.shape) * x.dtype.itemsize for x in scratch)

    def run(*refs):
        body(*refs[:count], *refs[count + len(after) :])

    return pl.pallas_call(
        run,
        out_shape=outs,
        in_specs=[SMEM] * smem
        + [VMEM] * (count - smem)
        + [pl.BlockSpec(memory_space=pl.ANY)] * len(after),
        out_specs=[VMEM] * len(outs),
        scratch_shapes=list(scratch),
        compiler_params=limits([*outs, *args], held),
        cost_estimate=pl.CostEstimate(flops=flops, bytes_accessed=moved, transcendentals=0),
    )(*args, *after)


def shape(dims, dtype):
    return jax.ShapeDtypeStruct(tuple(dims), dtype)


def mm(a, b, ca=1, cb=0):
    return lax.dot_general(a, b, (((ca,), (cb,)), ((), ())), preferred_element_type=F32)


def follow(x, after):
    def body(x_ref, out_ref):
        out_ref[...] = x_ref[...]

    return call(body, [shape(x.shape, x.dtype)], [x], after=after)[0]


def turn(weights, after):
    def body(*refs):
        for ref, out_ref in zip(refs, refs[len(weights) :]):
            out_ref[...] = ref[...].T

    return call(body, [shape(w.shape[::-1], w.dtype) for w in weights], weights, after=after)


def stack(parts, joined=False, after=()):
    count = parts[0].shape[0] if joined else 1

    def body(*refs):
        for k, ref in enumerate(refs[:-1]):
            if joined:
                refs[-1][k * count : (k + 1) * count] = ref[...]
            else:
                refs[-1][k] = ref[...]

    dims = parts[0].shape[1:] if joined else parts[0].shape
    out = shape((len(parts) * count, *dims), parts[0].dtype)
    return call(body, [out], parts, after=after)[0]


def densify(rows, cols, count, values, nd, rs, cs, after):
    rt, ct, half = nd * cs, nd * rs, rs // 2

    def body(rows_ref, cols_ref, count_ref, values_ref, tile_ref, turned_ref, acc):
        i, j = lax.axis_index("row"), lax.axis_index("col")
        z, c = i // 2, lax.rem(i, 2)
        acc[...] = jnp.zeros_like(acc)

        def add(s, carry):
            col = cols_ref[s]
            row = rows_ref[s] ^ j
            col = (z ^ (col // 2)) + half * (lax.rem(col, 2) ^ c)
            r = pl.multiple_of(row * nd, nd)
            c0 = pl.multiple_of(col * nd, nd)
            acc[pl.ds(r, nd), pl.ds(c0, nd)] += values_ref[s].astype(F32)
            return carry

        lax.fori_loop(0, count_ref[0], add, 0)
        tile_ref[...] = acc[...].astype(BF16)
        for k in range(rs):
            cut = acc[:, k * nd : (k + 1) * nd]
            turned_ref[k * nd : (k + 1) * nd, :] = cut.T.astype(BF16)

    return call(
        body,
        [shape((rt, ct), BF16), shape((ct, rt), BF16)],
        [rows, cols, count, values],
        [pltpu.VMEM((rt, ct), F32)],
        smem=3,
        flops=rt * ct,
        after=after,
    )


def tile_columns(tile_ref, places, nd):
    return jnp.concatenate([tile_ref[:, p * nd : (p + 1) * nd] for p in places], axis=1)


def row_sums(tile, nd, cs):
    rt, ct = tile.shape

    def body(tile_ref, mass_ref):
        j = lax.axis_index("col")
        ones = jnp.ones((8, ct), BF16)
        for k in range(cs):
            place = pl.multiple_of((j ^ k) * nd, nd)
            mass_ref[:, pl.ds(place, nd)] = mm(ones, tile_ref[k * nd : (k + 1) * nd, :], 1, 1)

    return call(body, [shape((8, rt), F32)], [tile], flops=16 * tile.size)[0]


def forward_first(tile, places, blocks, nd, after):
    rt = tile.shape[0]
    width = blocks[0].shape[1]

    def body(*refs):
        tile_ref, feat_refs = refs[0], refs[1 : 1 + len(blocks)]
        sum_ref = refs[1 + len(blocks)]
        feats = jnp.concatenate([r[...] for r in feat_refs], axis=0)
        sum_ref[...] = mm(tile_columns(tile_ref, places, nd), feats)

    return call(
        body,
        [shape((rt, width), F32)],
        [tile, *blocks],
        flops=2 * rt * len(places) * nd * width,
        after=after,
    )[0]


def forward_parts(begun, tile, places, blocks, nd, cs, after):
    width = blocks[0].shape[1]

    def body(*refs):
        sum_ref, tile_ref, feat_refs = refs[0], refs[1], refs[2 : 2 + len(blocks)]
        outs = refs[2 + len(blocks) :]
        feats = jnp.concatenate([r[...] for r in feat_refs], axis=0)
        parts = sum_ref[...] + mm(tile_columns(tile_ref, places, nd), feats)
        for k in range(cs):
            outs[k][...] = parts[k * nd : (k + 1) * nd].astype(outs[k].dtype)

    return call(
        body,
        [shape((nd, width), BF16 if k else F32) for k in range(cs)],
        [begun, tile, *blocks],
        flops=2 * tile.shape[0] * len(places) * nd * width,
        after=after,
    )


def activation(parts, masses, own, own_feat, w_neigh, bias, cotangent, after):
    cs = len(parts)
    nd, hid = own.shape
    depth = own_feat.shape[1]
    xw = 2 * depth // cs

    def body(*refs):
        part_refs = refs[:cs]
        mass_refs = refs[cs : cs + 2]
        own_ref, feat_ref, w_ref, bias_ref, cot_ref = refs[cs + 2 : cs + 7]
        out_ref, sum_ref, *packs = refs[cs + 7 : -1]
        both = refs[-1]
        j = lax.axis_index("col")
        here = pl.ds(pl.multiple_of(j * nd, nd), nd)
        inv = 1.0 / (mass_refs[0][:, here] + mass_refs[1][:, here] + 1.0)
        inv = jnp.broadcast_to(inv.T[:, :1], (nd, LANES))
        total = sum(r[...].astype(F32) for r in part_refs)
        mean = (total * jnp.concatenate([inv] * (depth // LANES), axis=1)).astype(BF16)
        both[:, :depth] = feat_ref[...]
        both[:, depth:] = mean
        pre = own_ref[...].astype(F32) + mm(mean, w_ref[...]) + bias_ref[...]
        slope = jnp.where(pre > 0, 1.0, jnp.exp(jnp.minimum(pre, 0.0)))
        out_ref[...] = jnp.where(pre > 0, pre, slope - 1.0).astype(BF16)
        grad = cot_ref[...].astype(F32) * slope
        sum_ref[...] = jnp.broadcast_to(jnp.sum(grad, axis=0, keepdims=True), (8, hid))
        grad = grad.astype(BF16)
        for k in range(cs):
            packs[k][:, :hid] = grad
            target = j ^ k
            if xw % LANES == 0:
                start = pl.multiple_of(target * xw, LANES)
                packs[k][:, hid:] = both[:, pl.ds(start, xw)]
            else:
                for d in range(cs):

                    @pl.when(target == d)
                    def _():
                        packs[k][:, hid:] = both[:, d * xw : (d + 1) * xw]

    return call(
        body,
        [shape((nd, hid), BF16), shape((8, hid), F32)] + [shape((nd, hid + xw), BF16)] * cs,
        [*parts, *masses, own, own_feat, w_neigh, bias, cotangent],
        [pltpu.VMEM((nd, 2 * depth), BF16)],
        flops=2 * own_feat.size * hid,
        after=after,
    )


def split_pair(total):
    high = total.astype(BF16).astype(F32)
    return jnp.concatenate([high, total - high], axis=0)


def weight_parts(packs, sums, rs, xr, nc, after):
    cs = len(packs)
    hid = sums.shape[1]
    nd, xw = packs[0].shape[0], packs[0].shape[1] - hid
    half = rs // 2

    def body(*refs):
        pack_refs = refs[:cs]
        sum_ref, keep_ref, send_ref, acc = refs[cs:]
        x_all = jnp.concatenate([r[:, hid:] for r in pack_refs], axis=0)
        g_all = jnp.concatenate([r[:, :hid] for r in pack_refs], axis=0)
        acc[...] = mm(x_all, g_all, 0, 0)
        i = lax.axis_index("row")
        z, c = i // 2, lax.rem(i, 2)
        for k in range(half):
            for core, ref in ((c, keep_ref), (1 - c, send_ref)):
                q = 2 * (z ^ k) + core
                row = pl.multiple_of((q // nc) * xr, xr)
                col = pl.multiple_of(lax.rem(q, nc) * LANES, LANES)
                ref[k, :xr, :] = acc[pl.ds(row, xr), pl.ds(col, LANES)].astype(ref.dtype)
                ref[k, xr:, :] = split_pair(sum_ref[:, pl.ds(col, LANES)]).astype(ref.dtype)

    dims = (half, xr + EXTRA, LANES)
    return call(
        body,
        [shape(dims, F32), shape(dims, BF16)],
        [*packs, sums],
        [pltpu.VMEM((xw, hid), F32)],
        flops=2 * cs * nd * xw * hid,
        after=after,
    )


def scaled_parts(packs, first, inverse, turned_neigh, turned_self, cs, rs, after=()):
    count = len(packs)
    nd = packs[0].shape[0]
    hid, depth = turned_neigh.shape

    def body(neigh_ref, own_ref, inv_ref, *refs):
        pack_refs, scaled_ref, self_ref = refs[:count], refs[count], refs[count + 1]
        i, j = lax.axis_index("row"), lax.axis_index("col")
        grads = jnp.concatenate([r[:, :hid] for r in pack_refs], axis=0)
        product = mm(grads, neigh_ref[...])
        for r in range(count):
            start = pl.multiple_of((j ^ (first + r)) * nd, nd)
            inv = inv_ref[pl.ds(start, nd), :]
            inv = jnp.concatenate([inv] * (depth // LANES), axis=1)
            rows = slice(r * nd, (r + 1) * nd)
            scaled_ref[rows, :] = (product[rows] * inv).astype(BF16)

        @pl.when(i * cs // rs == j)
        def _():
            self_ref[...] = mm(grads, own_ref[...])

    return call(
        body,
        [shape((count * nd, depth), BF16), shape((count * nd, depth), F32)],
        [turned_neigh, turned_self, inverse, *packs],
        flops=4 * count * nd * hid * depth,
        after=after,
    )


def halving_order(count):
    order = [0]
    step = count // 2
    while step:
        order = order + [d + step for d in order]
        step //= 2
    return order


def back_parts(turned, scaled, self_parts, nd, cs, rs, after):
    depth = scaled[0].shape[1]
    half = rs // 2
    count = len(scaled)
    each = cs // count

    def body(tile_ref, *refs):
        scaled_refs, self_refs = refs[:count], refs[count : 2 * count]
        keep_ref, send_ref, acc = refs[2 * count :]
        i, j = lax.axis_index("row"), lax.axis_index("col")
        z, c = i // 2, lax.rem(i, 2)
        acc[...] = mm(tile_ref[...], jnp.concatenate([r[...] for r in scaled_refs], axis=0))

        @pl.when(i * cs // rs == j)
        def _():
            for r in range(cs):
                q = i * cs - j * rs + (j ^ r)
                place = ((z ^ (q // 2)) + half * (lax.rem(q, 2) ^ c)) * nd
                rows = slice(r % each * nd, (r % each + 1) * nd)
                acc[pl.ds(pl.multiple_of(place, nd), nd), :] += self_refs[r // each][rows]

        for ref, base in ((send_ref, half), (keep_ref, 0)):
            for k, distance in enumerate(halving_order(half)):
                place = (base + distance) * nd
                ref[k] = acc[place : place + nd, :].astype(ref.dtype)

    dims = (half, nd, depth)
    return call(
        body,
        [shape(dims, F32), shape(dims, BF16)],
        [turned, *scaled, *self_parts],
        [pltpu.VMEM((rs * nd, depth), F32)],
        flops=2 * turned.size * depth,
        after=after,
    )


def fold(keep, came, after=()):
    count, rows, width = keep.shape
    half = count // 2

    def body(keep_ref, came_ref, *outs):
        total = keep_ref[...] + came_ref[...].astype(F32)
        outs[0][...] = total[:half]
        outs[1][...] = total[half:].astype(BF16)

    dims = (half, rows, width)
    return call(body, [shape(dims, F32), shape(dims, BF16)], [keep, came], after=after)


def pair_sum(keep, came):
    half, rows, width = keep.shape
    main = rows - EXTRA

    def body(keep_ref, came_ref, *outs):
        for k in range(half):
            total = keep_ref[k] + came_ref[k].astype(F32)
            dtype = outs[k].dtype
            outs[k][:main, :] = total[:main].astype(dtype)
            merged = total[main : main + 8] + total[main + 8 :]
            outs[k][main:, :] = split_pair(merged).astype(dtype)

    return call(
        body,
        [shape((rows, width), BF16 if k else F32) for k in range(half)],
        [keep, came],
    )


def last_sum(parts, passed):
    rows, width = parts[0].shape
    main = rows - EXTRA

    def body(*refs):
        *part_refs, passed_ref, out_ref, again_ref = refs
        total = part_refs[0][...]
        for ref in part_refs[1:]:
            total = total + ref[...].astype(F32)
        out_ref[:main, :] = total[:main].astype(BF16)
        merged = total[main : main + 8] + total[main + 8 :]
        out_ref[main:, :] = split_pair(merged).astype(BF16)
        again_ref[...] = passed_ref[...]

    outs = [shape((rows, width), BF16), shape(passed.shape, passed.dtype)]
    return call(body, outs, [*parts, passed])


def assemble(pieces, begun, depth, hid, xr, nc, cs, factors, after, adds=()):
    xw = 2 * depth // cs
    side = cs // 2
    copies = sum(len(where) for _, where, _ in pieces)
    arrays = [array for array, _, _ in pieces]
    inputs = arrays + list(begun) + list(adds)
    weight = shape((depth, hid), F32)

    def body(*refs):
        piece_refs = refs[: len(pieces)]
        self_ref, neigh_ref, bias_ref, *sum_ref, staged, sems = refs[len(inputs) :]
        i, j = lax.axis_index("row"), lax.axis_index("col")
        z, c = i // 2, lax.rem(i, 2)
        if begun:
            bias_ref[...] = refs[len(arrays) + 2][...]
        else:
            bias_ref[...] = jnp.zeros_like(bias_ref)
        waits = []
        at = 0
        for ref, (_, where, mine) in zip(piece_refs, pieces):
            for t, (distance, column) in enumerate(where):
                owner = j ^ column
                first = owner < side
                q = 2 * (z ^ distance) + (c if mine else 1 - c)
                col = pl.multiple_of(lax.rem(q, nc) * LANES, LANES)
                turn = q // nc
                row = pl.multiple_of(lax.rem(owner, side) * xw + turn * xr, xr)
                scale = jnp.where(first, factors[0], factors[1])
                staged[at] = ref[t, :xr, :].astype(F32) * scale
                for target, here in ((self_ref, first), (neigh_ref, jnp.logical_not(first))):
                    copy = pltpu.make_async_copy(
                        staged.at[at],
                        target.at[pl.ds(row, xr), pl.ds(col, LANES)],
                        sems.at[at],
                    )
                    pl.when(here)(copy.start)
                    waits.append((here, copy))

                @pl.when(turn == 0)
                def _():
                    total = ref[t, xr:, :].astype(F32)
                    total = (total[:1] + total[8:9]) * factors[0]
                    bias_ref[:, pl.ds(col, LANES)] += total

                at += 1
        if adds:
            keep_ref, came_ref = refs[len(inputs) - 2 : len(inputs)]
            sum_ref[0][...] = (keep_ref[0] + came_ref[0].astype(F32)).astype(BF16)
        for here, copy in waits:
            pl.when(here)(copy.wait)

    def run(*refs):
        body(*refs[: len(inputs)], *refs[len(inputs) + len(after) :])

    somewhere = pl.BlockSpec(memory_space=pl.ANY)
    sums = [shape(adds[0].shape[1:], BF16)] if adds else []
    moved = 2 * copies * xr * LANES * 6
    return pl.pallas_call(
        run,
        out_shape=[weight, weight, shape((1, hid), F32), *sums],
        in_specs=[VMEM] * len(arrays)
        + ([somewhere, somewhere, VMEM] if begun else [])
        + [VMEM] * len(adds)
        + [somewhere] * len(after),
        out_specs=[somewhere, somewhere, VMEM] + [VMEM] * len(sums),
        scratch_shapes=[
            pltpu.VMEM((copies, xr, LANES), F32),
            pltpu.SemaphoreType.DMA((copies,)),
        ],
        input_output_aliases={len(arrays): 0, len(arrays) + 1: 1} if begun else {},
        compiler_params=limits(arrays, copies * xr * LANES * 4),
        cost_estimate=pl.CostEstimate(flops=0, bytes_accessed=moved, transcendentals=0),
    )(*inputs, *after)


def local(
    features, w_neigh, w_self, bias, cotangent, block_rows, block_cols, block_vals, block_count
):
    rs = lax.axis_size("row")
    cs = lax.axis_size("col")
    nd, depth = features.shape
    hid = w_self.shape[1]
    rt = nd * cs
    half = rs // 2
    xw = 2 * depth // cs
    nc = min(rs, hid // LANES)
    nr = rs // nc
    xr = xw // nr

    def along_col(x, k):
        return lax.ppermute(x, "col", [(s, s ^ k) for s in range(cs)])

    def along_chips(x, k):
        return lax.ppermute(x, "row", [(s, s ^ (2 * k)) for s in range(rs)])

    def other_core(x):
        return lax.ppermute(x, "row", [(s, s ^ 1) for s in range(rs)])

    def gather_chips(x):
        found = {0: x}
        step = half // 2
        while step:
            found.update({d + step: along_chips(found[d], step) for d in list(found)})
            step //= 2
        return [found[d] for d in range(half)]

    if rs == 2 * cs:

        def send_own(block, t):
            pairs = []
            for z in range(half):
                for core in range(2):
                    q = 2 * (z ^ t) + core
                    source = (2 * z + core) * cs + z
                    pairs.append((source, (2 * z + q // cs) * cs + q % cs))
            return lax.ppermute(block, ("row", "col"), pairs)

    else:
        swap = [((b % rs) * cs + b // rs, b) for b in range(rs * cs)]

        def send_own(block, t):
            return lax.ppermute(block, ("row", "col"), swap if t == 0 else [])

    near = along_chips(features, 1)
    mine_first = {0: features, 1: near}
    step = half // 2
    while step > 1:
        evens = [d for d in mine_first if d % 2 == 0]
        mine_first.update({d + step: along_chips(mine_first[d], step) for d in evens})
        step //= 2
    theirs_first = {0: other_core(features), 1: other_core(near)}
    own_feats = {0: send_own(features, 0)}
    tile, turned = densify(
        block_rows.reshape(-1),
        block_cols.reshape(-1),
        block_count.reshape(-1),
        block_vals[0, 0],
        nd,
        rs,
        cs,
        [],
    )
    mine_last = {d + 1: along_chips(x, 1) for d, x in mine_first.items() if d > 1}
    theirs_first.update({d: other_core(x) for d, x in mine_first.items() if d > 1})
    theirs_last = {d: other_core(x) for d, x in mine_last.items()}
    own_feats[1] = send_own(near, 1)

    def placed(mine, theirs):
        places = list(mine) + [half + d for d in theirs]
        return places, [*mine.values(), *theirs.values()]

    begun = forward_first(
        tile, *placed(mine_first, theirs_first), nd, [own_feats[0], own_feats[1]]
    )
    degree = row_sums(tile, nd, cs)
    step = 1
    while step < cs:
        masses = [degree, along_col(degree, step)]
        degree = masses[0] + masses[1]
        step *= 2
    evens = {d: send_own(follow(x, [begun, masses[0]]), d) for d, x in mine_first.items() if d > 1}
    own_feats.update(evens)
    own_feats.update({d: send_own(x, d) for d, x in mine_last.items()})
    parts = forward_parts(begun, tile, *placed(mine_last, theirs_last), nd, cs, list(evens.values()))
    own_feat = sum(list(own_feats.values())[1:], own_feats[0])
    inverse = 1.0 / (degree[0] + 1.0)
    inverse = jnp.broadcast_to(inverse[:, None], (rt, LANES))
    own = jnp.dot(own_feat, w_self, preferred_element_type=F32).astype(BF16)

    turned_neigh, turned_self = turn([w_neigh, w_self], [parts[0]])
    parts = [parts[0]] + [along_col(parts[k], k) for k in range(1, cs)]
    output, sums, *packs = activation(
        parts, masses, own, own_feat, w_neigh, bias[None, :], cotangent, [turned_neigh]
    )
    packs = [packs[0]] + [along_col(packs[k], k) for k in range(1, cs)]

    mid = cs // 2
    scaled_args = (inverse, turned_neigh, turned_self, cs, rs)
    early = scaled_parts(packs[:mid], 0, *scaled_args)
    keep, send = weight_parts(packs, sums, rs, xr, nc, early[:1])
    came = other_core(send)
    late = scaled_parts(packs[mid:], mid, *scaled_args, [keep])
    scaled, self_parts = zip(early, late)
    chunks = pair_sum(keep, came)
    chunks = [chunks[0]] + [along_chips(chunks[k], k) for k in range(half - 1, 0, -1)]
    keep, send = back_parts(turned, scaled, self_parts, nd, cs, rs, [keep])
    chunk, send = last_sum(chunks, send)
    line = gather_chips(chunk)
    keep, send = fold(keep, other_core(send), line[1:])
    line = stack(line, after=[send])
    step = 1
    while 2 * step < half:
        keep, send = fold(keep, along_chips(send, step))
        step *= 2
    last = (keep, along_chips(send, step))

    def piece(array, first, column, mine):
        return array, [(first + t, column) for t in range(array.shape[0])], mine

    mid = half // 2
    if cs == 4 and mid:
        first, second = along_col(line, 1), along_col(line, 2)
        near = [(line, 0, 0), (first, 0, 1), (second, 0, 2)]
        rest = [(along_col(first[:mid], 2), 0, 3), (along_col(second[mid:], 1), mid, 3)]
    else:
        near = [(line, 0, 0)] + [(along_col(line, k), 0, k) for k in range(1, cs - 1)]
        rest = [(along_col(line, cs - 1), 0, cs - 1)]
    factor = 1.0 / math.sqrt(nd * rs * cs)
    sizes = (depth, hid, xr, nc, cs, (factor, 32.0 * factor))
    pieces = [piece(*x, True) for x in near + rest]
    *begun, grad_input = assemble(pieces, (), *sizes, (), last)
    pieces = [piece(other_core(x), *where, False) for x, *where in near + rest]
    total_self, total_neigh, total_bias = assemble(pieces, begun, *sizes, ())
    return output, grad_input, total_self, total_neigh, total_bias.reshape(-1)


def solution(mesh):
    in_specs = (
        P(("col", "row"), None),
        P(),
        P(),
        P(),
        P(("row", "col"), None),
        P("row", "col", None),
        P("row", "col", None),
        P("row", "col", None, None, None),
        P("row", "col"),
    )
    out_specs = (P(("row", "col"), None), P(("col", "row"), None), P(), P(), P())
    return jax.shard_map(local, mesh=mesh, in_specs=in_specs, out_specs=out_specs, check_vma=False)
```

```python
import math

import jax
import jax.numpy as jnp
from jax import lax
from jax.experimental import pallas as pl
from jax.experimental.pallas import tpu as pltpu
from jax.sharding import PartitionSpec as P

F32 = jnp.float32
BF16 = jnp.bfloat16
LANES = 128
EXTRA = 16
VMEM = pl.BlockSpec(memory_space=pltpu.VMEM)
SMEM = pl.BlockSpec(memory_space=pltpu.SMEM)
MIB = 1024 * 1024


def limits(arrays, scratch=0):
    held = sum(math.prod(a.shape) * a.dtype.itemsize for a in arrays) + scratch
    return pltpu.CompilerParams(vmem_limit_bytes=min(56 * MIB, 2 * held + 12 * MIB))


def call(body, outs, args, scratch=(), smem=0, flops=0, after=()):
    count = len(args)
    moved = sum(math.prod(a.shape) * a.dtype.itemsize for a in (*outs, *args))
    held = sum(math.prod(x.shape) * x.dtype.itemsize for x in scratch)

    def run(*refs):
        body(*refs[:count], *refs[count + len(after) :])

    return pl.pallas_call(
        run,
        out_shape=outs,
        in_specs=[SMEM] * smem
        + [VMEM] * (count - smem)
        + [pl.BlockSpec(memory_space=pl.ANY)] * len(after),
        out_specs=[VMEM] * len(outs),
        scratch_shapes=list(scratch),
        compiler_params=limits([*outs, *args], held),
        cost_estimate=pl.CostEstimate(flops=flops, bytes_accessed=moved, transcendentals=0),
    )(*args, *after)


def shape(dims, dtype):
    return jax.ShapeDtypeStruct(tuple(dims), dtype)


def mm(a, b, ca=1, cb=0):
    return lax.dot_general(a, b, (((ca,), (cb,)), ((), ())), preferred_element_type=F32)


def follow(x, after):
    def body(x_ref, out_ref):
        out_ref[...] = x_ref[...]

    return call(body, [shape(x.shape, x.dtype)], [x], after=after)[0]


def turn(weights, after):
    def body(*refs):
        for ref, out_ref in zip(refs, refs[len(weights) :]):
            out_ref[...] = ref[...].T

    return call(body, [shape(w.shape[::-1], w.dtype) for w in weights], weights, after=after)


def stack(parts, joined=False, after=()):
    count = parts[0].shape[0] if joined else 1

    def body(*refs):
        for k, ref in enumerate(refs[:-1]):
            if joined:
                refs[-1][k * count : (k + 1) * count] = ref[...]
            else:
                refs[-1][k] = ref[...]

    dims = parts[0].shape[1:] if joined else parts[0].shape
    out = shape((len(parts) * count, *dims), parts[0].dtype)
    return call(body, [out], parts, after=after)[0]


def densify(rows, cols, count, values, nd, rs, cs, after):
    rt, ct, half = nd * cs, nd * rs, rs // 2

    def body(rows_ref, cols_ref, count_ref, values_ref, tile_ref, turned_ref, acc):
        i, j = lax.axis_index("row"), lax.axis_index("col")
        z, c = i // 2, lax.rem(i, 2)
        acc[...] = jnp.zeros_like(acc)

        def add(s, carry):
            col = cols_ref[s]
            row = rows_ref[s] ^ j
            col = (z ^ (col // 2)) + half * (lax.rem(col, 2) ^ c)
            r = pl.multiple_of(row * nd, nd)
            c0 = pl.multiple_of(col * nd, nd)
            acc[pl.ds(r, nd), pl.ds(c0, nd)] += values_ref[s].astype(F32)
            return carry

        lax.fori_loop(0, count_ref[0], add, 0)
        tile_ref[...] = acc[...].astype(BF16)
        for k in range(rs):
            cut = acc[:, k * nd : (k + 1) * nd]
            turned_ref[k * nd : (k + 1) * nd, :] = cut.T.astype(BF16)

    return call(
        body,
        [shape((rt, ct), BF16), shape((ct, rt), BF16)],
        [rows, cols, count, values],
        [pltpu.VMEM((rt, ct), F32)],
        smem=3,
        flops=rt * ct,
        after=after,
    )


def tile_columns(tile_ref, places, nd):
    return jnp.concatenate([tile_ref[:, p * nd : (p + 1) * nd] for p in places], axis=1)


def row_sums(tile, nd, cs):
    rt, ct = tile.shape

    def body(tile_ref, mass_ref):
        j = lax.axis_index("col")
        ones = jnp.ones((8, ct), BF16)
        for k in range(cs):
            place = pl.multiple_of((j ^ k) * nd, nd)
            mass_ref[:, pl.ds(place, nd)] = mm(ones, tile_ref[k * nd : (k + 1) * nd, :], 1, 1)

    return call(body, [shape((8, rt), F32)], [tile], flops=16 * tile.size)[0]


def forward_first(tile, places, blocks, nd, after):
    rt = tile.shape[0]
    width = blocks[0].shape[1]

    def body(*refs):
        tile_ref, feat_refs = refs[0], refs[1 : 1 + len(blocks)]
        sum_ref = refs[1 + len(blocks)]
        feats = jnp.concatenate([r[...] for r in feat_refs], axis=0)
        sum_ref[...] = mm(tile_columns(tile_ref, places, nd), feats)

    return call(
        body,
        [shape((rt, width), F32)],
        [tile, *blocks],
        flops=2 * rt * len(places) * nd * width,
        after=after,
    )[0]


def forward_parts(begun, tile, places, blocks, nd, cs, after):
    width = blocks[0].shape[1]

    def body(*refs):
        sum_ref, tile_ref, feat_refs = refs[0], refs[1], refs[2 : 2 + len(blocks)]
        outs = refs[2 + len(blocks) :]
        feats = jnp.concatenate([r[...] for r in feat_refs], axis=0)
        parts = sum_ref[...] + mm(tile_columns(tile_ref, places, nd), feats)
        for k in range(cs):
            outs[k][...] = parts[k * nd : (k + 1) * nd].astype(outs[k].dtype)

    return call(
        body,
        [shape((nd, width), BF16 if k else F32) for k in range(cs)],
        [begun, tile, *blocks],
        flops=2 * tile.shape[0] * len(places) * nd * width,
        after=after,
    )


def activation(parts, masses, own, own_feat, w_neigh, bias, cotangent, after):
    cs = len(parts)
    nd, hid = own.shape
    depth = own_feat.shape[1]
    xw = 2 * depth // cs

    def body(*refs):
        part_refs = refs[:cs]
        mass_refs = refs[cs : cs + 2]
        own_ref, feat_ref, w_ref, bias_ref, cot_ref = refs[cs + 2 : cs + 7]
        out_ref, sum_ref, *packs = refs[cs + 7 : -1]
        both = refs[-1]
        j = lax.axis_index("col")
        here = pl.ds(pl.multiple_of(j * nd, nd), nd)
        inv = 1.0 / (mass_refs[0][:, here] + mass_refs[1][:, here] + 1.0)
        inv = jnp.broadcast_to(inv.T[:, :1], (nd, LANES))
        total = sum(r[...].astype(F32) for r in part_refs)
        mean = (total * jnp.concatenate([inv] * (depth // LANES), axis=1)).astype(BF16)
        both[:, :depth] = feat_ref[...]
        both[:, depth:] = mean
        pre = own_ref[...].astype(F32) + mm(mean, w_ref[...]) + bias_ref[...]
        slope = jnp.where(pre > 0, 1.0, jnp.exp(jnp.minimum(pre, 0.0)))
        out_ref[...] = jnp.where(pre > 0, pre, slope - 1.0).astype(BF16)
        grad = cot_ref[...].astype(F32) * slope
        sum_ref[...] = jnp.broadcast_to(jnp.sum(grad, axis=0, keepdims=True), (8, hid))
        grad = grad.astype(BF16)
        for k in range(cs):
            packs[k][:, :hid] = grad
            target = j ^ k
            if xw % LANES == 0:
                start = pl.multiple_of(target * xw, LANES)
                packs[k][:, hid:] = both[:, pl.ds(start, xw)]
            else:
                for d in range(cs):

                    @pl.when(target == d)
                    def _():
                        packs[k][:, hid:] = both[:, d * xw : (d + 1) * xw]

    return call(
        body,
        [shape((nd, hid), BF16), shape((8, hid), F32)] + [shape((nd, hid + xw), BF16)] * cs,
        [*parts, *masses, own, own_feat, w_neigh, bias, cotangent],
        [pltpu.VMEM((nd, 2 * depth), BF16)],
        flops=2 * own_feat.size * hid,
        after=after,
    )


def split_pair(total):
    high = total.astype(BF16).astype(F32)
    return jnp.concatenate([high, total - high], axis=0)


def weight_parts(packs, sums, rs, xr, nc, after):
    cs = len(packs)
    hid = sums.shape[1]
    nd, xw = packs[0].shape[0], packs[0].shape[1] - hid
    half = rs // 2

    def body(*refs):
        pack_refs = refs[:cs]
        sum_ref, keep_ref, send_ref, acc = refs[cs:]
        x_all = jnp.concatenate([r[:, hid:] for r in pack_refs], axis=0)
        g_all = jnp.concatenate([r[:, :hid] for r in pack_refs], axis=0)
        acc[...] = mm(x_all, g_all, 0, 0)
        i = lax.axis_index("row")
        z, c = i // 2, lax.rem(i, 2)
        for k in range(half):
            for core, ref in ((c, keep_ref), (1 - c, send_ref)):
                q = 2 * (z ^ k) + core
                row = pl.multiple_of((q // nc) * xr, xr)
                col = pl.multiple_of(lax.rem(q, nc) * LANES, LANES)
                ref[k, :xr, :] = acc[pl.ds(row, xr), pl.ds(col, LANES)].astype(ref.dtype)
                ref[k, xr:, :] = split_pair(sum_ref[:, pl.ds(col, LANES)]).astype(ref.dtype)

    dims = (half, xr + EXTRA, LANES)
    return call(
        body,
        [shape(dims, F32), shape(dims, BF16)],
        [*packs, sums],
        [pltpu.VMEM((xw, hid), F32)],
        flops=2 * cs * nd * xw * hid,
        after=after,
    )


def scaled_parts(packs, first, inverse, turned_neigh, turned_self, cs, rs, after=()):
    count = len(packs)
    nd = packs[0].shape[0]
    hid, depth = turned_neigh.shape

    def body(neigh_ref, own_ref, inv_ref, *refs):
        pack_refs, scaled_ref, self_ref = refs[:count], refs[count], refs[count + 1]
        i, j = lax.axis_index("row"), lax.axis_index("col")
        grads = jnp.concatenate([r[:, :hid] for r in pack_refs], axis=0)
        product = mm(grads, neigh_ref[...])
        for r in range(count):
            start = pl.multiple_of((j ^ (first + r)) * nd, nd)
            inv = inv_ref[pl.ds(start, nd), :]
            inv = jnp.concatenate([inv] * (depth // LANES), axis=1)
            rows = slice(r * nd, (r + 1) * nd)
            scaled_ref[rows, :] = (product[rows] * inv).astype(BF16)

        @pl.when(i * cs // rs == j)
        def _():
            self_ref[...] = mm(grads, own_ref[...])

    return call(
        body,
        [shape((count * nd, depth), BF16), shape((count * nd, depth), F32)],
        [turned_neigh, turned_self, inverse, *packs],
        flops=4 * count * nd * hid * depth,
        after=after,
    )


def halving_order(count):
    order = [0]
    step = count // 2
    while step:
        order = order + [d + step for d in order]
        step //= 2
    return order


def back_parts(turned, scaled, self_parts, nd, cs, rs, after):
    depth = scaled[0].shape[1]
    half = rs // 2
    count = len(scaled)
    each = cs // count

    def body(tile_ref, *refs):
        scaled_refs, self_refs = refs[:count], refs[count : 2 * count]
        keep_ref, send_ref, acc = refs[2 * count :]
        i, j = lax.axis_index("row"), lax.axis_index("col")
        z, c = i // 2, lax.rem(i, 2)
        acc[...] = mm(tile_ref[...], jnp.concatenate([r[...] for r in scaled_refs], axis=0))

        @pl.when(i * cs // rs == j)
        def _():
            for r in range(cs):
                q = i * cs - j * rs + (j ^ r)
                place = ((z ^ (q // 2)) + half * (lax.rem(q, 2) ^ c)) * nd
                rows = slice(r % each * nd, (r % each + 1) * nd)
                acc[pl.ds(pl.multiple_of(place, nd), nd), :] += self_refs[r // each][rows]

        for ref, base in ((send_ref, half), (keep_ref, 0)):
            for k, distance in enumerate(halving_order(half)):
                place = (base + distance) * nd
                ref[k] = acc[place : place + nd, :].astype(ref.dtype)

    dims = (half, nd, depth)
    return call(
        body,
        [shape(dims, F32), shape(dims, BF16)],
        [turned, *scaled, *self_parts],
        [pltpu.VMEM((rs * nd, depth), F32)],
        flops=2 * turned.size * depth,
        after=after,
    )


def fold(keep, came, after=()):
    count, rows, width = keep.shape
    half = count // 2

    def body(keep_ref, came_ref, *outs):
        total = keep_ref[...] + came_ref[...].astype(F32)
        outs[0][...] = total[:half]
        outs[1][...] = total[half:].astype(BF16)

    dims = (half, rows, width)
    return call(body, [shape(dims, F32), shape(dims, BF16)], [keep, came], after=after)


def pair_sum(keep, came):
    half, rows, width = keep.shape
    main = rows - EXTRA

    def body(keep_ref, came_ref, *outs):
        for k in range(half):
            total = keep_ref[k] + came_ref[k].astype(F32)
            dtype = outs[k].dtype
            outs[k][:main, :] = total[:main].astype(dtype)
            merged = total[main : main + 8] + total[main + 8 :]
            outs[k][main:, :] = split_pair(merged).astype(dtype)

    return call(
        body,
        [shape((rows, width), BF16 if k else F32) for k in range(half)],
        [keep, came],
    )


def last_sum(parts, passed):
    rows, width = parts[0].shape
    main = rows - EXTRA

    def body(*refs):
        *part_refs, passed_ref, out_ref, again_ref = refs
        total = part_refs[0][...]
        for ref in part_refs[1:]:
            total = total + ref[...].astype(F32)
        out_ref[:main, :] = total[:main].astype(BF16)
        merged = total[main : main + 8] + total[main + 8 :]
        out_ref[main:, :] = split_pair(merged).astype(BF16)
        again_ref[...] = passed_ref[...]

    outs = [shape((rows, width), BF16), shape(passed.shape, passed.dtype)]
    return call(body, outs, [*parts, passed])


def assemble(pieces, begun, depth, hid, xr, nc, cs, factors, after, adds=()):
    xw = 2 * depth // cs
    side = cs // 2
    copies = sum(len(where) for _, where, _ in pieces)
    arrays = [array for array, _, _ in pieces]
    inputs = arrays + list(begun) + list(adds)
    weight = shape((depth, hid), F32)

    def body(*refs):
        piece_refs = refs[: len(pieces)]
        self_ref, neigh_ref, bias_ref, *sum_ref, staged, sems = refs[len(inputs) :]
        i, j = lax.axis_index("row"), lax.axis_index("col")
        z, c = i // 2, lax.rem(i, 2)
        if begun:
            bias_ref[...] = refs[len(arrays) + 2][...]
        else:
            bias_ref[...] = jnp.zeros_like(bias_ref)
        waits = []
        at = 0
        for ref, (_, where, mine) in zip(piece_refs, pieces):
            for t, (distance, column) in enumerate(where):
                owner = j ^ column
                first = owner < side
                q = 2 * (z ^ distance) + (c if mine else 1 - c)
                col = pl.multiple_of(lax.rem(q, nc) * LANES, LANES)
                turn = q // nc
                row = pl.multiple_of(lax.rem(owner, side) * xw + turn * xr, xr)
                scale = jnp.where(first, factors[0], factors[1])
                staged[at] = ref[t, :xr, :].astype(F32) * scale
                for target, here in ((self_ref, first), (neigh_ref, jnp.logical_not(first))):
                    copy = pltpu.make_async_copy(
                        staged.at[at],
                        target.at[pl.ds(row, xr), pl.ds(col, LANES)],
                        sems.at[at],
                    )
                    pl.when(here)(copy.start)
                    waits.append((here, copy))

                @pl.when(turn == 0)
                def _():
                    total = ref[t, xr:, :].astype(F32)
                    total = (total[:1] + total[8:9]) * factors[0]
                    bias_ref[:, pl.ds(col, LANES)] += total

                at += 1
        if adds:
            keep_ref, came_ref = refs[len(inputs) - 2 : len(inputs)]
            sum_ref[0][...] = (keep_ref[0] + came_ref[0].astype(F32)).astype(BF16)
        for here, copy in waits:
            pl.when(here)(copy.wait)

    def run(*refs):
        body(*refs[: len(inputs)], *refs[len(inputs) + len(after) :])

    somewhere = pl.BlockSpec(memory_space=pl.ANY)
    sums = [shape(adds[0].shape[1:], BF16)] if adds else []
    moved = 2 * copies * xr * LANES * 6
    return pl.pallas_call(
        run,
        out_shape=[weight, weight, shape((1, hid), F32), *sums],
        in_specs=[VMEM] * len(arrays)
        + ([somewhere, somewhere, VMEM] if begun else [])
        + [VMEM] * len(adds)
        + [somewhere] * len(after),
        out_specs=[somewhere, somewhere, VMEM] + [VMEM] * len(sums),
        scratch_shapes=[
            pltpu.VMEM((copies, xr, LANES), F32),
            pltpu.SemaphoreType.DMA((copies,)),
        ],
        input_output_aliases={len(arrays): 0, len(arrays) + 1: 1} if begun else {},
        compiler_params=limits(arrays, copies * xr * LANES * 4),
        cost_estimate=pl.CostEstimate(flops=0, bytes_accessed=moved, transcendentals=0),
    )(*inputs, *after)


def local(
    features, w_neigh, w_self, bias, cotangent, block_rows, block_cols, block_vals, block_count
):
    rs = lax.axis_size("row")
    cs = lax.axis_size("col")
    nd, depth = features.shape
    hid = w_self.shape[1]
    rt = nd * cs
    half = rs // 2
    xw = 2 * depth // cs
    nc = min(rs, hid // LANES)
    nr = rs // nc
    xr = xw // nr

    def along_col(x, k):
        return lax.ppermute(x, "col", [(s, s ^ k) for s in range(cs)])

    def along_chips(x, k):
        return lax.ppermute(x, "row", [(s, s ^ (2 * k)) for s in range(rs)])

    def other_core(x):
        return lax.ppermute(x, "row", [(s, s ^ 1) for s in range(rs)])

    def gather_chips(x):
        found = {0: x}
        step = half // 2
        while step:
            found.update({d + step: along_chips(found[d], step) for d in list(found)})
            step //= 2
        return [found[d] for d in range(half)]

    if rs == 2 * cs:

        def send_own(block, t):
            pairs = []
            for z in range(half):
                for core in range(2):
                    q = 2 * (z ^ t) + core
                    source = (2 * z + core) * cs + z
                    pairs.append((source, (2 * z + q // cs) * cs + q % cs))
            return lax.ppermute(block, ("row", "col"), pairs)

    else:
        swap = [((b % rs) * cs + b // rs, b) for b in range(rs * cs)]

        def send_own(block, t):
            return lax.ppermute(block, ("row", "col"), swap if t == 0 else [])

    near = along_chips(features, 1)
    mine_first = {0: features, 1: near}
    step = half // 2
    while step > 1:
        evens = [d for d in mine_first if d % 2 == 0]
        mine_first.update({d + step: along_chips(mine_first[d], step) for d in evens})
        step //= 2
    theirs_first = {0: other_core(features), 1: other_core(near)}
    own_feats = {0: send_own(features, 0)}
    tile, turned = densify(
        block_rows.reshape(-1),
        block_cols.reshape(-1),
        block_count.reshape(-1),
        block_vals[0, 0],
        nd,
        rs,
        cs,
        [],
    )
    mine_last = {d + 1: along_chips(x, 1) for d, x in mine_first.items() if d > 1}
    theirs_first.update({d: other_core(x) for d, x in mine_first.items() if d > 1})
    theirs_last = {d: other_core(x) for d, x in mine_last.items()}
    own_feats[1] = send_own(near, 1)

    def placed(mine, theirs):
        places = list(mine) + [half + d for d in theirs]
        return places, [*mine.values(), *theirs.values()]

    begun = forward_first(
        tile, *placed(mine_first, theirs_first), nd, [own_feats[0], own_feats[1]]
    )
    degree = row_sums(tile, nd, cs)
    step = 1
    while step < cs:
        masses = [degree, along_col(degree, step)]
        degree = masses[0] + masses[1]
        step *= 2
    evens = {d: send_own(follow(x, [begun, masses[0]]), d) for d, x in mine_first.items() if d > 1}
    own_feats.update(evens)
    own_feats.update({d: send_own(x, d) for d, x in mine_last.items()})
    parts = forward_parts(begun, tile, *placed(mine_last, theirs_last), nd, cs, list(evens.values()))
    own_feat = sum(list(own_feats.values())[1:], own_feats[0])
    inverse = 1.0 / (degree[0] + 1.0)
    inverse = jnp.broadcast_to(inverse[:, None], (rt, LANES))
    own = jnp.dot(own_feat, w_self, preferred_element_type=F32).astype(BF16)

    turned_neigh, turned_self = turn([w_neigh, w_self], [parts[0]])
    parts = [parts[0]] + [along_col(parts[k], k) for k in range(1, cs)]
    output, sums, *packs = activation(
        parts, masses, own, own_feat, w_neigh, bias[None, :], cotangent, [turned_neigh]
    )
    packs = [packs[0]] + [along_col(packs[k], k) for k in range(1, cs)]

    mid = cs // 2
    scaled_args = (inverse, turned_neigh, turned_self, cs, rs)
    early = scaled_parts(packs[:mid], 0, *scaled_args)
    keep, send = weight_parts(packs, sums, rs, xr, nc, early[:1])
    came = other_core(send)
    late = scaled_parts(packs[mid:], mid, *scaled_args, [keep])
    scaled, self_parts = zip(early, late)
    chunks = pair_sum(keep, came)
    chunks = [chunks[0]] + [along_chips(chunks[k], k) for k in range(half - 1, 0, -1)]
    keep, send = back_parts(turned, scaled, self_parts, nd, cs, rs, [keep])
    chunk, send = last_sum(chunks, send)
    line = gather_chips(chunk)
    keep, send = fold(keep, other_core(send))
    line = stack(line, after=[send])
    step = 1
    while 2 * step < half:
        keep, send = fold(keep, along_chips(send, step))
        step *= 2
    last = (keep, along_chips(send, step))

    def piece(array, first, column, mine):
        return array, [(first + t, column) for t in range(array.shape[0])], mine

    mid = half // 2
    if cs == 4 and mid:
        first, second = along_col(line, 1), along_col(line, 2)
        near = [(line, 0, 0), (first, 0, 1), (second, 0, 2)]
        rest = [(along_col(first[:mid], 2), 0, 3), (along_col(second[mid:], 1), mid, 3)]
    else:
        near = [(line, 0, 0)] + [(along_col(line, k), 0, k) for k in range(1, cs - 1)]
        rest = [(along_col(line, cs - 1), 0, cs - 1)]
    factor = 1.0 / math.sqrt(nd * rs * cs)
    sizes = (depth, hid, xr, nc, cs, (factor, 32.0 * factor))
    pieces = [piece(*x, True) for x in near + rest]
    *begun, grad_input = assemble(pieces, (), *sizes, (), last)
    pieces = [piece(other_core(x), *where, False) for x, *where in near + rest]
    total_self, total_neigh, total_bias = assemble(pieces, begun, *sizes, ())
    return output, grad_input, total_self, total_neigh, total_bias.reshape(-1)


def solution(mesh):
    in_specs = (
        P(("col", "row"), None),
        P(),
        P(),
        P(),
        P(("row", "col"), None),
        P("row", "col", None),
        P("row", "col", None),
        P("row", "col", None, None, None),
        P("row", "col"),
    )
    out_specs = (P(("row", "col"), None), P(("col", "row"), None), P(), P(), P())
    return jax.shard_map(local, mesh=mesh, in_specs=in_specs, out_specs=out_specs, check_vma=False)
```

```python
import math

import jax
import jax.numpy as jnp
from jax import lax
from jax.experimental import pallas as pl
from jax.experimental.pallas import tpu as pltpu
from jax.sharding import PartitionSpec as P

F32 = jnp.float32
BF16 = jnp.bfloat16
LANES = 128
EXTRA = 16
VMEM = pl.BlockSpec(memory_space=pltpu.VMEM)
SMEM = pl.BlockSpec(memory_space=pltpu.SMEM)
MIB = 1024 * 1024


def limits(arrays, scratch=0):
    held = sum(math.prod(a.shape) * a.dtype.itemsize for a in arrays) + scratch
    return pltpu.CompilerParams(vmem_limit_bytes=min(56 * MIB, 2 * held + 12 * MIB))


def call(body, outs, args, scratch=(), smem=0, flops=0, after=()):
    count = len(args)
    moved = sum(math.prod(a.shape) * a.dtype.itemsize for a in (*outs, *args))
    held = sum(math.prod(x.shape) * x.dtype.itemsize for x in scratch)

    def run(*refs):
        body(*refs[:count], *refs[count + len(after) :])

    return pl.pallas_call(
        run,
        out_shape=outs,
        in_specs=[SMEM] * smem
        + [VMEM] * (count - smem)
        + [pl.BlockSpec(memory_space=pl.ANY)] * len(after),
        out_specs=[VMEM] * len(outs),
        scratch_shapes=list(scratch),
        compiler_params=limits([*outs, *args], held),
        cost_estimate=pl.CostEstimate(flops=flops, bytes_accessed=moved, transcendentals=0),
    )(*args, *after)


def shape(dims, dtype):
    return jax.ShapeDtypeStruct(tuple(dims), dtype)


def mm(a, b, ca=1, cb=0):
    return lax.dot_general(a, b, (((ca,), (cb,)), ((), ())), preferred_element_type=F32)


def follow(x, after):
    def body(x_ref, out_ref):
        out_ref[...] = x_ref[...]

    return call(body, [shape(x.shape, x.dtype)], [x], after=after)[0]


def turn(weights, after):
    def body(*refs):
        for ref, out_ref in zip(refs, refs[len(weights) :]):
            out_ref[...] = ref[...].T

    return call(body, [shape(w.shape[::-1], w.dtype) for w in weights], weights, after=after)


def stack(parts, joined=False, after=()):
    count = parts[0].shape[0] if joined else 1

    def body(*refs):
        for k, ref in enumerate(refs[:-1]):
            if joined:
                refs[-1][k * count : (k + 1) * count] = ref[...]
            else:
                refs[-1][k] = ref[...]

    dims = parts[0].shape[1:] if joined else parts[0].shape
    out = shape((len(parts) * count, *dims), parts[0].dtype)
    return call(body, [out], parts, after=after)[0]


def densify(rows, cols, count, values, nd, rs, cs, after):
    rt, ct, half = nd * cs, nd * rs, rs // 2

    def body(rows_ref, cols_ref, count_ref, values_ref, tile_ref, turned_ref, acc):
        i, j = lax.axis_index("row"), lax.axis_index("col")
        z, c = i // 2, lax.rem(i, 2)
        acc[...] = jnp.zeros_like(acc)

        def add(s, carry):
            col = cols_ref[s]
            row = rows_ref[s] ^ j
            col = (z ^ (col // 2)) + half * (lax.rem(col, 2) ^ c)
            r = pl.multiple_of(row * nd, nd)
            c0 = pl.multiple_of(col * nd, nd)
            acc[pl.ds(r, nd), pl.ds(c0, nd)] += values_ref[s].astype(F32)
            return carry

        lax.fori_loop(0, count_ref[0], add, 0)
        tile_ref[...] = acc[...].astype(BF16)
        for k in range(rs):
            cut = acc[:, k * nd : (k + 1) * nd]
            turned_ref[k * nd : (k + 1) * nd, :] = cut.T.astype(BF16)

    return call(
        body,
        [shape((rt, ct), BF16), shape((ct, rt), BF16)],
        [rows, cols, count, values],
        [pltpu.VMEM((rt, ct), F32)],
        smem=3,
        flops=rt * ct,
        after=after,
    )


def tile_columns(tile_ref, places, nd):
    return jnp.concatenate([tile_ref[:, p * nd : (p + 1) * nd] for p in places], axis=1)


def row_sums(tile, nd, cs):
    rt, ct = tile.shape

    def body(tile_ref, mass_ref):
        j = lax.axis_index("col")
        ones = jnp.ones((8, ct), BF16)
        for k in range(cs):
            place = pl.multiple_of((j ^ k) * nd, nd)
            mass_ref[:, pl.ds(place, nd)] = mm(ones, tile_ref[k * nd : (k + 1) * nd, :], 1, 1)

    return call(body, [shape((8, rt), F32)], [tile], flops=16 * tile.size)[0]


def forward_first(tile, places, blocks, nd, after):
    rt = tile.shape[0]
    width = blocks[0].shape[1]

    def body(*refs):
        tile_ref, feat_refs = refs[0], refs[1 : 1 + len(blocks)]
        sum_ref = refs[1 + len(blocks)]
        feats = jnp.concatenate([r[...] for r in feat_refs], axis=0)
        sum_ref[...] = mm(tile_columns(tile_ref, places, nd), feats)

    return call(
        body,
        [shape((rt, width), F32)],
        [tile, *blocks],
        flops=2 * rt * len(places) * nd * width,
        after=after,
    )[0]


def forward_parts(begun, tile, places, blocks, nd, cs, after):
    width = blocks[0].shape[1]

    def body(*refs):
        sum_ref, tile_ref, feat_refs = refs[0], refs[1], refs[2 : 2 + len(blocks)]
        outs = refs[2 + len(blocks) :]
        feats = jnp.concatenate([r[...] for r in feat_refs], axis=0)
        parts = sum_ref[...] + mm(tile_columns(tile_ref, places, nd), feats)
        for k in range(cs):
            outs[k][...] = parts[k * nd : (k + 1) * nd].astype(outs[k].dtype)

    return call(
        body,
        [shape((nd, width), BF16 if k else F32) for k in range(cs)],
        [begun, tile, *blocks],
        flops=2 * tile.shape[0] * len(places) * nd * width,
        after=after,
    )


def activation(parts, masses, own, own_feat, w_neigh, bias, cotangent, after):
    cs = len(parts)
    nd, hid = own.shape
    depth = own_feat.shape[1]
    xw = 2 * depth // cs

    def body(*refs):
        part_refs = refs[:cs]
        mass_refs = refs[cs : cs + 2]
        own_ref, feat_ref, w_ref, bias_ref, cot_ref = refs[cs + 2 : cs + 7]
        out_ref, sum_ref, *packs = refs[cs + 7 : -1]
        both = refs[-1]
        j = lax.axis_index("col")
        here = pl.ds(pl.multiple_of(j * nd, nd), nd)
        inv = 1.0 / (mass_refs[0][:, here] + mass_refs[1][:, here] + 1.0)
        inv = jnp.broadcast_to(inv.T[:, :1], (nd, LANES))
        total = sum(r[...].astype(F32) for r in part_refs)
        mean = (total * jnp.concatenate([inv] * (depth // LANES), axis=1)).astype(BF16)
        both[:, :depth] = feat_ref[...]
        both[:, depth:] = mean
        pre = own_ref[...].astype(F32) + mm(mean, w_ref[...]) + bias_ref[...]
        slope = jnp.where(pre > 0, 1.0, jnp.exp(jnp.minimum(pre, 0.0)))
        out_ref[...] = jnp.where(pre > 0, pre, slope - 1.0).astype(BF16)
        grad = cot_ref[...].astype(F32) * slope
        sum_ref[...] = jnp.broadcast_to(jnp.sum(grad, axis=0, keepdims=True), (8, hid))
        grad = grad.astype(BF16)
        for k in range(cs):
            packs[k][:, :hid] = grad
            target = j ^ k
            if xw % LANES == 0:
                start = pl.multiple_of(target * xw, LANES)
                packs[k][:, hid:] = both[:, pl.ds(start, xw)]
            else:
                for d in range(cs):

                    @pl.when(target == d)
                    def _():
                        packs[k][:, hid:] = both[:, d * xw : (d + 1) * xw]

    return call(
        body,
        [shape((nd, hid), BF16), shape((8, hid), F32)] + [shape((nd, hid + xw), BF16)] * cs,
        [*parts, *masses, own, own_feat, w_neigh, bias, cotangent],
        [pltpu.VMEM((nd, 2 * depth), BF16)],
        flops=2 * own_feat.size * hid,
        after=after,
    )


def split_pair(total):
    high = total.astype(BF16).astype(F32)
    return jnp.concatenate([high, total - high], axis=0)


def weight_parts(packs, sums, rs, xr, nc, after):
    cs = len(packs)
    hid = sums.shape[1]
    nd, xw = packs[0].shape[0], packs[0].shape[1] - hid
    half = rs // 2

    def body(*refs):
        pack_refs = refs[:cs]
        sum_ref, keep_ref, send_ref, acc = refs[cs:]
        x_all = jnp.concatenate([r[:, hid:] for r in pack_refs], axis=0)
        g_all = jnp.concatenate([r[:, :hid] for r in pack_refs], axis=0)
        acc[...] = mm(x_all, g_all, 0, 0)
        i = lax.axis_index("row")
        z, c = i // 2, lax.rem(i, 2)
        for k in range(half):
            for core, ref in ((c, keep_ref), (1 - c, send_ref)):
                q = 2 * (z ^ k) + core
                row = pl.multiple_of((q // nc) * xr, xr)
                col = pl.multiple_of(lax.rem(q, nc) * LANES, LANES)
                ref[k, :xr, :] = acc[pl.ds(row, xr), pl.ds(col, LANES)].astype(ref.dtype)
                ref[k, xr:, :] = split_pair(sum_ref[:, pl.ds(col, LANES)]).astype(ref.dtype)

    dims = (half, xr + EXTRA, LANES)
    return call(
        body,
        [shape(dims, F32), shape(dims, BF16)],
        [*packs, sums],
        [pltpu.VMEM((xw, hid), F32)],
        flops=2 * cs * nd * xw * hid,
        after=after,
    )


def scaled_parts(packs, first, inverse, turned_neigh, turned_self, cs, rs, after=()):
    count = len(packs)
    nd = packs[0].shape[0]
    hid, depth = turned_neigh.shape

    def body(neigh_ref, own_ref, inv_ref, *refs):
        pack_refs, scaled_ref, self_ref = refs[:count], refs[count], refs[count + 1]
        i, j = lax.axis_index("row"), lax.axis_index("col")
        grads = jnp.concatenate([r[:, :hid] for r in pack_refs], axis=0)
        product = mm(grads, neigh_ref[...])
        for r in range(count):
            start = pl.multiple_of((j ^ (first + r)) * nd, nd)
            inv = inv_ref[pl.ds(start, nd), :]
            inv = jnp.concatenate([inv] * (depth // LANES), axis=1)
            rows = slice(r * nd, (r + 1) * nd)
            scaled_ref[rows, :] = (product[rows] * inv).astype(BF16)

        @pl.when(i * cs // rs == j)
        def _():
            self_ref[...] = mm(grads, own_ref[...])

    return call(
        body,
        [shape((count * nd, depth), BF16), shape((count * nd, depth), F32)],
        [turned_neigh, turned_self, inverse, *packs],
        flops=4 * count * nd * hid * depth,
        after=after,
    )


def halving_order(count):
    order = [0]
    step = count // 2
    while step:
        order = order + [d + step for d in order]
        step //= 2
    return order


def back_parts(turned, scaled, self_parts, nd, cs, rs, after):
    depth = scaled[0].shape[1]
    half = rs // 2
    count = len(scaled)
    each = cs // count

    def body(tile_ref, *refs):
        scaled_refs, self_refs = refs[:count], refs[count : 2 * count]
        keep_ref, send_ref, acc = refs[2 * count :]
        i, j = lax.axis_index("row"), lax.axis_index("col")
        z, c = i // 2, lax.rem(i, 2)
        acc[...] = mm(tile_ref[...], jnp.concatenate([r[...] for r in scaled_refs], axis=0))

        @pl.when(i * cs // rs == j)
        def _():
            for r in range(cs):
                q = i * cs - j * rs + (j ^ r)
                place = ((z ^ (q // 2)) + half * (lax.rem(q, 2) ^ c)) * nd
                rows = slice(r % each * nd, (r % each + 1) * nd)
                acc[pl.ds(pl.multiple_of(place, nd), nd), :] += self_refs[r // each][rows]

        for ref, base in ((send_ref, half), (keep_ref, 0)):
            for k, distance in enumerate(halving_order(half)):
                place = (base + distance) * nd
                ref[k] = acc[place : place + nd, :].astype(ref.dtype)

    dims = (half, nd, depth)
    return call(
        body,
        [shape(dims, F32), shape(dims, BF16)],
        [turned, *scaled, *self_parts],
        [pltpu.VMEM((rs * nd, depth), F32)],
        flops=2 * turned.size * depth,
        after=after,
    )


def fold(keep, came, after=()):
    count, rows, width = keep.shape
    half = count // 2

    def body(keep_ref, came_ref, *outs):
        total = keep_ref[...] + came_ref[...].astype(F32)
        outs[0][...] = total[:half]
        outs[1][...] = total[half:].astype(BF16)

    dims = (half, rows, width)
    return call(body, [shape(dims, F32), shape(dims, BF16)], [keep, came], after=after)


def pair_sum(keep, came):
    half, rows, width = keep.shape
    main = rows - EXTRA

    def body(keep_ref, came_ref, *outs):
        for k in range(half):
            total = keep_ref[k] + came_ref[k].astype(F32)
            dtype = outs[k].dtype
            outs[k][:main, :] = total[:main].astype(dtype)
            merged = total[main : main + 8] + total[main + 8 :]
            outs[k][main:, :] = split_pair(merged).astype(dtype)

    return call(
        body,
        [shape((rows, width), BF16 if k else F32) for k in range(half)],
        [keep, came],
    )


def last_sum(parts, passed):
    rows, width = parts[0].shape
    main = rows - EXTRA

    def body(*refs):
        *part_refs, passed_ref, out_ref, again_ref = refs
        total = part_refs[0][...]
        for ref in part_refs[1:]:
            total = total + ref[...].astype(F32)
        out_ref[:main, :] = total[:main].astype(BF16)
        merged = total[main : main + 8] + total[main + 8 :]
        out_ref[main:, :] = split_pair(merged).astype(BF16)
        again_ref[...] = passed_ref[...]

    outs = [shape((rows, width), BF16), shape(passed.shape, passed.dtype)]
    return call(body, outs, [*parts, passed])


def assemble(pieces, begun, depth, hid, xr, nc, cs, factors, after, adds=()):
    xw = 2 * depth // cs
    side = cs // 2
    copies = sum(len(where) for _, where, _ in pieces)
    arrays = [array for array, _, _ in pieces]
    inputs = arrays + list(begun) + list(adds)
    weight = shape((depth, hid), F32)

    def body(*refs):
        piece_refs = refs[: len(pieces)]
        self_ref, neigh_ref, bias_ref, *sum_ref, staged, sems = refs[len(inputs) :]
        i, j = lax.axis_index("row"), lax.axis_index("col")
        z, c = i // 2, lax.rem(i, 2)
        if begun:
            bias_ref[...] = refs[len(arrays) + 2][...]
        else:
            bias_ref[...] = jnp.zeros_like(bias_ref)
        waits = []
        at = 0
        for ref, (_, where, mine) in zip(piece_refs, pieces):
            for t, (distance, column) in enumerate(where):
                owner = j ^ column
                first = owner < side
                q = 2 * (z ^ distance) + (c if mine else 1 - c)
                col = pl.multiple_of(lax.rem(q, nc) * LANES, LANES)
                turn = q // nc
                row = pl.multiple_of(lax.rem(owner, side) * xw + turn * xr, xr)
                scale = jnp.where(first, factors[0], factors[1])
                staged[at] = ref[t, :xr, :].astype(F32) * scale
                for target, here in ((self_ref, first), (neigh_ref, jnp.logical_not(first))):
                    copy = pltpu.make_async_copy(
                        staged.at[at],
                        target.at[pl.ds(row, xr), pl.ds(col, LANES)],
                        sems.at[at],
                    )
                    pl.when(here)(copy.start)
                    waits.append((here, copy))

                @pl.when(turn == 0)
                def _():
                    total = ref[t, xr:, :].astype(F32)
                    total = (total[:1] + total[8:9]) * factors[0]
                    bias_ref[:, pl.ds(col, LANES)] += total

                at += 1
        if adds:
            keep_ref, came_ref = refs[len(inputs) - 2 : len(inputs)]
            sum_ref[0][...] = (keep_ref[0] + came_ref[0].astype(F32)).astype(BF16)
        for here, copy in waits:
            pl.when(here)(copy.wait)

    def run(*refs):
        body(*refs[: len(inputs)], *refs[len(inputs) + len(after) :])

    somewhere = pl.BlockSpec(memory_space=pl.ANY)
    sums = [shape(adds[0].shape[1:], BF16)] if adds else []
    moved = 2 * copies * xr * LANES * 6
    return pl.pallas_call(
        run,
        out_shape=[weight, weight, shape((1, hid), F32), *sums],
        in_specs=[VMEM] * len(arrays)
        + ([somewhere, somewhere, VMEM] if begun else [])
        + [VMEM] * len(adds)
        + [somewhere] * len(after),
        out_specs=[somewhere, somewhere, VMEM] + [VMEM] * len(sums),
        scratch_shapes=[
            pltpu.VMEM((copies, xr, LANES), F32),
            pltpu.SemaphoreType.DMA((copies,)),
        ],
        input_output_aliases={len(arrays): 0, len(arrays) + 1: 1} if begun else {},
        compiler_params=limits(arrays, copies * xr * LANES * 4),
        cost_estimate=pl.CostEstimate(flops=0, bytes_accessed=moved, transcendentals=0),
    )(*inputs, *after)


def local(
    features, w_neigh, w_self, bias, cotangent, block_rows, block_cols, block_vals, block_count
):
    rs = lax.axis_size("row")
    cs = lax.axis_size("col")
    nd, depth = features.shape
    hid = w_self.shape[1]
    rt = nd * cs
    half = rs // 2
    xw = 2 * depth // cs
    nc = min(rs, hid // LANES)
    nr = rs // nc
    xr = xw // nr

    def along_col(x, k):
        return lax.ppermute(x, "col", [(s, s ^ k) for s in range(cs)])

    def along_chips(x, k):
        return lax.ppermute(x, "row", [(s, s ^ (2 * k)) for s in range(rs)])

    def other_core(x):
        return lax.ppermute(x, "row", [(s, s ^ 1) for s in range(rs)])

    def gather_chips(x):
        far_first = {k: along_chips(x, k) for k in range(half - 1, 0, -1)}
        return [x] + [far_first[k] for k in range(1, half)]

    if rs == 2 * cs:

        def send_own(block, t):
            pairs = []
            for z in range(half):
                for core in range(2):
                    q = 2 * (z ^ t) + core
                    source = (2 * z + core) * cs + z
                    pairs.append((source, (2 * z + q // cs) * cs + q % cs))
            return lax.ppermute(block, ("row", "col"), pairs)

    else:
        swap = [((b % rs) * cs + b // rs, b) for b in range(rs * cs)]

        def send_own(block, t):
            return lax.ppermute(block, ("row", "col"), swap if t == 0 else [])

    near = along_chips(features, 1)
    mine_first = {0: features, 1: near}
    step = half // 2
    while step > 1:
        evens = [d for d in mine_first if d % 2 == 0]
        mine_first.update({d + step: along_chips(mine_first[d], step) for d in evens})
        step //= 2
    theirs_first = {0: other_core(features), 1: other_core(near)}
    own_feats = {0: send_own(features, 0)}
    tile, turned = densify(
        block_rows.reshape(-1),
        block_cols.reshape(-1),
        block_count.reshape(-1),
        block_vals[0, 0],
        nd,
        rs,
        cs,
        [],
    )
    mine_last = {d + 1: along_chips(x, 1) for d, x in mine_first.items() if d > 1}
    theirs_first.update({d: other_core(x) for d, x in mine_first.items() if d > 1})
    theirs_last = {d: other_core(x) for d, x in mine_last.items()}
    own_feats[1] = send_own(near, 1)

    def placed(mine, theirs):
        places = list(mine) + [half + d for d in theirs]
        return places, [*mine.values(), *theirs.values()]

    begun = forward_first(
        tile, *placed(mine_first, theirs_first), nd, [own_feats[0], own_feats[1]]
    )
    degree = row_sums(tile, nd, cs)
    step = 1
    while step < cs:
        masses = [degree, along_col(degree, step)]
        degree = masses[0] + masses[1]
        step *= 2
    evens = {d: send_own(follow(x, [begun, masses[0]]), d) for d, x in mine_first.items() if d > 1}
    own_feats.update(evens)
    own_feats.update({d: send_own(x, d) for d, x in mine_last.items()})
    parts = forward_parts(begun, tile, *placed(mine_last, theirs_last), nd, cs, list(evens.values()))
    own_feat = sum(list(own_feats.values())[1:], own_feats[0])
    inverse = 1.0 / (degree[0] + 1.0)
    inverse = jnp.broadcast_to(inverse[:, None], (rt, LANES))
    own = jnp.dot(own_feat, w_self, preferred_element_type=F32).astype(BF16)

    turned_neigh, turned_self = turn([w_neigh, w_self], [parts[0]])
    parts = [parts[0]] + [along_col(parts[k], k) for k in range(1, cs)]
    output, sums, *packs = activation(
        parts, masses, own, own_feat, w_neigh, bias[None, :], cotangent, [turned_neigh]
    )
    packs = [packs[0]] + [along_col(packs[k], k) for k in range(1, cs)]

    mid = cs // 2
    scaled_args = (inverse, turned_neigh, turned_self, cs, rs)
    early = scaled_parts(packs[:mid], 0, *scaled_args)
    keep, send = weight_parts(packs, sums, rs, xr, nc, early[:1])
    came = other_core(send)
    late = scaled_parts(packs[mid:], mid, *scaled_args, [keep])
    scaled, self_parts = zip(early, late)
    chunks = pair_sum(keep, came)
    chunks = [chunks[0]] + [along_chips(chunks[k], k) for k in range(half - 1, 0, -1)]
    keep, send = back_parts(turned, scaled, self_parts, nd, cs, rs, [keep])
    chunk, send = last_sum(chunks, send)
    line = gather_chips(chunk)
    keep, send = fold(keep, other_core(send), line[1:])
    line = stack(line, after=[send])
    step = 1
    while 2 * step < half:
        keep, send = fold(keep, along_chips(send, step))
        step *= 2
    last = (keep, along_chips(send, step))

    def piece(array, first, column, mine):
        return array, [(first + t, column) for t in range(array.shape[0])], mine

    mid = half // 2
    if cs == 4 and mid:
        first, second = along_col(line, 1), along_col(line, 2)
        near = [(line, 0, 0), (first, 0, 1), (second, 0, 2)]
        rest = [(along_col(first[:mid], 2), 0, 3), (along_col(second[mid:], 1), mid, 3)]
    else:
        near = [(line, 0, 0)] + [(along_col(line, k), 0, k) for k in range(1, cs - 1)]
        rest = [(along_col(line, cs - 1), 0, cs - 1)]
    factor = 1.0 / math.sqrt(nd * rs * cs)
    sizes = (depth, hid, xr, nc, cs, (factor, 32.0 * factor))
    pieces = [piece(*x, True) for x in near + rest]
    *begun, grad_input = assemble(pieces, (), *sizes, (), last)
    pieces = [piece(other_core(x), *where, False) for x, *where in near + rest]
    total_self, total_neigh, total_bias = assemble(pieces, begun, *sizes, ())
    return output, grad_input, total_self, total_neigh, total_bias.reshape(-1)


def solution(mesh):
    in_specs = (
        P(("col", "row"), None),
        P(),
        P(),
        P(),
        P(("row", "col"), None),
        P("row", "col", None),
        P("row", "col", None),
        P("row", "col", None, None, None),
        P("row", "col"),
    )
    out_specs = (P(("row", "col"), None), P(("col", "row"), None), P(), P(), P())
    return jax.shard_map(local, mesh=mesh, in_specs=in_specs, out_specs=out_specs, check_vma=False)
```
